32 devices in a mesh: dp: 8 (over z, x), rep: 4 (over y, core).
Axes of the slice: x: 2, y: 2, z: 4, core: 2. Of those that a mesh axis runs over, the one named last changes fastest.
Arguments:
- images: bfloat16 [384, 8, 8, 512], P(('dp', 'rep')), may hold values from -8 to 8
- micro_ids: int32 [384], P(('dp', 'rep')), may hold values from 0 to 3, as said below
- labels: int32 [384], P(('dp', 'rep')), may hold values from 0 to 9
- conv_weight: float32 [4608, 512], replicated, may hold values from -0.09375 to 0.09375
- conv_first: bfloat16 [4608, 512], replicated, may hold values from -1.1444092e-05 to 1.1444092e-05
- conv_second: bfloat16 [4608, 512], replicated, may hold values from 4.2188475e-14 to 1.687539e-13
- eig_scales: float32 [512, 512], replicated, may hold values from 0.01 to 0.1
- basis_in: float32 [512, 512], replicated, may hold values from -0.25 to 0.25
- basis_out: float32 [512, 512], replicated, may hold values from -0.25 to 0.25
- batchnorm_gain: float32 [512], replicated, may hold values from 0.5 to 1.5
- batchnorm_shift: float32 [512], replicated, may hold values from -2.5 to 2.5
- norm_first: float32 [2, 512], replicated, may hold values from -3.0517578e-05 to 3.0517578e-05
- norm_second: float32 [2, 512], replicated, may hold values from 3.8047728e-13 to 1.5219091e-12
- head: float32 [513, 10], replicated, may hold values from -0.25 to 0.25
- head_first: float32 [513, 10], replicated, may hold values from -3.0517578e-05 to 3.0517578e-05
- head_second: float32 [513, 10], replicated, may hold values from 3.8047728e-13 to 1.5219091e-12
Outputs:
- loss_parts: float32 [2], replicated
- grad_norm: float32 [], replicated
- conv_new: float32 [4608, 512], replicated
- conv_first_new: float32 [4608, 512], replicated
- conv_second_new: float32 [4608, 512], replicated
- scales_new: float32 [512, 512], replicated
- norm_new: float32 [2, 512], replicated
- norm_first_new: float32 [2, 512], replicated
- norm_second_new: float32 [2, 512], replicated
- head_new: float32 [513, 10], replicated
- head_first_new: float32 [513, 10], replicated
- head_second_new: float32 [513, 10], replicated
The draws below stay inside these ranges and needn't reach their ends.
Inputs may be any that keep to these rules, and one draw needn't show every extreme that they name: `micro_ids`: in each aligned block of 12 slots the used slots (below 3) come first; in the last block all 12 slots are used, its first three in micro-batches 0, 1 and 2.
All inputs are finite; a program needn't handle non-finite values.
Results may differ from the reference program's by a relative error of at most 0.0027.
Values sent between devices are 32-bit elements; how exact they have to be, the bound alone decides.
A program may use at most 128 MiB of HBM per device.

```python
import math
import jax
import jax.numpy as jnp
from jax import lax

C = 512
NCLS = 10
B_DEV = 12
H = 8
W = 8
STEP = 5
IMAGES = 384
NPAR = 2365450


def draw_images(key, part):
    key = jax.random.fold_in(key, 11)
    rows = jnp.arange(H).astype(jnp.float32) / max(H - 1, 1)
    base = jnp.clip(jax.random.normal(key, (IMAGES, H, W, C), jnp.float32), -4.0, 4.0)
    row_scale = 0.6 + 1.4 * rows
    return (base * row_scale[None, :, None, None]).astype(jnp.bfloat16)


def draw_micro_ids(key, part):
    key = jax.random.fold_in(key, 7)
    key_jit, key_pick = jax.random.split(key)
    devices = IMAGES // B_DEV
    owner = jnp.arange(IMAGES) // B_DEV
    slot = jnp.arange(IMAGES) % B_DEV
    least = B_DEV // 3
    target = least + (B_DEV - least) * owner // max(devices - 1, 1)
    jitter = jax.random.randint(key_jit, (devices,), -1, 2)[owner]
    used = jnp.clip(target + jitter, 1, B_DEV)
    used = jnp.where(owner == devices - 1, B_DEV, used)
    pick = jax.random.randint(key_pick, (IMAGES,), 0, 10)
    micro = jnp.where(pick < 5, 0, jnp.where(pick < 8, 1, 2))
    micro = jnp.where((owner == devices - 1) & (slot < 3), slot, micro)
    return jnp.where(slot < used, micro, 3).astype(jnp.int32)


def place_ends(array, key, low, top_value):
    longest = array.shape.index(max(array.shape))
    spots = []
    for shift in (0, 1):
        where = [jax.random.randint(jax.random.fold_in(key, axis), (), 0, length) for axis, length in enumerate(array.shape)]
        where[longest] = (where[longest] + shift) % array.shape[longest]
        spots.append(tuple(where))
    return array.at[spots[0]].set(low).at[spots[1]].set(top_value)


def normal_values(own_key, shape, scale, reach, held_as=jnp.bfloat16):
    drawn = jax.random.normal(own_key, shape, jnp.float32) * scale
    return jnp.minimum(jnp.maximum(drawn, -reach), reach).astype(held_as)


def setup_inputs(seed: int = 0) -> dict:
    arg_keys = jax.random.split(jax.random.key(seed), 17)
    images = draw_images(jax.random.fold_in(arg_keys[16], 71), 0)
    micro_ids = draw_micro_ids(jax.random.fold_in(arg_keys[16], 71), 0)
    labels = place_ends(jax.random.randint(arg_keys[2], (IMAGES,), 0, NCLS), jax.random.fold_in(arg_keys[2], 1), 0, NCLS - 1).astype(jnp.int32)
    conv_weight = normal_values(arg_keys[3], (9 * C, C), (9 * C) ** -0.5, 0.09375, jnp.float32)
    conv_first = normal_values(arg_keys[4], (9 * C, C), (0.00111 * NPAR ** -0.5), 1.1444091796875e-05)
    conv_second = jnp.clip(jnp.exp(jax.random.uniform(arg_keys[5], (9 * C, C), jnp.float32, math.log(4.218847493575595e-14), math.log(1.687538997430238e-13))), 4.218847493575595e-14, 1.687538997430238e-13).astype(jnp.bfloat16)
    eig_scales = jnp.clip(jnp.exp(jax.random.uniform(arg_keys[6], (C, C), jnp.float32, math.log(0.01), math.log(0.1))), 0.01, 0.1)
    basis_in = normal_values(arg_keys[7], (C, C), C ** -0.5, 0.25, jnp.float32)
    basis_out = normal_values(arg_keys[8], (C, C), C ** -0.5, 0.25, jnp.float32)
    batchnorm_gain = jnp.clip(1.0 + 0.1 * jax.random.normal(arg_keys[9], (C,), jnp.float32), 0.5, 1.5)
    batchnorm_shift = normal_values(arg_keys[10], (C,), 0.5, 2.5, jnp.float32)
    norm_first = normal_values(arg_keys[11], (2, C), (0.00333 * NPAR ** -0.5), 3.0517578125e-05, jnp.float32)
    norm_second = jnp.clip(jnp.exp(jax.random.uniform(arg_keys[12], (2, C), jnp.float32, math.log(3.8047727945675347e-13), math.log(1.5219091178270139e-12))), 3.8047727945675347e-13, 1.5219091178270139e-12)
    head = normal_values(arg_keys[13], (C + 1, NCLS), C ** -0.5, 0.25, jnp.float32)
    head_first = normal_values(arg_keys[14], (C + 1, NCLS), (0.00333 * NPAR ** -0.5), 3.0517578125e-05, jnp.float32)
    head_second = jnp.clip(jnp.exp(jax.random.uniform(arg_keys[15], (C + 1, NCLS), jnp.float32, math.log(3.8047727945675347e-13), math.log(1.5219091178270139e-12))), 3.8047727945675347e-13, 1.5219091178270139e-12)
    return dict(images=images, micro_ids=micro_ids, labels=labels, conv_weight=conv_weight, conv_first=conv_first, conv_second=conv_second, eig_scales=eig_scales, basis_in=basis_in, basis_out=basis_out, batchnorm_gain=batchnorm_gain, batchnorm_shift=batchnorm_shift, norm_first=norm_first, norm_second=norm_second, head=head, head_first=head_first, head_second=head_second)


@jax.custom_vjp
def low(v):
    return lax.optimization_barrier(v.astype(jnp.bfloat16)).astype(jnp.float32)

@jax.custom_vjp
def low_back(v):
    return v

def low_keep(v):
    return (low(v), None)

def low_pass(kept, grad):
    return (grad,)

def back_keep(v):
    return (v, None)

def back_low(kept, grad):
    return (low(grad),)
low.defvjp(low_keep, low_pass)
low_back.defvjp(back_keep, back_low)
highest_precision = lax.Precision.HIGHEST
norm_eps = 1e-05
damping = 0.001
clip_limit = 0.01

def box_sum(field):
    padded = jnp.pad(field, ((0, 0), (1, 1), (1, 1), (0, 0)))
    hgt, wid = (field.shape[1], field.shape[2])
    total = jnp.zeros_like(field)
    for row_off in range(3):
        for col_off in range(3):
            total = total + padded[:, row_off:row_off + hgt, col_off:col_off + wid, :]
    return total

def forward(conv_w, norm_gain_vector, norm_shift_vector, head_w, probe, inputs, micro, labels):
    count_img = inputs.shape[0]
    kernel = low(conv_w).reshape(3, 3, C, C)
    convolution_block = lax.conv_general_dilated(inputs, kernel, (1, 1), ((1, 1), (1, 1)), dimension_numbers=('NHWC', 'HWIO', 'NHWC'), precision=highest_precision)
    convolution_block = low_back(convolution_block + probe)
    micro_member = (micro[:, None] == jnp.arange(3)[None, :]).astype(jnp.float32)
    live = (micro < 3).astype(jnp.float32)
    pixels = lax.optimization_barrier(jnp.sum(micro_member, axis=0)) * (H * W)
    sums = jnp.einsum('nm,nhwc->mc', micro_member, convolution_block, precision=highest_precision)
    squares = jnp.einsum('nm,nhwc->mc', micro_member, convolution_block * convolution_block, precision=highest_precision)
    mean = sums / pixels[:, None]
    var = squares / pixels[:, None] - mean * mean
    rstd = lax.rsqrt(var + norm_eps)
    image_mean = jnp.dot(micro_member, mean, precision=highest_precision)
    image_inverse_deviation = jnp.dot(micro_member, rstd, precision=highest_precision) + (1.0 - live)[:, None]
    normalized_input = (convolution_block - image_mean[:, None, None, :]) * image_inverse_deviation[:, None, None, :]
    activation_map = jax.nn.softplus(norm_gain_vector * normalized_input + norm_shift_vector)
    blocks = activation_map.reshape(count_img, H // 2, 2, W // 2, 2, C)
    cell = jnp.log(lax.optimization_barrier(jnp.sum(jnp.exp(blocks), axis=(2, 4))))
    pooled = lax.optimization_barrier(jnp.mean(cell, axis=(1, 2)))
    logits = jnp.dot(low(pooled), low(head_w[:C]), precision=highest_precision) + head_w[C]
    logp = jax.nn.log_softmax(logits)
    onehot = (labels[:, None] == jnp.arange(NCLS)[None, :]).astype(jnp.float32)
    per_img = -(0.9 * lax.optimization_barrier(jnp.sum(onehot * logp, axis=1)) + 0.1 / NCLS * lax.optimization_barrier(jnp.sum(logp, axis=1)))
    loss_sum = jnp.sum(live * per_img)
    count = jnp.sum(live)
    return (loss_sum / count, (loss_sum, count))

def adamw(weight, grad, first, second, rate):
    first = 0.9 * first + 0.1 * grad
    second = 0.999 * second + 0.001 * grad * grad
    step_size = first / (1.0 - 0.9 ** STEP) / (jnp.sqrt(second / (1.0 - 0.999 ** STEP)) + 1e-08)
    return (weight - rate * (step_size + 0.01 * weight), first, second)

def reference(images, micro_ids, labels, conv_weight, conv_first, conv_second, eig_scales, basis_in, basis_out, batchnorm_gain, batchnorm_shift, norm_first, norm_second, head, head_first, head_second):
    inputs = images.astype(jnp.float32)
    probe = jnp.zeros(inputs.shape[:3] + (C,), jnp.float32)

    def loss_fn(conv_w, norm_gain_vector, norm_shift_vector, head_w, probe_in):
        return forward(conv_w, norm_gain_vector, norm_shift_vector, head_w, probe_in, inputs, micro_ids, labels)
    loss, pull, aux = jax.vjp(loss_fn, conv_weight, batchnorm_gain, batchnorm_shift, head, probe, has_aux=True)
    loss_sum, count = aux
    g_conv, g_gain, g_shift, g_head, g_out = pull(jnp.ones((), jnp.float32))
    turned = jnp.dot(inputs.reshape(-1, C), basis_in, precision=highest_precision).reshape(inputs.shape)
    box = box_sum(turned * turned).reshape(-1, C)
    gturned = jnp.dot(g_out.reshape(-1, C), basis_out, precision=highest_precision)
    stat = jnp.dot(box.T, gturned * gturned, precision=highest_precision) * (count * (H * W) * (H * W))
    scales_new = 0.95 * eig_scales + 0.05 * stat
    blocks = g_conv.reshape(9, C, C)
    rot = jnp.einsum('ji,tjk->tik', basis_in, blocks, precision=highest_precision)
    rot = jnp.einsum('tik,kl->til', rot, basis_out, precision=highest_precision)
    rot = rot / (scales_new + damping)
    back = jnp.einsum('ij,tjk->tik', basis_in, rot, precision=highest_precision)
    precond = jnp.einsum('tik,lk->til', back, basis_out, precision=highest_precision).reshape(9 * C, C)
    g_norm = jnp.stack([g_gain, g_shift])
    grad_norm = jnp.sqrt(jnp.sum(precond * precond) + jnp.sum(g_norm * g_norm) + jnp.sum(g_head * g_head))
    factor = jnp.minimum(1.0, clip_limit / (grad_norm + 1e-06))
    conv_new, conv_m, conv_v = adamw(conv_weight, factor * precond, conv_first.astype(jnp.float32), conv_second.astype(jnp.float32), 0.02)
    norm_new, norm_m, norm_v = adamw(jnp.stack([batchnorm_gain, batchnorm_shift]), factor * g_norm, norm_first, norm_second, 0.1)
    head_new, head_m, head_v = adamw(head, factor * g_head, head_first, head_second, 0.05)
    loss_parts = jnp.stack([loss_sum, count])
    return (loss_parts, grad_norm, conv_new, conv_m, conv_v, scales_new, norm_new, norm_m, norm_v, head_new, head_m, head_v)
```

```python
import functools
import itertools

import jax
import jax.numpy as jnp
from jax import lax
from jax.experimental import pallas as pl
from jax.experimental.pallas import tpu as pltpu
from jax.sharding import PartitionSpec as P

NCLS = 10
STEP = 5
NORM_EPS = 1e-05
DAMPING = 0.001
CLIP = 0.01
MESH = pl.DeviceIdType.MESH
F32 = jnp.float32
BF16 = jnp.bfloat16
HIGHEST = lax.Precision.HIGHEST
TAPS = 9
STAT = 9
UNITS = (0, 1, 9, 2, 3, 4, 5, 6, 7, 8)
ORDERS = {
    0: (0, 2, 1, 3, 4),
    1: (0, 3, 2, 1, 4),
    9: (0, 1, 2, 3, 4),
    2: (0, 2, 1, 3, 4),
    3: (0, 3, 2, 1, 4),
    4: (0, 3, 2, 1, 4),
    5: (0, 1, 2, 3, 4),
    6: (0, 2, 1, 3, 4),
    7: (0, 1, 3, 4, 2),
    8: (0, 1, 2, 3, 4),
}


def plan(extra):
    free, pending, tasks, held = {}, [], [], []
    serial = itertools.count()
    queue = list(UNITS)
    rank = {"ag": 0, "rs": 1, "sm": 1, "post": 2, "mm": 3, "fin": 4}
    clock, stat_ready = 0.0, False

    def send(dim, rows, now):
        size = rows * 2.048
        if dim == 0:
            need, lag = [("c", size / 550.0)], 0.9
        elif dim in (1, 2):
            need, lag = [(dim, size / 45.7)], 2.0
        elif dim == 3:
            need, lag = [("low", size / 45.7)], 2.0
        else:
            need, lag = [("high", size / 22.8), ("low", size / 45.7)], 2.8
        end = now
        for name, length in need:
            free[name] = max(free.get(name, 0.0), now) + length
            end = max(end, free[name])
        return end + lag

    def push(when, *task):
        pending.append((when, next(serial), task))

    push(0.0, "mm", queue.pop(0))
    push(send(0, 16, 0.0), "sm", 0)
    while pending:
        ready = [p for p in pending if p[0] <= clock]
        if not ready:
            clock = min(p[0] for p in pending)
            continue
        pick = min(ready, key=lambda p: (rank[p[2][0]], -p[2][-1] if len(p[2]) > 2 else 0, p[0], p[1]))
        pending.remove(pick)
        task = pick[2]
        tasks.append(task)
        kind, unit = task[0], task[1]
        if kind == "mm":
            push(send(0, 256, clock + 0.75), "rs", unit, 0)
            clock += 1.5
            if queue:
                push(clock, "mm", queue.pop(0))
        elif kind == "sm":
            clock += 0.05
            if unit + 1 < 5 + extra:
                push(send(min(unit + 1, 4), 16, clock), "sm", unit + 1)
        elif kind == "rs":
            stage = task[2]
            clock += 0.05 + (256 >> stage) * 0.0012
            if stage < 4 + extra:
                dim = ORDERS[unit][stage + 1] if stage < 4 else 4
                push(send(dim, max(256 >> (stage + 1), 16), clock), "rs", unit, stage + 1)
            elif unit == STAT or stat_ready:
                push(clock, "post", unit)
            else:
                held.append(unit)
        elif kind == "post":
            clock += 0.8
            if unit == STAT:
                stat_ready = True
                for other in held:
                    push(clock, "post", other)
            push(send(ORDERS[unit][4], 16, clock), "ag", unit, 0)
        elif kind == "ag":
            stage = task[2]
            clock += 0.05
            if stage < 4:
                push(send(ORDERS[unit][3 - stage], 16 << (stage + 1), clock), "ag", unit, stage + 1)
            else:
                push(clock, "fin", unit)
        else:
            clock += 1.2
    return tasks


def split(value):
    high = value.astype(BF16)
    return high, (value - high.astype(F32)).astype(BF16)


def dot(a, b, dims=((1,), (0,))):
    return lax.dot_general(a, b, (dims, ((), ())), preferred_element_type=F32)


def dot_exact(a, b, dims=((1,), (0,))):
    return lax.dot_general(a, b, (dims, ((), ())), precision=HIGHEST, preferred_element_type=F32)


def main_kernel(
    sizes,
    micro,
    labels,
    images,
    gain_ref,
    shift_ref,
    head,
    weight,
    eig_hbm,
    in_hbm,
    out_hbm,
    precond,
    scales,
    facts,
    work,
    half_sum,
    away,
    got0,
    got1,
    got2,
    got3,
    got4,
    got_more,
    small,
    small_got,
    tile_in,
    tile_core,
    tile_slots,
    tile_out,
    narrow,
    wide,
    conv,
    share,
    turned_hi,
    turned_lo,
    box_hi,
    box_lo,
    grad_low,
    rot_hi,
    rot_lo,
    rot2_hi,
    rot2_lo,
    eig,
    in_hi,
    in_lo,
    in_t_hi,
    in_t_lo,
    out_hi,
    out_lo,
    out_t_hi,
    out_t_lo,
    gathered_hi,
    gathered_lo,
    result,
    rows_stat,
    pooled,
    shares,
    shares_x,
    dpool,
    head_pad,
    scale_rows,
    square_sum,
    w_sem,
    load_sem,
    out_sem,
    rs_send,
    rs_recv,
    ag_send,
    ag_recv,
    sm_send,
    sm_recv,
    core_send,
    core_recv,
    chip_send,
    chip_recv,
):
    dp_count, rep_count, count_img = sizes
    area = 64
    cells = 16
    chips = dp_count * rep_count // 2
    dp = lax.axis_index("dp")
    rep = lax.axis_index("rep")
    core = rep % 2
    chip = dp * (rep_count // 2) + rep // 2
    bits = [("rep", 1), ("dp", 1), ("rep", 2), ("dp", 2), ("dp", 4)]
    step = 8
    while step < dp_count:
        bits.append(("dp", step))
        step *= 2
    step = 4
    while step < rep_count:
        bits.append(("rep", step))
        step *= 2
    extra = len(bits) - 5
    mine = [((dp if name == "dp" else rep) // weight_of) % 2 for name, weight_of in bits]

    def partner(k):
        name, weight_of = bits[k]
        change = (1 - 2 * mine[k]) * weight_of
        return (dp + change, rep) if name == "dp" else (dp, rep + change)

    def chip_device(q):
        return (q // (rep_count // 2), (q % (rep_count // 2)) * 2 + core)

    weight_copies = [pltpu.make_async_copy(weight.at[t], work.at[t], w_sem.at[t]) for t in range(TAPS)]
    for copy in weight_copies:
        copy.start()
    loads = [
        pltpu.make_async_copy(src, dst, load_sem.at[k])
        for k, (src, dst) in enumerate(((in_hbm, result.at[0]), (out_hbm, result.at[1]), (eig_hbm, eig)))
    ]
    for copy in loads:
        copy.start()

    barrier = pltpu.get_barrier_semaphore()

    def greet(k, carry):
        pl.semaphore_signal(barrier, inc=1, device_id=chip_device((chip + k) % chips), device_id_type=MESH)
        return carry

    lax.fori_loop(1, chips, greet, 0)
    pl.semaphore_signal(barrier, inc=1, device_id=partner(0), device_id_type=MESH)

    stride = count_img * 8
    column = lax.broadcasted_iota(jnp.int32, (2, 8, 512), 1)
    for k in range(3):
        narrow[k, 0:stride] = jnp.zeros((stride, 512), BF16)
        narrow[k, 9 * stride : 10 * stride] = jnp.zeros((stride, 512), BF16)

    def build(h, carry):
        for pair in range(count_img // 2):
            block = images[2 * pair : 2 * pair + 2, h].astype(F32)
            left = jnp.where(column == 0, 0.0, pltpu.roll(block, 1, 1))
            right = jnp.where(column == 7, 0.0, pltpu.roll(block, 7, 1))
            at = pl.ds(pl.multiple_of((h + 1) * stride + 16 * pair, 16), 16)
            at_wide = pl.ds(pl.multiple_of(h * 128 + 16 * pair, 16), 16)
            for k, value in enumerate((left, block, right)):
                low = value.reshape(16, 512).astype(BF16)
                narrow[k, at] = low
                wide[k, at_wide] = low
        fill = pl.ds(pl.multiple_of(h * 128 + stride, 16), 128 - stride)
        for k in range(3):
            wide[k, fill] = jnp.zeros((128 - stride, 512), BF16)
        grad_low[fill] = jnp.zeros((128 - stride, 512), BF16)
        return carry

    lax.fori_loop(0, 8, build, 0)

    def clear(h, carry):
        conv[h] = jnp.zeros((stride, 512), F32)
        return carry

    lax.fori_loop(0, 8, clear, 0)

    def conv_row(dy, carry):
        for dx in range(3):
            tap = dy * 3 + dx
            pltpu.make_async_copy(weight.at[tap], work.at[tap], w_sem.at[tap]).wait()

            def cast(k, inner):
                piece = work[tap, k // 4, (k // 2) % 2, k % 2].reshape(64, 512)
                turned_lo[dx, pl.ds(pl.multiple_of(k * 64, 64), 64), 0:512] = piece.astype(BF16)
                return inner

            lax.fori_loop(0, 8, cast, 0)
        for m in range(2):
            for n in range(2):
                total = None
                for dx in range(3):
                    rows = pl.ds(pl.multiple_of(dy * stride + m * 4 * stride, 16), 4 * stride)
                    term = dot(narrow[dx, rows], turned_lo[dx, :, n * 256 : n * 256 + 256])
                    total = term if total is None else total + term
                conv[4 * m : 4 * m + 4, :, n * 256 : n * 256 + 256] += total.reshape(4, stride, 256)
        return carry

    lax.fori_loop(0, 3, conv_row, 0)

    def member(n):
        return [jnp.where(micro[n] == m, 1.0, 0.0).astype(F32) for m in range(3)]

    def gather_sums(n, carry):
        at = pl.ds(pl.multiple_of(n * 8, 8), 8)
        first = jnp.zeros((8, 512), F32)
        second = jnp.zeros((8, 512), F32)
        for h in range(8):
            value = conv[h, at]
            first = first + value
            second = second + value * value
        kinds = member(n)
        return tuple(c + k * first for c, k in zip(carry[:3], kinds)) + tuple(
            c + k * second for c, k in zip(carry[3:6], kinds)
        )

    zero_tile = jnp.zeros((8, 512), F32)
    sums = lax.fori_loop(0, count_img, gather_sums, (zero_tile,) * 6)
    counts = [jnp.zeros((), F32)] * 3
    for n in range(count_img):
        counts = [c + k for c, k in zip(counts, member(n))]
    row8 = lax.broadcasted_iota(jnp.int32, (8, 512), 0)
    lane8 = lax.broadcasted_iota(jnp.int32, (8, 512), 1)

    def stack_rows(rows):
        tile = zero_tile
        for k, row in enumerate(rows):
            tile = jnp.where(row8 == k, jnp.broadcast_to(row, (8, 512)), tile)
        return tile

    count_row = zero_tile
    for m in range(3):
        count_row = jnp.where(lane8 % 256 == m, counts[m], count_row)
    tile_in[0] = jnp.where(row8 == 6, count_row, stack_rows([jnp.sum(s, axis=0, keepdims=True) for s in sums]))

    def core_half(which):
        return pl.ds(pl.multiple_of(which * 256, 256), 256)

    def tile_copy(i):
        return pltpu.make_async_remote_copy(
            src_ref=tile_in.at[i, :, core_half(1 - core)],
            dst_ref=tile_core.at[i],
            send_sem=core_send.at[2 * i],
            recv_sem=core_recv.at[2 * i],
            device_id=partner(0),
            device_id_type=MESH,
        )

    def tile_start(i):
        tile_copy(i).start()
        tile_copy(i).wait()
        tile_slots[i, 0] = tile_in[i, :, core_half(core)] + tile_core[i]

        def give(k, carry):
            pltpu.make_async_remote_copy(
                src_ref=tile_slots.at[i, 0],
                dst_ref=tile_slots.at[i, k],
                send_sem=chip_send.at[i],
                recv_sem=chip_recv.at[i],
                device_id=chip_device((chip + k) % chips),
                device_id_type=MESH,
            ).start()
            return carry

        lax.fori_loop(1, chips, give, 0)

    def tile_end(i):
        others = tile_slots.at[i, pl.ds(1, chips - 1)]
        pltpu.make_async_remote_copy(
            src_ref=others,
            dst_ref=others,
            send_sem=chip_send.at[i],
            recv_sem=chip_recv.at[i],
            device_id=partner(0),
            device_id_type=MESH,
        ).wait()

        def add(k, total):
            return total + tile_slots[i, (chip - k + chips) % chips]

        tile_out[i, core] = lax.fori_loop(0, chips, add, jnp.zeros((8, 256), F32))
        back = pltpu.make_async_remote_copy(
            src_ref=tile_out.at[i, core],
            dst_ref=tile_out.at[i, core],
            send_sem=core_send.at[2 * i + 1],
            recv_sem=core_recv.at[2 * i + 1],
            device_id=partner(0),
            device_id_type=MESH,
        )
        back.start()
        back.wait()
        return jnp.concatenate([tile_out[i, 0], tile_out[i, 1]], axis=1)

    pl.semaphore_wait(barrier, chips)
    tile_start(0)

    for copy in loads:
        copy.wait()
    value = result[0]
    in_hi[...], in_lo[...] = split(value)
    in_t_hi[...], in_t_lo[...] = split(value.T)
    value = result[1]
    out_hi[...], out_lo[...] = split(value)
    out_t_hi[...], out_t_lo[...] = split(value.T)
    for dx in range(3):
        for ref in (turned_hi, turned_lo):
            ref[dx, :, 0:128] = jnp.zeros((512, 128), BF16)
            ref[dx, :, 1152:1280] = jnp.zeros((512, 128), BF16)

    def turn(j, carry):
        total = None
        for dx in range(3):
            rows = wide[dx, pl.ds(pl.multiple_of(256 * j, 256), 256)]
            value = dot(in_t_hi[...], rows, ((1,), (1,))) + dot(in_t_lo[...], rows, ((1,), (1,)))
            at = pl.ds(pl.multiple_of(128 + 256 * j, 128), 256)
            turned_hi[dx, :, at], turned_lo[dx, :, at] = split(value)
            total = value * value if total is None else total + value * value
        result[j // 2, :, pl.ds(pl.multiple_of((j % 2) * 256, 256), 256)] = total
        return carry

    lax.fori_loop(0, 4, turn, 0)

    def squares(h):
        return result[h // 4, :, (h % 4) * 128 : (h % 4) * 128 + 128]

    for h in range(8):
        value = squares(h)
        if h > 0:
            value = value + squares(h - 1)
        if h < 7:
            value = value + squares(h + 1)
        box_hi[:, h * 128 : h * 128 + 128], box_lo[:, h * 128 : h * 128 + 128] = split(value)

    totals = tile_end(0)

    gain = gain_ref[...]
    shift = shift_ref[...]
    live_total = totals[6:7, 0:1] + totals[6:7, 1:2] + totals[6:7, 2:3]
    pixels = [totals[6:7, m : m + 1] * float(area) for m in range(3)]
    mean_rows, rstd_rows = [], []
    for m in range(3):
        mean = totals[m : m + 1] / pixels[m]
        var = totals[3 + m : 4 + m] / pixels[m] - mean * mean
        mean_rows.append(mean)
        rstd_rows.append(lax.rsqrt(var + NORM_EPS))
    rows_stat[0] = stack_rows(mean_rows)
    rows_stat[1] = stack_rows(rstd_rows)

    def image_rows(n, k):
        kinds = member(n)
        row = sum(kinds[m] * rows_stat[k, m : m + 1] for m in range(3))
        return row, 1.0 - (kinds[0] + kinds[1] + kinds[2])

    even = lax.broadcasted_iota(jnp.int32, (8, 512), 0) % 2 == 0
    pooled[...] = jnp.zeros((16, 512), F32)
    shares[...] = jnp.zeros((16, 512), F32)
    shares_x[...] = jnp.zeros((16, 512), F32)

    def forward(n, carry):
        mean, dead = image_rows(n, 0)
        rstd, _ = image_rows(n, 1)
        rstd = rstd + dead
        at = pl.ds(pl.multiple_of(n * 8, 8), 8)
        cell_sum, share_sum, share_x_sum = zero_tile, zero_tile, zero_tile
        for a in range(4):
            xs = [(conv[2 * a + k, at] - mean) * rstd for k in range(2)]
            exps = [jnp.exp(gain * x + shift) for x in xs]
            both = exps[0] + exps[1]
            both = both + jnp.where(even, pltpu.roll(both, 7, 0), pltpu.roll(both, 1, 0))
            both = both + 4.0
            cell_sum = cell_sum + jnp.log(both)
            inverse = 1.0 / both
            for k in range(2):
                part = exps[k] * inverse
                share[2 * a + k, at] = part
                share_sum = share_sum + part
                share_x_sum = share_x_sum + part * xs[k]
        row = pl.ds(n, 1)
        pooled[row] = jnp.sum(cell_sum, axis=0, keepdims=True) * (0.5 / cells)
        shares[row] = jnp.sum(share_sum, axis=0, keepdims=True)
        shares_x[row] = jnp.sum(share_x_sum, axis=0, keepdims=True)
        return carry

    lax.fori_loop(0, count_img, forward, 0)

    head_pad[...] = jnp.zeros((128, 640), F32)
    head_pad[0:NCLS, 0:513] = head[...]
    head_rows = head_pad[:, 0:512].astype(BF16)
    pooled_low = pooled[...].astype(BF16)
    logits = dot(pooled_low, head_rows, ((1,), (1,))) + head_pad[:, 512:640].T[0:1, :]
    row16 = lax.broadcasted_iota(jnp.int32, (16, 128), 0)
    lane16 = lax.broadcasted_iota(jnp.int32, (16, 128), 1)
    label_of = jnp.zeros((16, 128), jnp.int32)
    micro_of = jnp.full((16, 128), 3, jnp.int32)
    for n in range(count_img):
        label_of = jnp.where(row16 == n, labels[n], label_of)
        micro_of = jnp.where(row16 == n, micro[n], micro_of)
    is_class = lane16 < NCLS
    live = jnp.where(micro_of < 3, 1.0, 0.0)
    onehot = jnp.where(lane16 == label_of, 1.0, 0.0)
    top = jnp.max(jnp.where(is_class, logits, -3e38), axis=1, keepdims=True)
    shifted = jnp.where(is_class, logits - top, 0.0)
    log_sum = jnp.log(jnp.sum(jnp.where(is_class, jnp.exp(shifted), 0.0), axis=1, keepdims=True))
    logp = jnp.where(is_class, shifted - log_sum, 0.0)
    per_img = -(
        0.9 * jnp.sum(onehot * logp, axis=1, keepdims=True) + 0.1 / NCLS * jnp.sum(logp, axis=1, keepdims=True)
    )
    loss = jnp.sum(live[:, 0:1] * per_img, axis=0, keepdims=True)
    dlogits = jnp.where(is_class, jnp.exp(logp) - 0.9 * onehot - 0.1 / NCLS, 0.0) * (live / live_total)
    dpool[...] = dot_exact(dlogits, head_rows.astype(F32)) * (1.0 / cells)
    head_grad = dot_exact(dlogits, pooled_low.astype(F32), ((0,), (0,)))
    row16w = lax.broadcasted_iota(jnp.int32, (16, 512), 0)
    bias_grad = jnp.concatenate(
        [jnp.sum(dlogits, axis=0, keepdims=True), jnp.zeros((1, 384), F32)], axis=1
    )
    block = jnp.where(row16w < NCLS, head_grad[0:16], 0.0)
    block = jnp.where(row16w == NCLS, bias_grad, block)
    small[...] = jnp.where(row16w == NCLS + 1, loss, block)

    back_rows = []
    for which in (shares, shares_x):
        for m in range(3):
            inside = jnp.where(micro_of[:, 0:1] == m, 1.0, 0.0)
            back_rows.append(jnp.sum(inside * (dpool[...] * which[...]), axis=0, keepdims=True))
    tile_in[1] = stack_rows(back_rows)
    tile_start(1)
    totals = tile_end(1)
    norm_grads = [
        totals[3:4] + totals[4:5] + totals[5:6],
        totals[0:1] + totals[1:2] + totals[2:3],
    ]
    rows_stat[2] = stack_rows([gain * totals[m : m + 1] / pixels[m] for m in range(3)])
    rows_stat[3] = stack_rows([gain * totals[3 + m : 4 + m] / pixels[m] for m in range(3)])

    def backward(pair, carry):
        parts = []
        for k in range(2):
            n = 2 * pair + k
            mean, dead = image_rows(n, 0)
            rstd, _ = image_rows(n, 1)
            rstd = rstd + dead
            offset, _ = image_rows(n, 2)
            slope, _ = image_rows(n, 3)
            parts.append((mean, rstd, offset, slope, gain * dpool[pl.ds(n, 1)], pl.ds(pl.multiple_of(n * 8, 8), 8)))
        for h in range(8):
            values = []
            for mean, rstd, offset, slope, factor, at in parts:
                xhat = (conv[h, at] - mean) * rstd
                values.append(rstd * (factor * share[h, at] - offset - xhat * slope))
            rows = pl.ds(pl.multiple_of(h * 128 + 16 * pair, 16), 16)
            grad_low[rows] = jnp.concatenate(values, axis=0).astype(BF16)
        return carry

    lax.fori_loop(0, count_img // 2, backward, 0)

    def rotate(k, carry):
        rows = pl.ds(pl.multiple_of(k * 256, 256), 256)
        value = dot(grad_low[rows], out_hi[...]) + dot(grad_low[rows], out_lo[...])
        rot_hi[rows], rot_lo[rows] = split(value)
        rot2_hi[rows], rot2_lo[rows] = split(value * value)
        return carry

    lax.fori_loop(0, 4, rotate, 0)

    got = (got0, got1, got2, got3, got4)
    left_home = []

    def region(unit, fixed, first=1):
        return (unit,) + tuple(fixed.get(k, slice(None)) for k in range(first, 5))

    def rs_copy(unit, stage):
        if stage < 5:
            order = ORDERS[unit]
            fixed = {k: mine[k] for k in order[:stage]}
            fixed[order[stage]] = 1 - mine[order[stage]]
            target, to = got[stage].at[unit], partner(order[stage])
        else:
            fixed = dict(enumerate(mine[:5]))
            target, to = got_more.at[unit, stage - 5], partner(stage)
        source = half_sum.at[region(unit, fixed)] if stage else away.at[UNITS.index(unit) % 2]
        return pltpu.make_async_remote_copy(
            src_ref=source,
            dst_ref=target,
            send_sem=rs_send.at[unit, stage],
            recv_sem=rs_recv.at[unit, stage],
            device_id=to,
            device_id_type=MESH,
        )

    def ag_copy(unit, stage):
        order = ORDERS[unit]
        where = work.at[region(unit, {k: mine[k] for k in order[: 5 - stage]}, 0)]
        return pltpu.make_async_remote_copy(
            src_ref=where,
            dst_ref=where,
            send_sem=ag_send.at[unit, stage],
            recv_sem=ag_recv.at[unit, stage],
            device_id=partner(order[4 - stage]),
            device_id_type=MESH,
        )

    def sm_copy(stage):
        return pltpu.make_async_remote_copy(
            src_ref=small,
            dst_ref=small_got.at[stage],
            send_sem=sm_send.at[stage],
            recv_sem=sm_recv.at[stage],
            device_id=partner(stage),
            device_id_type=MESH,
        )

    def do_mm(unit):
        dy, dx = unit // 3, unit % 3
        slot = UNITS.index(unit) % 2
        if UNITS.index(unit) >= 2:
            before = UNITS[UNITS.index(unit) - 2]
            if before not in left_home:
                left_home.append(before)
                rs_copy(before, 0).wait_send()
        for stays, half in enumerate((1 - core, core)):
            rows = pl.ds(pl.multiple_of(half * 256, 256), 256)

            def tile(k, carry):
                cols = pl.ds(pl.multiple_of(k * 256, 256), 256)
                if unit == STAT:
                    left_hi, left_lo = box_hi[rows], box_lo[rows]
                    right_hi, right_lo = rot2_hi[:, cols], rot2_lo[:, cols]
                else:
                    left_hi = turned_hi[dx, rows, dy * 128 : dy * 128 + 1024]
                    left_lo = turned_lo[dx, rows, dy * 128 : dy * 128 + 1024]
                    right_hi, right_lo = rot_hi[:, cols], rot_lo[:, cols]
                value = dot(left_hi, right_hi) + dot(left_hi, right_lo) + dot(left_lo, right_hi)
                value = value.reshape(2, 2, 2, 2, 16, 256)
                if stays:
                    half_sum[unit, :, :, :, :, :, cols] = value
                else:
                    away[slot, :, :, :, :, :, cols] = value
                return carry

            lax.fori_loop(0, 2, tile, 0)
            if not stays:
                rs_copy(unit, 0).start()

    def do_rs(unit, stage):
        if stage == 0 and unit in left_home:
            rs_copy(unit, stage).wait_recv()
        else:
            rs_copy(unit, stage).wait()
            left_home.append(unit)
        if stage < 5:
            order = ORDERS[unit]
            fixed = {k: mine[k] for k in order[: stage + 1]}
            source, at = got[stage], (unit,)
        else:
            fixed = dict(enumerate(mine[:5]))
            source, at = got_more, (unit, stage - 5)
        left = [k for k in range(1, 5) if k not in fixed]

        def add(i, carry):
            inner = dict(fixed)
            where = at
            if len(left) >= 3:
                inner[left[0]], inner[left[1]] = i // 2, i % 2
                where = at + (i // 2, i % 2)
            half_sum[region(unit, inner)] += source[where]
            return carry

        if len(left) >= 3:
            lax.fori_loop(0, 4, add, 0)
        else:
            add(0, 0)
        if stage < 4 + extra:
            rs_copy(unit, stage + 1).start()

    own = dict(enumerate(mine[:5]))
    own_block = (((mine[0] * 2 + mine[1]) * 2 + mine[2]) * 2 + mine[3]) * 2 + mine[4]

    def do_post(unit):
        at = region(unit, own, 0)
        value = half_sum[region(unit, own)]
        if unit == STAT:
            rows = pl.ds(pl.multiple_of(own_block * 16, 16), 16)
            value = 0.95 * eig[rows] + 0.05 * (value * (live_total * float(area * area)))
            scale_rows[...] = value + DAMPING
            work[at] = value
        else:
            high, low = split(value / scale_rows[...])
            work[at] = dot(high, out_t_hi[...]) + dot(high, out_t_lo[...]) + dot(low, out_t_hi[...])
        ag_copy(unit, 0).start()

    def do_ag(unit, stage):
        ag_copy(unit, stage).wait()
        if stage < 4:
            ag_copy(unit, stage + 1).start()

    done = []

    def result_copy(k):
        unit = done[k]
        return pltpu.make_async_copy(
            result.at[k % 2], precond.at[pl.ds(unit * 512, 512)], out_sem.at[k % 2]
        )

    scales_copy = pltpu.make_async_copy(work.at[STAT], scales, out_sem.at[2])

    def do_fin(unit):
        if unit == STAT:
            scales_copy.start()
            return
        k = len(done)
        done.append(unit)
        if k >= 2:
            result_copy(k - 2).wait()

        def cut(i, carry):
            rows = pl.ds(pl.multiple_of(i * 64, 64), 64)
            value = work[unit, i // 4, (i // 2) % 2, i % 2].reshape(64, 512)
            gathered_hi[rows], gathered_lo[rows] = split(value)
            return carry

        lax.fori_loop(0, 8, cut, 0)

        def tile(i, carry):
            rows = pl.ds(pl.multiple_of((i // 2) * 256, 256), 256)
            cols = pl.ds(pl.multiple_of((i % 2) * 256, 256), 256)
            value = (
                dot(in_hi[rows], gathered_hi[:, cols])
                + dot(in_hi[rows], gathered_lo[:, cols])
                + dot(in_lo[rows], gathered_hi[:, cols])
            )
            result[k % 2, rows, cols] = value
            square_sum[...] += jnp.sum((value * value).reshape(32, 8, 256), axis=0)
            return carry

        lax.fori_loop(0, 4, tile, 0)
        result_copy(k).start()

    def do_sm(stage):
        sm_copy(stage).wait()
        small[...] += small_got[stage]
        if stage < 4 + extra:
            sm_copy(stage + 1).start()

    square_sum[...] = jnp.zeros((8, 256), F32)
    sm_copy(0).start()
    run = {"mm": do_mm, "rs": do_rs, "post": do_post, "ag": do_ag, "fin": do_fin, "sm": do_sm}
    for task in plan(extra):
        run[task[0]](*task[1:])

    block = small[...]
    head_part = jnp.where(row16w <= NCLS, block, 0.0)
    squared = (
        jnp.sum(jnp.sum(square_sum[...], axis=0, keepdims=True), axis=1, keepdims=True)
        + jnp.sum(norm_grads[0] * norm_grads[0] + norm_grads[1] * norm_grads[1], axis=1, keepdims=True)
        + jnp.sum(jnp.sum(head_part * head_part, axis=0, keepdims=True), axis=1, keepdims=True)
    )
    norm = jnp.sqrt(squared)
    factor = jnp.minimum(1.0, CLIP / (norm + 1e-06))
    facts[0:16] = block
    facts[16:24] = stack_rows(norm_grads + [block[NCLS + 1 : NCLS + 2], live_total, norm, factor])
    for k in range(max(len(done) - 2, 0), len(done)):
        result_copy(k).wait()
    scales_copy.wait()


def adamw(weight, grad, first, second, rate):
    first = 0.9 * first + 0.1 * grad
    second = 0.999 * second + 0.001 * grad * grad
    step_size = first / (1.0 - 0.9**STEP) / (jnp.sqrt(second / (1.0 - 0.999**STEP)) + 1e-08)
    return (weight - rate * (step_size + 0.01 * weight), first, second)


def adamw_positive(weight, grad, first, second, rate):
    first = 0.9 * first + 0.1 * grad
    second = 0.999 * second + 0.001 * grad * grad
    scaled = second * (1.0 / (1.0 - 0.999**STEP))
    root = scaled * lax.rsqrt(scaled) + 1e-08
    step = first * (rate / (1.0 - 0.9**STEP)) / root
    return (weight * (1.0 - 0.01 * rate) - step, first, second)


CHUNKS = 18
RING = 4


def update_kernel(
    facts,
    gain,
    shift,
    norm_first,
    norm_second,
    head,
    head_first,
    head_second,
    precond,
    weight,
    first,
    second,
    scales,
    loss_parts,
    grad_norm,
    norm_new,
    norm_m,
    norm_v,
    head_new,
    head_m,
    head_v,
    conv_new,
    conv_m,
    conv_v,
    scales_new,
    in_precond,
    in_weight,
    in_first,
    in_second,
    out_new,
    out_m,
    out_v,
    scales_held,
    in_sem,
    out_sem,
    scale_sem,
):
    tall = TAPS * 512 // CHUNKS
    pairs = ((precond, in_precond), (weight, in_weight), (first, in_first), (second, in_second))
    outs = ((out_new, conv_new), (out_m, conv_m), (out_v, conv_v))

    def load(k, i):
        rows = pl.ds(pl.multiple_of(i * tall, tall), tall)
        return pltpu.make_async_copy(pairs[k][0].at[rows], pairs[k][1].at[rows], in_sem.at[k, i])

    def store(k, i):
        rows = pl.ds(pl.multiple_of(i * tall, tall), tall)
        return pltpu.make_async_copy(outs[k][0].at[i % RING], outs[k][1].at[rows], out_sem.at[k, i % RING])

    def start(i, carry):
        for k in range(4):
            load(k, i).start()
        return carry

    lax.fori_loop(0, CHUNKS, start, 0)
    scale_in = pltpu.make_async_copy(scales, scales_held, scale_sem.at[0])
    scale_out = pltpu.make_async_copy(scales_held, scales_new, scale_sem.at[1])
    scale_in.start()

    factor = facts[21:22, 0:1]
    loss_parts[0] = facts[18, 0]
    loss_parts[1] = facts[19, 0]
    grad_norm[0] = facts[20, 0]
    grads = factor * facts[16:18, :]
    weights = jnp.concatenate([gain[...], shift[...]], axis=0)
    norm_new[...], norm_m[...], norm_v[...] = adamw(weights, grads, norm_first[...], norm_second[...], 0.1)
    block = factor * facts[0:16, :]
    head_new[:, 0:512], head_m[:, 0:512], head_v[:, 0:512] = adamw(
        head[:, 0:512], block[0:NCLS], head_first[:, 0:512], head_second[:, 0:512], 0.05
    )
    bias = jnp.concatenate([block[0:16, 0:128], jnp.zeros((112, 128), F32)], axis=0).T[0:NCLS, NCLS : NCLS + 1]
    head_new[:, 512:513], head_m[:, 512:513], head_v[:, 512:513] = adamw(
        head[:, 512:513], bias, head_first[:, 512:513], head_second[:, 512:513], 0.05
    )

    def chunk(i, carry):
        for k in range(4):
            load(k, i).wait()

        @pl.when(i >= RING)
        def _():
            for k in range(3):
                store(k, i).wait()

        def piece(j, inner):
            rows = pl.ds(pl.multiple_of(i * tall + j * 32, 32), 32)
            at = pl.ds(pl.multiple_of(j * 32, 32), 32)
            out_new[i % RING, at], out_m[i % RING, at], out_v[i % RING, at] = adamw_positive(
                in_weight[rows],
                factor * in_precond[rows],
                in_first[rows].astype(F32),
                in_second[rows].astype(F32),
                0.02,
            )
            return inner

        lax.fori_loop(0, tall // 32, piece, 0)
        for k in range(3):
            store(k, i).start()
        return carry

    lax.fori_loop(0, CHUNKS, chunk, 0)
    scale_in.wait()
    scale_out.start()
    for i in range(CHUNKS - RING, CHUNKS):
        for k in range(3):
            store(k, i).wait()
    scale_out.wait()


def shards(
    sizes,
    images,
    micro_ids,
    labels,
    conv_weight,
    conv_first,
    conv_second,
    eig_scales,
    basis_in,
    basis_out,
    batchnorm_gain,
    batchnorm_shift,
    norm_first,
    norm_second,
    head,
    head_first,
    head_second,
):
    dp_count, rep_count = sizes
    count_img = images.shape[0]
    chips = dp_count * rep_count // 2
    bit_count = (dp_count * rep_count - 1).bit_length()
    extra = bit_count - 5
    vmem = pl.BlockSpec(memory_space=pltpu.VMEM)
    smem = pl.BlockSpec(memory_space=pltpu.SMEM)
    hbm = pl.BlockSpec(memory_space=pl.ANY)
    gain = batchnorm_gain.reshape(1, 512)
    shift = batchnorm_shift.reshape(1, 512)
    pixels = 8 * count_img
    square = (512, 512)
    dma = pltpu.SemaphoreType.DMA
    scratch = [
        pltpu.VMEM((10, 2, 2, 2, 2, 2, 16, 512), F32),
        pltpu.VMEM((10, 2, 2, 2, 2, 16, 512), F32),
        pltpu.VMEM((2, 2, 2, 2, 2, 16, 512), F32),
        pltpu.VMEM((10, 2, 2, 2, 2, 16, 512), F32),
        pltpu.VMEM((10, 2, 2, 2, 16, 512), F32),
        pltpu.VMEM((10, 2, 2, 16, 512), F32),
        pltpu.VMEM((10, 2, 16, 512), F32),
        pltpu.VMEM((10, 16, 512), F32),
        pltpu.VMEM((10, max(extra, 1), 16, 512) if extra else (1, 1, 8, 128), F32),
        pltpu.VMEM((16, 512), F32),
        pltpu.VMEM((bit_count, 16, 512), F32),
        pltpu.VMEM((2, 8, 512), F32),
        pltpu.VMEM((2, 8, 256), F32),
        pltpu.VMEM((2, chips, 8, 256), F32),
        pltpu.VMEM((2, 2, 8, 256), F32),
        pltpu.VMEM((3, 10 * pixels, 512), BF16),
        pltpu.VMEM((3, 1024, 512), BF16),
        pltpu.VMEM((8, pixels, 512), F32),
        pltpu.VMEM((8, pixels, 512), F32),
        pltpu.VMEM((3, 512, 1280), BF16),
        pltpu.VMEM((3, 512, 1280), BF16),
        pltpu.VMEM((512, 1024), BF16),
        pltpu.VMEM((512, 1024), BF16),
        pltpu.VMEM((1024, 512), BF16),
    ]
    scratch += [pltpu.VMEM((1024, 512), BF16)] * 4
    scratch += [pltpu.VMEM(square, F32)]
    scratch += [pltpu.VMEM(square, BF16)] * 10
    scratch += [
        pltpu.VMEM((2, 512, 512), F32),
        pltpu.VMEM((4, 8, 512), F32),
        pltpu.VMEM((16, 512), F32),
        pltpu.VMEM((16, 512), F32),
        pltpu.VMEM((16, 512), F32),
        pltpu.VMEM((16, 512), F32),
        pltpu.VMEM((128, 640), F32),
        pltpu.VMEM((16, 512), F32),
        pltpu.VMEM((8, 256), F32),
        dma((TAPS,)),
        dma((3,)),
        dma((3,)),
        dma((10, bit_count)),
        dma((10, bit_count)),
        dma((10, 5)),
        dma((10, 5)),
        dma((bit_count,)),
        dma((bit_count,)),
        dma((4,)),
        dma((4,)),
        dma((2,)),
        dma((2,)),
    ]
    precond, scales, facts = pl.pallas_call(
        functools.partial(main_kernel, (dp_count, rep_count, count_img)),
        out_shape=(
            jax.ShapeDtypeStruct((TAPS * 512, 512), F32),
            jax.ShapeDtypeStruct((2, 2, 2, 2, 2, 16, 512), F32),
            jax.ShapeDtypeStruct((24, 512), F32),
        ),
        in_specs=[smem, smem, vmem, vmem, vmem, vmem, hbm, hbm, hbm, hbm],
        out_specs=(hbm, hbm, vmem),
        scratch_shapes=scratch,
        compiler_params=pltpu.CompilerParams(
            collective_id=0, has_side_effects=True, vmem_limit_bytes=63 * 2**20
        ),
        name="reduce_and_precondition",
    )(
        micro_ids,
        labels,
        images,
        gain,
        shift,
        head.T,
        conv_weight.reshape(TAPS, 2, 2, 2, 2, 2, 16, 512),
        eig_scales,
        basis_in,
        basis_out,
    )
    tall = TAPS * 512 // CHUNKS
    head_shape = (NCLS, 513)
    outs = pl.pallas_call(
        update_kernel,
        out_shape=(
            jax.ShapeDtypeStruct((2,), F32),
            jax.ShapeDtypeStruct((1,), F32),
            *[jax.ShapeDtypeStruct((2, 512), F32)] * 3,
            *[jax.ShapeDtypeStruct(head_shape, F32)] * 3,
            *[jax.ShapeDtypeStruct((TAPS * 512, 512), F32)] * 3,
            jax.ShapeDtypeStruct(square, F32),
        ),
        in_specs=[vmem] * 8 + [hbm] * 5,
        out_specs=(smem, smem) + (vmem,) * 6 + (hbm,) * 4,
        scratch_shapes=[
            pltpu.VMEM((TAPS * 512, 512), F32),
            pltpu.VMEM((TAPS * 512, 512), F32),
            pltpu.VMEM((TAPS * 512, 512), BF16),
            pltpu.VMEM((TAPS * 512, 512), BF16),
            *[pltpu.VMEM((RING, tall, 512), F32)] * 3,
            pltpu.VMEM(square, F32),
            dma((4, CHUNKS)),
            dma((3, RING)),
            dma((2,)),
        ],
        compiler_params=pltpu.CompilerParams(vmem_limit_bytes=62 * 2**20),
        name="adamw",
    )(
        facts,
        gain,
        shift,
        norm_first,
        norm_second,
        head.T,
        head_first.T,
        head_second.T,
        precond,
        conv_weight,
        conv_first,
        conv_second,
        scales.reshape(square),
    )
    loss_parts, grad_norm, norm_new, norm_m, norm_v, head_new, head_m, head_v, conv_new, conv_m, conv_v, scales_new = outs
    return (
        loss_parts,
        grad_norm.reshape(()),
        conv_new,
        conv_m,
        conv_v,
        scales_new,
        norm_new,
        norm_m,
        norm_v,
        head_new.T,
        head_m.T,
        head_v.T,
    )


def solution(mesh):
    split_images = P(("dp", "rep"))
    in_specs = (P(("dp", "rep"), None, None, None), split_images, split_images) + (P(),) * 13
    sizes = (mesh.shape["dp"], mesh.shape["rep"])
    return jax.shard_map(
        functools.partial(shards, sizes), mesh=mesh, in_specs=in_specs, out_specs=(P(),) * 12, check_vma=False
    )
```

```python
import functools

import jax
import jax.numpy as jnp
from jax import lax
from jax.experimental import pallas as pl
from jax.experimental.pallas import tpu as pltpu
from jax.sharding import PartitionSpec as P

NCLS = 10
STEP = 5
NORM_EPS = 1e-05
DAMPING = 0.001
CLIP = 0.01
MESH = pl.DeviceIdType.MESH
F32 = jnp.float32
BF16 = jnp.bfloat16
HIGHEST = lax.Precision.HIGHEST
TAPS = 9
STAT = 9
AWAY = 4
UNITS = (13, 4, 14, 5, 7, 18, 3, 19, 15, 12, 0, 17, 9, 10, 16, 11, 6, 2, 1, 8)
RS_ORDER = (
    (3, 1, 2, 4), (1, 2, 3, 4), (1, 2, 3, 4), (2, 1, 3, 4), (3, 1, 4, 2),
    (1, 3, 4, 2), (1, 2, 3, 4), (3, 1, 2, 4), (1, 2, 3, 4), (2, 1, 3, 4),
    (2, 3, 4, 1), (2, 3, 1, 4), (1, 2, 3, 4), (2, 3, 1, 4), (1, 2, 3, 4),
    (3, 1, 4, 2), (1, 2, 3, 4), (2, 3, 4, 1), (2, 1, 3, 4), (1, 2, 3, 4),
)
AG_ORDER = (
    (1, 3, 4, 2), (3, 4, 2, 1), (2, 3, 1, 4), (1, 3, 4, 2), (1, 2, 3, 4),
    (1, 2, 3, 4), (3, 1, 2, 4), (1, 2, 3, 4), (2, 3, 4, 1), (3, 4, 1, 2),
    (2, 1, 3, 4), (2, 1, 3, 4), (1, 2, 3, 4), (2, 1, 3, 4), (2, 3, 1, 4),
    (3, 2, 1, 4), (1, 2, 3, 4), (2, 3, 4, 1), (1, 2, 3, 4), (2, 1, 3, 4),
)
TASKS = (
    (0, 13, 0), (0, 4, 0), (0, 14, 0), (5, 0, 0), (1, 13, 0), (0, 5, 0), (1, 4, 0), (1, 14, 0),
    (0, 7, 0), (0, 18, 0), (1, 5, 0), (1, 7, 0), (5, 1, 0), (0, 3, 0), (1, 18, 0), (0, 19, 0),
    (1, 3, 0), (1, 13, 1), (0, 15, 0), (1, 19, 0), (1, 14, 1), (1, 4, 1), (5, 2, 0), (0, 12, 0),
    (0, 0, 0), (1, 15, 0), (0, 17, 0), (1, 12, 0), (1, 7, 1), (1, 5, 1), (1, 0, 0), (1, 18, 1),
    (1, 17, 0), (0, 9, 0), (1, 13, 2), (0, 10, 0), (5, 3, 0), (0, 16, 0), (1, 9, 0), (1, 19, 1),
    (1, 3, 1), (1, 10, 0), (0, 11, 0), (1, 16, 0), (1, 4, 2), (1, 14, 2), (0, 6, 0), (1, 15, 1),
    (0, 2, 0), (1, 11, 0), (0, 1, 0), (1, 5, 2), (1, 6, 0), (0, 8, 0), (1, 2, 0), (1, 12, 1),
    (1, 1, 0), (1, 17, 1), (1, 8, 0), (1, 7, 2), (1, 0, 1), (1, 18, 2), (1, 9, 1), (5, 4, 0),
    (1, 13, 3), (1, 14, 3), (1, 4, 3), (1, 19, 2), (1, 3, 2), (1, 5, 3), (1, 17, 2), (1, 18, 3),
    (1, 10, 1), (1, 16, 1), (1, 13, 4), (1, 19, 3), (1, 14, 4), (1, 3, 3), (1, 15, 2), (1, 11, 1),
    (1, 17, 3), (1, 18, 4), (1, 10, 2), (1, 12, 2), (1, 6, 1), (1, 7, 3), (1, 4, 4), (1, 19, 4),
    (2, 9, 0), (1, 5, 4), (1, 3, 4), (2, 2, 0), (1, 15, 3), (1, 11, 2), (1, 16, 2), (1, 2, 1),
    (1, 12, 3), (1, 6, 2), (1, 10, 3), (1, 15, 4), (2, 7, 0), (1, 7, 4), (3, 18, 0), (1, 1, 1),
    (3, 19, 0), (1, 16, 3), (1, 2, 2), (3, 4, 0), (1, 6, 3), (3, 5, 0), (1, 12, 4), (2, 6, 0),
    (1, 8, 1), (3, 18, 1), (3, 14, 0), (3, 19, 1), (1, 1, 2), (3, 15, 0), (1, 0, 2), (1, 2, 3),
    (1, 16, 4), (3, 4, 1), (1, 9, 2), (1, 17, 4), (2, 8, 0), (3, 5, 1), (1, 8, 2), (1, 6, 4),
    (1, 11, 3), (2, 3, 0), (1, 10, 4), (3, 12, 0), (3, 14, 1), (1, 1, 3), (3, 18, 2), (3, 13, 0),
    (1, 0, 3), (1, 9, 3), (1, 2, 4), (2, 1, 0), (3, 19, 2), (3, 15, 1), (1, 8, 3), (3, 4, 2),
    (3, 16, 0), (3, 17, 0), (1, 11, 4), (2, 5, 0), (3, 5, 2), (3, 6, 0), (3, 12, 1), (3, 3, 0),
    (3, 7, 0), (3, 18, 3), (3, 14, 2), (3, 13, 1), (1, 1, 4), (3, 18, 4), (3, 19, 3), (4, 18, 0),
    (1, 0, 4), (2, 0, 0), (1, 9, 4), (3, 4, 3), (3, 15, 2), (3, 2, 0), (3, 19, 4), (3, 16, 1),
    (1, 8, 4), (2, 4, 0), (3, 6, 1), (4, 19, 0), (3, 4, 4), (4, 4, 0), (3, 12, 2), (3, 11, 0),
    (3, 10, 0), (3, 5, 3), (3, 17, 1), (3, 7, 1), (3, 3, 1), (3, 13, 2), (3, 5, 4), (4, 5, 0),
    (3, 0, 0), (3, 1, 0), (3, 14, 3), (3, 2, 1), (3, 8, 0), (3, 15, 3), (3, 11, 1), (3, 16, 2),
    (3, 6, 2), (3, 14, 4), (3, 9, 0), (4, 14, 0), (3, 10, 1), (3, 15, 4), (4, 15, 0), (3, 17, 2),
    (3, 7, 2), (3, 12, 3), (3, 3, 2), (3, 11, 2), (3, 12, 4), (3, 13, 3), (4, 12, 0), (3, 0, 1),
    (3, 1, 1), (3, 2, 2), (3, 13, 4), (4, 13, 0), (3, 8, 1), (3, 16, 3), (3, 9, 1), (3, 17, 3),
    (3, 16, 4), (4, 16, 0), (3, 10, 2), (3, 17, 4), (3, 6, 3), (4, 17, 0), (3, 0, 2), (3, 11, 3),
    (3, 6, 4), (4, 6, 0), (3, 7, 3), (3, 1, 2), (3, 11, 4), (4, 11, 0), (3, 2, 3), (3, 8, 2),
    (3, 7, 4), (4, 7, 0), (3, 3, 3), (3, 2, 4), (3, 9, 2), (4, 2, 0), (3, 10, 3), (3, 3, 4),
    (4, 3, 0), (3, 1, 3), (3, 0, 3), (3, 10, 4), (4, 10, 0), (3, 1, 4), (3, 8, 3), (4, 1, 0),
    (3, 0, 4), (3, 9, 3), (4, 0, 0), (3, 8, 4), (4, 8, 0), (3, 9, 4), (4, 9, 0),
)


def split(value):
    high = value.astype(BF16)
    return high, (value - high.astype(F32)).astype(BF16)


def dot(a, b, dims=((1,), (0,))):
    return lax.dot_general(a, b, (dims, ((), ())), preferred_element_type=F32)


def dot_exact(a, b, dims=((1,), (0,))):
    return lax.dot_general(a, b, (dims, ((), ())), precision=HIGHEST, preferred_element_type=F32)


def main_kernel(
    sizes,
    micro,
    labels,
    images,
    gain_ref,
    shift_ref,
    head,
    weight,
    eig_hbm,
    in_hbm,
    out_hbm,
    precond,
    scales,
    facts,
    work,
    half_sum,
    away,
    got0,
    got1,
    got2,
    got3,
    got4,
    got_more,
    small,
    small_got,
    tile_in,
    tile_core,
    tile_slots,
    tile_out,
    narrow,
    wide,
    conv,
    share,
    weight_low,
    turned_hi,
    box_hi,
    box_lo,
    grad_low,
    rot_hi,
    rot2_hi,
    rot2_lo,
    eig,
    in_hi,
    in_lo,
    in_t_hi,
    in_t_lo,
    out_hi,
    out_lo,
    out_t_hi,
    out_t_lo,
    gathered_hi,
    gathered_lo,
    result,
    rows_stat,
    pooled,
    shares,
    shares_x,
    dpool,
    head_pad,
    scale_rows,
    square_sum,
    w_sem,
    load_sem,
    out_sem,
    rs_send,
    rs_recv,
    ag_send,
    ag_recv,
    sm_send,
    sm_recv,
    core_send,
    core_recv,
    chip_send,
    chip_recv,
):
    dp_count, rep_count, count_img = sizes
    area = 64
    cells = 16
    chips = dp_count * rep_count // 2
    dp = lax.axis_index("dp")
    rep = lax.axis_index("rep")
    core = rep % 2
    chip = dp * (rep_count // 2) + rep // 2
    bits = [("rep", 1), ("dp", 1), ("rep", 2), ("dp", 2), ("dp", 4)]
    step = 8
    while step < dp_count:
        bits.append(("dp", step))
        step *= 2
    step = 4
    while step < rep_count:
        bits.append(("rep", step))
        step *= 2
    extra = len(bits) - 5
    mine = [((dp if name == "dp" else rep) // weight_of) % 2 for name, weight_of in bits]

    def partner(k):
        name, weight_of = bits[k]
        change = (1 - 2 * mine[k]) * weight_of
        return (dp + change, rep) if name == "dp" else (dp, rep + change)

    def chip_device(q):
        return (q // (rep_count // 2), (q % (rep_count // 2)) * 2 + core)

    def weight_copy(unit):
        tap, cols = unit // 2, pl.ds(pl.multiple_of((unit % 2) * 256, 256), 256)
        return pltpu.make_async_copy(weight.at[tap, :, :, :, :, :, :, cols], work.at[unit], w_sem.at[unit])

    def start_weight(unit, carry):
        weight_copy(unit).start()
        return carry

    lax.fori_loop(0, 2 * TAPS, start_weight, 0)
    loads = [
        pltpu.make_async_copy(src, dst, load_sem.at[k])
        for k, (src, dst) in enumerate(
            (
                (in_hbm.at[:, 0:256], result.at[0]),
                (in_hbm.at[:, 256:512], result.at[1]),
                (out_hbm.at[:, 0:256], result.at[2]),
                (out_hbm.at[:, 256:512], result.at[3]),
                (eig_hbm, eig),
            )
        )
    ]
    for copy in loads:
        copy.start()

    barrier = pltpu.get_barrier_semaphore()

    def greet(k, carry):
        pl.semaphore_signal(barrier, inc=1, device_id=chip_device((chip + k) % chips), device_id_type=MESH)
        return carry

    lax.fori_loop(1, chips, greet, 0)
    pl.semaphore_signal(barrier, inc=1, device_id=partner(0), device_id_type=MESH)

    stride = count_img * 8
    column = lax.broadcasted_iota(jnp.int32, (2, 8, 512), 1)
    for k in range(3):
        narrow[k, 0:stride] = jnp.zeros((stride, 512), BF16)
        narrow[k, 9 * stride : 10 * stride] = jnp.zeros((stride, 512), BF16)

    def build(h, carry):
        for pair in range(count_img // 2):
            block = images[2 * pair : 2 * pair + 2, h].astype(F32)
            left = jnp.where(column == 0, 0.0, pltpu.roll(block, 1, 1))
            right = jnp.where(column == 7, 0.0, pltpu.roll(block, 7, 1))
            at = pl.ds(pl.multiple_of((h + 1) * stride + 16 * pair, 16), 16)
            at_wide = pl.ds(pl.multiple_of(h * 128 + 16 * pair, 16), 16)
            for k, value in enumerate((left, block, right)):
                low = value.reshape(16, 512).astype(BF16)
                narrow[k, at] = low
                wide[k, at_wide] = low
        fill = pl.ds(pl.multiple_of(h * 128 + stride, 16), 128 - stride)
        for k in range(3):
            wide[k, fill] = jnp.zeros((128 - stride, 512), BF16)
        grad_low[fill] = jnp.zeros((128 - stride, 512), BF16)
        return carry

    lax.fori_loop(0, 8, build, 0)

    def clear(h, carry):
        conv[h] = jnp.zeros((stride, 512), F32)
        return carry

    lax.fori_loop(0, 8, clear, 0)

    def conv_row(dy, carry):
        for dx in range(3):
            for j in range(2):
                unit = 2 * (dy * 3 + dx) + j
                weight_copy(unit).wait()

                def cast(k, inner):
                    piece = work[unit, k // 4, (k // 2) % 2, k % 2].reshape(64, 256)
                    weight_low[dx, pl.ds(pl.multiple_of(k * 64, 64), 64), j * 256 : j * 256 + 256] = piece.astype(BF16)
                    return inner

                lax.fori_loop(0, 8, cast, 0)
        for m in range(2):
            for n in range(2):
                total = None
                for dx in range(3):
                    rows = pl.ds(pl.multiple_of(dy * stride + m * 4 * stride, 16), 4 * stride)
                    term = dot(narrow[dx, rows], weight_low[dx, :, n * 256 : n * 256 + 256])
                    total = term if total is None else total + term
                conv[4 * m : 4 * m + 4, :, n * 256 : n * 256 + 256] += total.reshape(4, stride, 256)
        return carry

    lax.fori_loop(0, 3, conv_row, 0)

    def member(n):
        return [jnp.where(micro[n] == m, 1.0, 0.0).astype(F32) for m in range(3)]

    def gather_sums(n, carry):
        at = pl.ds(pl.multiple_of(n * 8, 8), 8)
        first = jnp.zeros((8, 512), F32)
        second = jnp.zeros((8, 512), F32)
        for h in range(8):
            value = conv[h, at]
            first = first + value
            second = second + value * value
        kinds = member(n)
        return tuple(c + k * first for c, k in zip(carry[:3], kinds)) + tuple(
            c + k * second for c, k in zip(carry[3:6], kinds)
        )

    zero_tile = jnp.zeros((8, 512), F32)
    sums = lax.fori_loop(0, count_img, gather_sums, (zero_tile,) * 6)
    counts = [jnp.zeros((), F32)] * 3
    for n in range(count_img):
        counts = [c + k for c, k in zip(counts, member(n))]
    row8 = lax.broadcasted_iota(jnp.int32, (8, 512), 0)
    lane8 = lax.broadcasted_iota(jnp.int32, (8, 512), 1)

    def stack_rows(rows):
        tile = zero_tile
        for k, row in enumerate(rows):
            tile = jnp.where(row8 == k, jnp.broadcast_to(row, (8, 512)), tile)
        return tile

    count_row = zero_tile
    for m in range(3):
        count_row = jnp.where(lane8 % 256 == m, counts[m], count_row)
    tile_in[0] = jnp.where(row8 == 6, count_row, stack_rows([jnp.sum(s, axis=0, keepdims=True) for s in sums]))

    def core_half(which):
        return pl.ds(pl.multiple_of(which * 256, 256), 256)

    def tile_copy(i):
        return pltpu.make_async_remote_copy(
            src_ref=tile_in.at[i, :, core_half(1 - core)],
            dst_ref=tile_core.at[i],
            send_sem=core_send.at[2 * i],
            recv_sem=core_recv.at[2 * i],
            device_id=partner(0),
            device_id_type=MESH,
        )

    def tile_start(i):
        tile_copy(i).start()
        tile_copy(i).wait()
        tile_slots[i, 0] = tile_in[i, :, core_half(core)] + tile_core[i]

        def give(k, carry):
            pltpu.make_async_remote_copy(
                src_ref=tile_slots.at[i, 0],
                dst_ref=tile_slots.at[i, k],
                send_sem=chip_send.at[i],
                recv_sem=chip_recv.at[i],
                device_id=chip_device((chip + k) % chips),
                device_id_type=MESH,
            ).start()
            return carry

        lax.fori_loop(1, chips, give, 0)

    def tile_end(i):
        others = tile_slots.at[i, pl.ds(1, chips - 1)]
        pltpu.make_async_remote_copy(
            src_ref=others,
            dst_ref=others,
            send_sem=chip_send.at[i],
            recv_sem=chip_recv.at[i],
            device_id=partner(0),
            device_id_type=MESH,
        ).wait()

        def add(k, total):
            return total + tile_slots[i, (chip - k + chips) % chips]

        tile_out[i, core] = lax.fori_loop(0, chips, add, jnp.zeros((8, 256), F32))
        back = pltpu.make_async_remote_copy(
            src_ref=tile_out.at[i, core],
            dst_ref=tile_out.at[i, core],
            send_sem=core_send.at[2 * i + 1],
            recv_sem=core_recv.at[2 * i + 1],
            device_id=partner(0),
            device_id_type=MESH,
        )
        back.start()
        back.wait()
        return jnp.concatenate([tile_out[i, 0], tile_out[i, 1]], axis=1)

    pl.semaphore_wait(barrier, chips)
    tile_start(0)

    for copy in loads:
        copy.wait()
    value = jnp.concatenate([result[0], result[1]], axis=1)
    in_hi[...], in_lo[...] = split(value)
    in_t_hi[...], in_t_lo[...] = split(value.T)
    value = jnp.concatenate([result[2], result[3]], axis=1)
    out_hi[...], out_lo[...] = split(value)
    out_t_hi[...], out_t_lo[...] = split(value.T)
    for dx in range(3):
        turned_hi[dx, :, 0:128] = jnp.zeros((512, 128), BF16)
        turned_hi[dx, :, 1152:1280] = jnp.zeros((512, 128), BF16)

    def turn(j, carry):
        total = None
        for dx in range(3):
            rows = wide[dx, pl.ds(pl.multiple_of(256 * j, 256), 256)]
            value = dot(in_t_hi[...], rows, ((1,), (1,))) + dot(in_t_lo[...], rows, ((1,), (1,)))
            at = pl.ds(pl.multiple_of(128 + 256 * j, 128), 256)
            turned_hi[dx, :, at] = value.astype(BF16)
            total = value * value if total is None else total + value * value
        result[j] = total
        return carry

    lax.fori_loop(0, 4, turn, 0)

    def squares(h):
        return result[h // 2, :, (h % 2) * 128 : (h % 2) * 128 + 128]

    for h in range(8):
        value = squares(h)
        if h > 0:
            value = value + squares(h - 1)
        if h < 7:
            value = value + squares(h + 1)
        box_hi[:, h * 128 : h * 128 + 128], box_lo[:, h * 128 : h * 128 + 128] = split(value)

    totals = tile_end(0)

    gain = gain_ref[...]
    shift = shift_ref[...]
    live_total = totals[6:7, 0:1] + totals[6:7, 1:2] + totals[6:7, 2:3]
    pixels = [totals[6:7, m : m + 1] * float(area) for m in range(3)]
    mean_rows, rstd_rows = [], []
    for m in range(3):
        mean = totals[m : m + 1] / pixels[m]
        var = totals[3 + m : 4 + m] / pixels[m] - mean * mean
        mean_rows.append(mean)
        rstd_rows.append(lax.rsqrt(var + NORM_EPS))
    rows_stat[0] = stack_rows(mean_rows)
    rows_stat[1] = stack_rows(rstd_rows)

    def image_rows(n, k):
        kinds = member(n)
        row = sum(kinds[m] * rows_stat[k, m : m + 1] for m in range(3))
        return row, 1.0 - (kinds[0] + kinds[1] + kinds[2])

    even = lax.broadcasted_iota(jnp.int32, (8, 512), 0) % 2 == 0
    pooled[...] = jnp.zeros((16, 512), F32)
    shares[...] = jnp.zeros((16, 512), F32)
    shares_x[...] = jnp.zeros((16, 512), F32)

    def forward(n, carry):
        mean, dead = image_rows(n, 0)
        rstd, _ = image_rows(n, 1)
        rstd = rstd + dead
        at = pl.ds(pl.multiple_of(n * 8, 8), 8)
        cell_sum, share_sum, share_x_sum = zero_tile, zero_tile, zero_tile
        for a in range(4):
            xs = [(conv[2 * a + k, at] - mean) * rstd for k in range(2)]
            exps = [jnp.exp(gain * x + shift) for x in xs]
            both = exps[0] + exps[1]
            both = both + jnp.where(even, pltpu.roll(both, 7, 0), pltpu.roll(both, 1, 0))
            both = both + 4.0
            cell_sum = cell_sum + jnp.log(both)
            inverse = 1.0 / both
            for k in range(2):
                part = exps[k] * inverse
                share[2 * a + k, at] = part
                share_sum = share_sum + part
                share_x_sum = share_x_sum + part * xs[k]
        row = pl.ds(n, 1)
        pooled[row] = jnp.sum(cell_sum, axis=0, keepdims=True) * (0.5 / cells)
        shares[row] = jnp.sum(share_sum, axis=0, keepdims=True)
        shares_x[row] = jnp.sum(share_x_sum, axis=0, keepdims=True)
        return carry

    lax.fori_loop(0, count_img, forward, 0)

    head_pad[...] = jnp.zeros((128, 640), F32)
    head_pad[0:NCLS, 0:513] = head[...]
    head_rows = head_pad[:, 0:512].astype(BF16)
    pooled_low = pooled[...].astype(BF16)
    logits = dot(pooled_low, head_rows, ((1,), (1,))) + head_pad[:, 512:640].T[0:1, :]
    row16 = lax.broadcasted_iota(jnp.int32, (16, 128), 0)
    lane16 = lax.broadcasted_iota(jnp.int32, (16, 128), 1)
    label_of = jnp.zeros((16, 128), jnp.int32)
    micro_of = jnp.full((16, 128), 3, jnp.int32)
    for n in range(count_img):
        label_of = jnp.where(row16 == n, labels[n], label_of)
        micro_of = jnp.where(row16 == n, micro[n], micro_of)
    is_class = lane16 < NCLS
    live = jnp.where(micro_of < 3, 1.0, 0.0)
    onehot = jnp.where(lane16 == label_of, 1.0, 0.0)
    top = jnp.max(jnp.where(is_class, logits, -3e38), axis=1, keepdims=True)
    shifted = jnp.where(is_class, logits - top, 0.0)
    log_sum = jnp.log(jnp.sum(jnp.where(is_class, jnp.exp(shifted), 0.0), axis=1, keepdims=True))
    logp = jnp.where(is_class, shifted - log_sum, 0.0)
    per_img = -(
        0.9 * jnp.sum(onehot * logp, axis=1, keepdims=True) + 0.1 / NCLS * jnp.sum(logp, axis=1, keepdims=True)
    )
    loss = jnp.sum(live[:, 0:1] * per_img, axis=0, keepdims=True)
    dlogits = jnp.where(is_class, jnp.exp(logp) - 0.9 * onehot - 0.1 / NCLS, 0.0) * (live / live_total)
    dpool[...] = dot_exact(dlogits, head_rows.astype(F32)) * (1.0 / cells)
    head_grad = dot_exact(dlogits, pooled_low.astype(F32), ((0,), (0,)))
    row16w = lax.broadcasted_iota(jnp.int32, (16, 512), 0)
    bias_grad = jnp.concatenate(
        [jnp.sum(dlogits, axis=0, keepdims=True), jnp.zeros((1, 384), F32)], axis=1
    )
    block = jnp.where(row16w < NCLS, head_grad[0:16], 0.0)
    block = jnp.where(row16w == NCLS, bias_grad, block)
    small[...] = jnp.where(row16w == NCLS + 1, loss, block)

    back_rows = []
    for which in (shares, shares_x):
        for m in range(3):
            inside = jnp.where(micro_of[:, 0:1] == m, 1.0, 0.0)
            back_rows.append(jnp.sum(inside * (dpool[...] * which[...]), axis=0, keepdims=True))
    tile_in[1] = stack_rows(back_rows)
    tile_start(1)
    totals = tile_end(1)
    norm_grads = [
        totals[3:4] + totals[4:5] + totals[5:6],
        totals[0:1] + totals[1:2] + totals[2:3],
    ]
    rows_stat[2] = stack_rows([gain * totals[m : m + 1] / pixels[m] for m in range(3)])
    rows_stat[3] = stack_rows([gain * totals[3 + m : 4 + m] / pixels[m] for m in range(3)])

    def backward(pair, carry):
        parts = []
        for k in range(2):
            n = 2 * pair + k
            mean, dead = image_rows(n, 0)
            rstd, _ = image_rows(n, 1)
            rstd = rstd + dead
            offset, _ = image_rows(n, 2)
            slope, _ = image_rows(n, 3)
            parts.append((mean, rstd, offset, slope, gain * dpool[pl.ds(n, 1)], pl.ds(pl.multiple_of(n * 8, 8), 8)))
        for h in range(8):
            values = []
            for mean, rstd, offset, slope, factor, at in parts:
                xhat = (conv[h, at] - mean) * rstd
                values.append(rstd * (factor * share[h, at] - offset - xhat * slope))
            rows = pl.ds(pl.multiple_of(h * 128 + 16 * pair, 16), 16)
            grad_low[rows] = jnp.concatenate(values, axis=0).astype(BF16)
        return carry

    lax.fori_loop(0, count_img // 2, backward, 0)

    def rotate(k, carry):
        rows = pl.ds(pl.multiple_of(k * 256, 256), 256)
        value = dot(grad_low[rows], out_hi[...]) + dot(grad_low[rows], out_lo[...])
        rot_hi[rows] = value.astype(BF16)
        rot2_hi[rows], rot2_lo[rows] = split(value * value)
        return carry

    lax.fori_loop(0, 4, rotate, 0)

    got = (got0, got1, got2, got3, got4)
    left_home = set()

    def region(unit, fixed, first=1):
        return (unit,) + tuple(fixed.get(k, slice(None)) for k in range(first, 5))

    def rs_copy(unit, stage):
        if stage < 5:
            order = (0,) + RS_ORDER[unit]
            fixed = {k: mine[k] for k in order[:stage]}
            fixed[order[stage]] = 1 - mine[order[stage]]
            target, to = got[stage].at[unit], partner(order[stage])
        else:
            fixed = dict(enumerate(mine[:5]))
            target, to = got_more.at[unit, stage - 5], partner(stage)
        source = half_sum.at[region(unit, fixed)] if stage else away.at[UNITS.index(unit) % AWAY]
        return pltpu.make_async_remote_copy(
            src_ref=source,
            dst_ref=target,
            send_sem=rs_send.at[unit, stage],
            recv_sem=rs_recv.at[unit, stage],
            device_id=to,
            device_id_type=MESH,
        )

    def ag_copy(unit, stage):
        order = (0,) + AG_ORDER[unit]
        where = work.at[region(unit, {k: mine[k] for k in order[: 5 - stage]}, 0)]
        return pltpu.make_async_remote_copy(
            src_ref=where,
            dst_ref=where,
            send_sem=ag_send.at[unit, stage],
            recv_sem=ag_recv.at[unit, stage],
            device_id=partner(order[4 - stage]),
            device_id_type=MESH,
        )

    def sm_copy(stage):
        return pltpu.make_async_remote_copy(
            src_ref=small,
            dst_ref=small_got.at[stage],
            send_sem=sm_send.at[stage],
            recv_sem=sm_recv.at[stage],
            device_id=partner(stage),
            device_id_type=MESH,
        )

    def do_mm(unit, stage):
        tap, cols = unit // 2, slice((unit % 2) * 256, (unit % 2) * 256 + 256)
        dy, dx = tap // 3, tap % 3
        place = UNITS.index(unit)
        if place >= AWAY and UNITS[place - AWAY] not in left_home:
            left_home.add(UNITS[place - AWAY])
            rs_copy(UNITS[place - AWAY], 0).wait_send()
        for stays, half in enumerate((1 - core, core)):
            rows = pl.ds(pl.multiple_of(half * 256, 256), 256)
            if tap == STAT:
                value = (
                    dot(box_hi[rows], rot2_hi[:, cols])
                    + dot(box_hi[rows], rot2_lo[:, cols])
                    + dot(box_lo[rows], rot2_hi[:, cols])
                )
            else:
                value = dot(turned_hi[dx, rows, dy * 128 : dy * 128 + 1024], rot_hi[:, cols])
            value = value.reshape(2, 2, 2, 2, 16, 256)
            if stays:
                half_sum[unit] = value
            else:
                away[place % AWAY] = value
                rs_copy(unit, 0).start()

    def do_rs(unit, stage):
        if stage == 0 and unit in left_home:
            rs_copy(unit, stage).wait_recv()
        else:
            rs_copy(unit, stage).wait()
            if stage == 0:
                left_home.add(unit)
        if stage < 5:
            fixed = {k: mine[k] for k in ((0,) + RS_ORDER[unit])[: stage + 1]}
            source, at = got[stage], (unit,)
        else:
            fixed = dict(enumerate(mine[:5]))
            source, at = got_more, (unit, stage - 5)
        left = [k for k in range(1, 5) if k not in fixed]

        def add(i, carry):
            inner = dict(fixed)
            where = at
            if len(left) >= 3:
                inner[left[0]], inner[left[1]] = i // 2, i % 2
                where = at + (i // 2, i % 2)
            half_sum[region(unit, inner)] += source[where]
            return carry

        if len(left) >= 3:
            lax.fori_loop(0, 4, add, 0)
        else:
            add(0, 0)
        if stage < 4 + extra:
            rs_copy(unit, stage + 1).start()
        if stage >= 4 and stage < 4 + extra:
            do_rs(unit, stage + 1)

    own = dict(enumerate(mine[:5]))
    own_block = (((mine[0] * 2 + mine[1]) * 2 + mine[2]) * 2 + mine[3]) * 2 + mine[4]

    def do_post(tap, stage):
        pair = (2 * tap, 2 * tap + 1)
        value = jnp.concatenate([half_sum[region(unit, own)] for unit in pair], axis=1)
        if tap == STAT:
            rows = pl.ds(pl.multiple_of(own_block * 16, 16), 16)
            value = 0.95 * eig[rows] + 0.05 * (value * (live_total * float(area * area)))
            scale_rows[...] = value + DAMPING
        else:
            high, low = split(value / scale_rows[...])
            value = dot(high, out_t_hi[...]) + dot(high, out_t_lo[...]) + dot(low, out_t_hi[...])
        for k, unit in enumerate(pair):
            work[region(unit, own, 0)] = value[:, 256 * k : 256 * k + 256]
            ag_copy(unit, 0).start()

    def do_ag(unit, stage):
        ag_copy(unit, stage).wait()
        if stage < 4:
            ag_copy(unit, stage + 1).start()

    done = []

    def result_copy(k):
        tap, cols = done[k] // 2, slice((done[k] % 2) * 256, (done[k] % 2) * 256 + 256)
        return pltpu.make_async_copy(result.at[k % 4], precond.at[pl.ds(tap * 512, 512), cols], out_sem.at[k % 4])

    scale_copies = [
        pltpu.make_async_copy(
            work.at[2 * STAT + k], scales.at[:, :, :, :, :, :, 256 * k : 256 * k + 256], out_sem.at[4 + k]
        )
        for k in range(2)
    ]

    def do_fin(unit, stage):
        if unit // 2 == STAT:
            scale_copies[unit % 2].start()
            return
        k = len(done)
        done.append(unit)
        if k >= 4:
            result_copy(k - 4).wait()

        def cut(i, carry):
            rows = pl.ds(pl.multiple_of(i * 64, 64), 64)
            value = work[unit, i // 4, (i // 2) % 2, i % 2].reshape(64, 256)
            gathered_hi[rows], gathered_lo[rows] = split(value)
            return carry

        lax.fori_loop(0, 8, cut, 0)

        def tile(i, carry):
            rows = pl.ds(pl.multiple_of(i * 256, 256), 256)
            value = (
                dot(in_hi[rows], gathered_hi[...])
                + dot(in_hi[rows], gathered_lo[...])
                + dot(in_lo[rows], gathered_hi[...])
            )
            result[k % 4, rows] = value
            square_sum[...] += jnp.sum((value * value).reshape(32, 8, 256), axis=0)
            return carry

        lax.fori_loop(0, 2, tile, 0)
        result_copy(k).start()

    def do_sm(stage, unused):
        sm_copy(stage).wait()
        small[...] += small_got[stage]
        if stage < 4 + extra:
            sm_copy(stage + 1).start()
        if stage >= 4 and stage < 4 + extra:
            do_sm(stage + 1, 0)

    square_sum[...] = jnp.zeros((8, 256), F32)
    sm_copy(0).start()
    run = (do_mm, do_rs, do_post, do_ag, do_fin, do_sm)
    for kind, which, stage in TASKS:
        run[kind](which, stage)

    block = small[...]
    head_part = jnp.where(row16w <= NCLS, block, 0.0)
    squared = (
        jnp.sum(jnp.sum(square_sum[...], axis=0, keepdims=True), axis=1, keepdims=True)
        + jnp.sum(norm_grads[0] * norm_grads[0] + norm_grads[1] * norm_grads[1], axis=1, keepdims=True)
        + jnp.sum(jnp.sum(head_part * head_part, axis=0, keepdims=True), axis=1, keepdims=True)
    )
    norm = jnp.sqrt(squared)
    factor = jnp.minimum(1.0, CLIP / (norm + 1e-06))
    facts[0:16] = block
    facts[16:24] = stack_rows(norm_grads + [block[NCLS + 1 : NCLS + 2], live_total, norm, factor])
    for k in range(max(len(done) - 4, 0), len(done)):
        result_copy(k).wait()
    for copy in scale_copies:
        copy.wait()


def adamw(weight, grad, first, second, rate):
    first = 0.9 * first + 0.1 * grad
    second = 0.999 * second + 0.001 * grad * grad
    step_size = first / (1.0 - 0.9**STEP) / (jnp.sqrt(second / (1.0 - 0.999**STEP)) + 1e-08)
    return (weight - rate * (step_size + 0.01 * weight), first, second)


def adamw_positive(weight, grad, first, second, rate):
    first = 0.9 * first + 0.1 * grad
    second = 0.999 * second + 0.001 * grad * grad
    scaled = second * (1.0 / (1.0 - 0.999**STEP))
    root = scaled * lax.rsqrt(scaled) + 1e-08
    step = first * (rate / (1.0 - 0.9**STEP)) / root
    return (weight * (1.0 - 0.01 * rate) - step, first, second)


CHUNKS = 18
RING = 4


def update_kernel(
    facts,
    gain,
    shift,
    norm_first,
    norm_second,
    head,
    head_first,
    head_second,
    precond,
    weight,
    first,
    second,
    scales,
    loss_parts,
    grad_norm,
    norm_new,
    norm_m,
    norm_v,
    head_new,
    head_m,
    head_v,
    conv_new,
    conv_m,
    conv_v,
    scales_new,
    in_precond,
    in_weight,
    in_first,
    in_second,
    out_new,
    out_m,
    out_v,
    scales_held,
    in_sem,
    out_sem,
    scale_sem,
):
    tall = TAPS * 512 // CHUNKS
    pairs = ((precond, in_precond), (weight, in_weight), (first, in_first), (second, in_second))
    outs = ((out_new, conv_new), (out_m, conv_m), (out_v, conv_v))

    def load(k, i):
        rows = pl.ds(pl.multiple_of(i * tall, tall), tall)
        return pltpu.make_async_copy(pairs[k][0].at[rows], pairs[k][1].at[rows], in_sem.at[k, i])

    def store(k, i):
        rows = pl.ds(pl.multiple_of(i * tall, tall), tall)
        return pltpu.make_async_copy(outs[k][0].at[i % RING], outs[k][1].at[rows], out_sem.at[k, i % RING])

    def start(i, carry):
        for k in range(4):
            load(k, i).start()
        return carry

    lax.fori_loop(0, CHUNKS, start, 0)
    scale_in = pltpu.make_async_copy(scales, scales_held, scale_sem.at[0])
    scale_out = pltpu.make_async_copy(scales_held, scales_new, scale_sem.at[1])
    scale_in.start()

    factor = facts[21:22, 0:1]
    loss_parts[0] = facts[18, 0]
    loss_parts[1] = facts[19, 0]
    grad_norm[0] = facts[20, 0]
    grads = factor * facts[16:18, :]
    weights = jnp.concatenate([gain[...], shift[...]], axis=0)
    norm_new[...], norm_m[...], norm_v[...] = adamw(weights, grads, norm_first[...], norm_second[...], 0.1)
    block = factor * facts[0:16, :]
    head_new[:, 0:512], head_m[:, 0:512], head_v[:, 0:512] = adamw(
        head[:, 0:512], block[0:NCLS], head_first[:, 0:512], head_second[:, 0:512], 0.05
    )
    bias = jnp.concatenate([block[0:16, 0:128], jnp.zeros((112, 128), F32)], axis=0).T[0:NCLS, NCLS : NCLS + 1]
    head_new[:, 512:513], head_m[:, 512:513], head_v[:, 512:513] = adamw(
        head[:, 512:513], bias, head_first[:, 512:513], head_second[:, 512:513], 0.05
    )

    def chunk(i, carry):
        for k in range(4):
            load(k, i).wait()

        @pl.when(i >= RING)
        def _():
            for k in range(3):
                store(k, i).wait()

        def piece(j, inner):
            rows = pl.ds(pl.multiple_of(i * tall + j * 32, 32), 32)
            at = pl.ds(pl.multiple_of(j * 32, 32), 32)
            out_new[i % RING, at], out_m[i % RING, at], out_v[i % RING, at] = adamw_positive(
                in_weight[rows],
                factor * in_precond[rows],
                in_first[rows].astype(F32),
                in_second[rows].astype(F32),
                0.02,
            )
            return inner

        lax.fori_loop(0, tall // 32, piece, 0)
        for k in range(3):
            store(k, i).start()
        return carry

    lax.fori_loop(0, CHUNKS, chunk, 0)
    scale_in.wait()
    scale_out.start()
    for i in range(CHUNKS - RING, CHUNKS):
        for k in range(3):
            store(k, i).wait()
    scale_out.wait()


def shards(
    sizes,
    images,
    micro_ids,
    labels,
    conv_weight,
    conv_first,
    conv_second,
    eig_scales,
    basis_in,
    basis_out,
    batchnorm_gain,
    batchnorm_shift,
    norm_first,
    norm_second,
    head,
    head_first,
    head_second,
):
    dp_count, rep_count = sizes
    count_img = images.shape[0]
    chips = dp_count * rep_count // 2
    bit_count = (dp_count * rep_count - 1).bit_length()
    extra = bit_count - 5
    vmem = pl.BlockSpec(memory_space=pltpu.VMEM)
    smem = pl.BlockSpec(memory_space=pltpu.SMEM)
    hbm = pl.BlockSpec(memory_space=pl.ANY)
    gain = batchnorm_gain.reshape(1, 512)
    shift = batchnorm_shift.reshape(1, 512)
    pixels = 8 * count_img
    square = (512, 512)
    dma = pltpu.SemaphoreType.DMA
    scratch = [
        pltpu.VMEM((20, 2, 2, 2, 2, 2, 16, 256), F32),
        pltpu.VMEM((20, 2, 2, 2, 2, 16, 256), F32),
        pltpu.VMEM((AWAY, 2, 2, 2, 2, 16, 256), F32),
        pltpu.VMEM((20, 2, 2, 2, 2, 16, 256), F32),
        pltpu.VMEM((20, 2, 2, 2, 16, 256), F32),
        pltpu.VMEM((20, 2, 2, 16, 256), F32),
        pltpu.VMEM((20, 2, 16, 256), F32),
        pltpu.VMEM((20, 16, 256), F32),
        pltpu.VMEM((20, extra, 16, 256) if extra else (1, 1, 8, 128), F32),
        pltpu.VMEM((16, 512), F32),
        pltpu.VMEM((bit_count, 16, 512), F32),
        pltpu.VMEM((2, 8, 512), F32),
        pltpu.VMEM((2, 8, 256), F32),
        pltpu.VMEM((2, chips, 8, 256), F32),
        pltpu.VMEM((2, 2, 8, 256), F32),
        pltpu.VMEM((3, 10 * pixels, 512), BF16),
        pltpu.VMEM((3, 1024, 512), BF16),
        pltpu.VMEM((8, pixels, 512), F32),
        pltpu.VMEM((8, pixels, 512), F32),
        pltpu.VMEM((3, 512, 512), BF16),
        pltpu.VMEM((3, 512, 1280), BF16),
        pltpu.VMEM((512, 1024), BF16),
        pltpu.VMEM((512, 1024), BF16),
        pltpu.VMEM((1024, 512), BF16),
    ]
    scratch += [pltpu.VMEM((1024, 512), BF16)] * 3
    scratch += [pltpu.VMEM(square, F32)]
    scratch += [pltpu.VMEM(square, BF16)] * 8 + [pltpu.VMEM((512, 256), BF16)] * 2
    scratch += [
        pltpu.VMEM((4, 512, 256), F32),
        pltpu.VMEM((4, 8, 512), F32),
        pltpu.VMEM((16, 512), F32),
        pltpu.VMEM((16, 512), F32),
        pltpu.VMEM((16, 512), F32),
        pltpu.VMEM((16, 512), F32),
        pltpu.VMEM((128, 640), F32),
        pltpu.VMEM((16, 512), F32),
        pltpu.VMEM((8, 256), F32),
        dma((2 * TAPS,)),
        dma((5,)),
        dma((6,)),
        dma((20, bit_count)),
        dma((20, bit_count)),
        dma((20, 5)),
        dma((20, 5)),
        dma((bit_count,)),
        dma((bit_count,)),
        dma((4,)),
        dma((4,)),
        dma((2,)),
        dma((2,)),
    ]
    precond, scales, facts = pl.pallas_call(
        functools.partial(main_kernel, (dp_count, rep_count, count_img)),
        out_shape=(
            jax.ShapeDtypeStruct((TAPS * 512, 512), F32),
            jax.ShapeDtypeStruct((2, 2, 2, 2, 2, 16, 512), F32),
            jax.ShapeDtypeStruct((24, 512), F32),
        ),
        in_specs=[smem, smem, vmem, vmem, vmem, vmem, hbm, hbm, hbm, hbm],
        out_specs=(hbm, hbm, vmem),
        scratch_shapes=scratch,
        compiler_params=pltpu.CompilerParams(
            collective_id=0, has_side_effects=True, vmem_limit_bytes=63 * 2**20
        ),
        name="reduce_and_precondition",
    )(
        micro_ids,
        labels,
        images,
        gain,
        shift,
        head.T,
        conv_weight.reshape(TAPS, 2, 2, 2, 2, 2, 16, 512),
        eig_scales,
        basis_in,
        basis_out,
    )
    tall = TAPS * 512 // CHUNKS
    head_shape = (NCLS, 513)
    outs = pl.pallas_call(
        update_kernel,
        out_shape=(
            jax.ShapeDtypeStruct((2,), F32),
            jax.ShapeDtypeStruct((1,), F32),
            *[jax.ShapeDtypeStruct((2, 512), F32)] * 3,
            *[jax.ShapeDtypeStruct(head_shape, F32)] * 3,
            *[jax.ShapeDtypeStruct((TAPS * 512, 512), F32)] * 3,
            jax.ShapeDtypeStruct(square, F32),
        ),
        in_specs=[vmem] * 8 + [hbm] * 5,
        out_specs=(smem, smem) + (vmem,) * 6 + (hbm,) * 4,
        scratch_shapes=[
            pltpu.VMEM((TAPS * 512, 512), F32),
            pltpu.VMEM((TAPS * 512, 512), F32),
            pltpu.VMEM((TAPS * 512, 512), BF16),
            pltpu.VMEM((TAPS * 512, 512), BF16),
            *[pltpu.VMEM((RING, tall, 512), F32)] * 3,
            pltpu.VMEM(square, F32),
            dma((4, CHUNKS)),
            dma((3, RING)),
            dma((2,)),
        ],
        compiler_params=pltpu.CompilerParams(vmem_limit_bytes=62 * 2**20),
        name="adamw",
    )(
        facts,
        gain,
        shift,
        norm_first,
        norm_second,
        head.T,
        head_first.T,
        head_second.T,
        precond,
        conv_weight,
        conv_first,
        conv_second,
        scales.reshape(square),
    )
    loss_parts, grad_norm, norm_new, norm_m, norm_v, head_new, head_m, head_v, conv_new, conv_m, conv_v, scales_new = outs
    return (
        loss_parts,
        grad_norm.reshape(()),
        conv_new,
        conv_m,
        conv_v,
        scales_new,
        norm_new,
        norm_m,
        norm_v,
        head_new.T,
        head_m.T,
        head_v.T,
    )


def solution(mesh):
    split_images = P(("dp", "rep"))
    in_specs = (P(("dp", "rep"), None, None, None), split_images, split_images) + (P(),) * 13
    sizes = (mesh.shape["dp"], mesh.shape["rep"])
    return jax.shard_map(
        functools.partial(shards, sizes), mesh=mesh, in_specs=in_specs, out_specs=(P(),) * 12, check_vma=False
    )
```

```python
import functools

import jax
import jax.numpy as jnp
from jax import lax
from jax.experimental import pallas as pl
from jax.experimental.pallas import tpu as pltpu
from jax.sharding import PartitionSpec as P

NCLS = 10
STEP = 5
NORM_EPS = 1e-05
DAMPING = 0.001
CLIP = 0.01
MESH = pl.DeviceIdType.MESH
F32 = jnp.float32
BF16 = jnp.bfloat16
HIGHEST = lax.Precision.HIGHEST
TAPS = 9
STAT = 9
AWAY = 4
UNITS = (13, 4, 14, 5, 7, 18, 3, 19, 15, 12, 0, 17, 9, 10, 16, 11, 6, 2, 1, 8)
RS_ORDER = (
    (3, 1, 2, 4), (1, 2, 3, 4), (1, 2, 3, 4), (2, 1, 3, 4), (3, 1, 4, 2),
    (1, 3, 4, 2), (1, 2, 3, 4), (3, 1, 2, 4), (1, 2, 3, 4), (2, 1, 3, 4),
    (2, 3, 4, 1), (2, 3, 1, 4), (1, 2, 3, 4), (2, 3, 1, 4), (1, 2, 3, 4),
    (3, 1, 4, 2), (1, 2, 3, 4), (2, 3, 4, 1), (2, 1, 3, 4), (1, 2, 3, 4),
)
AG_ORDER = (
    (1, 3, 4, 2), (3, 4, 2, 1), (2, 3, 1, 4), (1, 3, 4, 2), (1, 2, 3, 4),
    (1, 2, 3, 4), (3, 1, 2, 4), (1, 2, 3, 4), (2, 3, 4, 1), (3, 4, 1, 2),
    (2, 1, 3, 4), (2, 1, 3, 4), (1, 2, 3, 4), (2, 1, 3, 4), (2, 3, 1, 4),
    (3, 2, 1, 4), (1, 2, 3, 4), (2, 3, 4, 1), (1, 2, 3, 4), (2, 1, 3, 4),
)
TASKS = (
    (0, 13, 0), (0, 4, 0), (0, 14, 0), (5, 0, 0), (1, 13, 0), (0, 5, 0), (1, 4, 0), (1, 14, 0),
    (0, 7, 0), (0, 18, 0), (1, 5, 0), (1, 7, 0), (5, 1, 0), (0, 3, 0), (1, 18, 0), (0, 19, 0),
    (1, 3, 0), (1, 13, 1), (0, 15, 0), (1, 19, 0), (1, 14, 1), (1, 4, 1), (5, 2, 0), (0, 12, 0),
    (0, 0, 0), (1, 15, 0), (0, 17, 0), (1, 12, 0), (1, 7, 1), (1, 5, 1), (1, 0, 0), (1, 18, 1),
    (1, 17, 0), (0, 9, 0), (1, 13, 2), (0, 10, 0), (5, 3, 0), (0, 16, 0), (1, 9, 0), (1, 19, 1),
    (1, 3, 1), (1, 10, 0), (0, 11, 0), (1, 16, 0), (1, 4, 2), (1, 14, 2), (0, 6, 0), (1, 15, 1),
    (0, 2, 0), (1, 11, 0), (0, 1, 0), (1, 5, 2), (1, 6, 0), (0, 8, 0), (1, 2, 0), (1, 12, 1),
    (1, 1, 0), (1, 17, 1), (1, 8, 0), (1, 7, 2), (1, 0, 1), (1, 18, 2), (1, 9, 1), (5, 4, 0),
    (1, 13, 3), (1, 14, 3), (1, 4, 3), (1, 19, 2), (1, 3, 2), (1, 5, 3), (1, 17, 2), (1, 18, 3),
    (1, 10, 1), (1, 16, 1), (1, 13, 4), (1, 19, 3), (1, 14, 4), (1, 3, 3), (1, 15, 2), (1, 11, 1),
    (1, 17, 3), (1, 18, 4), (1, 10, 2), (1, 12, 2), (1, 6, 1), (1, 7, 3), (1, 4, 4), (1, 19, 4),
    (2, 9, 0), (1, 5, 4), (1, 3, 4), (2, 2, 0), (1, 15, 3), (1, 11, 2), (1, 16, 2), (1, 2, 1),
    (1, 12, 3), (1, 6, 2), (1, 10, 3), (1, 15, 4), (2, 7, 0), (1, 7, 4), (3, 18, 0), (1, 1, 1),
    (3, 19, 0), (1, 16, 3), (1, 2, 2), (3, 4, 0), (1, 6, 3), (3, 5, 0), (1, 12, 4), (2, 6, 0),
    (1, 8, 1), (3, 18, 1), (3, 14, 0), (3, 19, 1), (1, 1, 2), (3, 15, 0), (1, 0, 2), (1, 2, 3),
    (1, 16, 4), (3, 4, 1), (1, 9, 2), (1, 17, 4), (2, 8, 0), (3, 5, 1), (1, 8, 2), (1, 6, 4),
    (1, 11, 3), (2, 3, 0), (1, 10, 4), (3, 12, 0), (3, 14, 1), (1, 1, 3), (3, 18, 2), (3, 13, 0),
    (1, 0, 3), (1, 9, 3), (1, 2, 4), (2, 1, 0), (3, 19, 2), (3, 15, 1), (1, 8, 3), (3, 4, 2),
    (3, 16, 0), (3, 17, 0), (1, 11, 4), (2, 5, 0), (3, 5, 2), (3, 6, 0), (3, 12, 1), (3, 3, 0),
    (3, 7, 0), (3, 18, 3), (3, 14, 2), (3, 13, 1), (1, 1, 4), (3, 18, 4), (3, 19, 3), (4, 18, 0),
    (1, 0, 4), (2, 0, 0), (1, 9, 4), (3, 4, 3), (3, 15, 2), (3, 2, 0), (3, 19, 4), (3, 16, 1),
    (1, 8, 4), (2, 4, 0), (3, 6, 1), (4, 19, 0), (3, 4, 4), (4, 4, 0), (3, 12, 2), (3, 11, 0),
    (3, 10, 0), (3, 5, 3), (3, 17, 1), (3, 7, 1), (3, 3, 1), (3, 13, 2), (3, 5, 4), (4, 5, 0),
    (3, 0, 0), (3, 1, 0), (3, 14, 3), (3, 2, 1), (3, 8, 0), (3, 15, 3), (3, 11, 1), (3, 16, 2),
    (3, 6, 2), (3, 14, 4), (3, 9, 0), (4, 14, 0), (3, 10, 1), (3, 15, 4), (4, 15, 0), (3, 17, 2),
    (3, 7, 2), (3, 12, 3), (3, 3, 2), (3, 11, 2), (3, 12, 4), (3, 13, 3), (4, 12, 0), (3, 0, 1),
    (3, 1, 1), (3, 2, 2), (3, 13, 4), (4, 13, 0), (3, 8, 1), (3, 16, 3), (3, 9, 1), (3, 17, 3),
    (3, 16, 4), (4, 16, 0), (3, 10, 2), (3, 17, 4), (3, 6, 3), (4, 17, 0), (3, 0, 2), (3, 11, 3),
    (3, 6, 4), (4, 6, 0), (3, 7, 3), (3, 1, 2), (3, 11, 4), (4, 11, 0), (3, 2, 3), (3, 8, 2),
    (3, 7, 4), (4, 7, 0), (3, 3, 3), (3, 2, 4), (3, 9, 2), (4, 2, 0), (3, 10, 3), (3, 3, 4),
    (4, 3, 0), (3, 1, 3), (3, 0, 3), (3, 10, 4), (4, 10, 0), (3, 1, 4), (3, 8, 3), (4, 1, 0),
    (3, 0, 4), (3, 9, 3), (4, 0, 0), (3, 8, 4), (4, 8, 0), (3, 9, 4), (4, 9, 0),
)
GOT_COUNT = (6, 17, 14, 10, 11)
RECV_COUNT, SEND_COUNT = 59, 20
RS_SLOT = (
    (4, 11, 12, 2, 5), (1, 15, 0, 1, 0), (4, 14, 3, 0, 3), (0, 7, 7, 6, 6), (1, 2, 1, 2, 3),
    (3, 4, 3, 3, 5), (3, 2, 2, 4, 2), (4, 3, 4, 8, 8), (2, 16, 1, 4, 7), (1, 12, 13, 3, 6),
    (2, 13, 0, 2, 10), (0, 1, 1, 9, 4), (3, 9, 10, 1, 0), (0, 0, 0, 0, 0), (2, 1, 2, 1, 1),
    (2, 8, 9, 0, 7), (5, 0, 11, 3, 1), (0, 10, 8, 7, 9), (5, 5, 5, 4, 2), (1, 6, 6, 5, 4),
)
AG_RECV = (
    (12, 17, 10, 24, 6), (29, 6, 11, 4, 1), (22, 14, 18, 12, 2), (4, 28, 4, 23, 0), (2, 8, 0, 20, 1),
    (3, 9, 17, 26, 2), (2, 9, 33, 20, 0), (18, 10, 3, 22, 1), (15, 38, 13, 5, 0), (34, 8, 14, 16, 2),
    (25, 35, 9, 15, 3), (24, 31, 5, 21, 3), (10, 3, 23, 37, 2), (13, 6, 11, 16, 0), (5, 11, 19, 13, 0),
    (7, 15, 21, 30, 1), (1, 8, 32, 7, 1), (16, 27, 36, 19, 2), (0, 4, 12, 5, 58), (1, 6, 14, 7, 0),
)
RS_SEND = (
    (10, 10, 10, 10, 10), (18, 18, 4, 4, 4), (17, 17, 14, 14, 14), (6, 6, 6, 6, 2), (1, 1, 1, 1, 1),
    (3, 3, 3, 3, 3), (16, 16, 11, 11, 11), (4, 4, 4, 4, 4), (19, 19, 17, 17, 17), (12, 12, 12, 12, 12),
    (13, 13, 13, 5, 5), (15, 15, 7, 7, 7), (9, 9, 9, 9, 9), (0, 0, 0, 0, 0), (2, 2, 2, 2, 2),
    (8, 8, 8, 6, 6), (14, 14, 14, 13, 13), (11, 11, 11, 11, 8), (5, 5, 5, 5, 5), (7, 7, 7, 7, 0),
)
AG_SEND = (
    (1, 1, 1, 1, 1), (4, 3, 3, 3, 3), (14, 12, 6, 6, 5), (16, 16, 16, 13, 6), (2, 2, 2, 2, 2),
    (3, 3, 3, 3, 3), (11, 11, 11, 11, 7), (18, 18, 15, 12, 7), (8, 8, 2, 2, 0), (14, 4, 4, 4, 1),
    (7, 7, 7, 0, 0), (19, 5, 5, 5, 5), (9, 5, 5, 2, 2), (16, 9, 9, 9, 2), (6, 6, 6, 6, 4),
    (15, 15, 15, 10, 10), (8, 8, 0, 0, 0), (13, 13, 13, 10, 8), (0, 0, 0, 0, 0), (1, 1, 1, 1, 0),
)


def split(value):
    high = value.astype(BF16)
    return high, (value - high.astype(F32)).astype(BF16)


def dot(a, b, dims=((1,), (0,))):
    return lax.dot_general(a, b, (dims, ((), ())), preferred_element_type=F32)


def dot_exact(a, b, dims=((1,), (0,))):
    return lax.dot_general(a, b, (dims, ((), ())), precision=HIGHEST, preferred_element_type=F32)


def main_kernel(
    sizes,
    micro_hbm,
    labels_hbm,
    images_hbm,
    gain_hbm,
    shift_hbm,
    head_hbm,
    weight,
    eig_hbm,
    in_hbm,
    out_hbm,
    precond,
    scales,
    facts,
    micro,
    labels,
    images,
    gain_ref,
    shift_ref,
    head,
    work,
    half_sum,
    away,
    got0,
    got1,
    got2,
    got3,
    got4,
    got_more,
    small,
    small_got,
    tile_in,
    tile_core,
    tile_slots,
    tile_out,
    narrow,
    wide,
    conv,
    share,
    weight_low,
    turned_hi,
    box_hi,
    box_lo,
    grad_low,
    rot_hi,
    rot2_hi,
    rot2_lo,
    basis_out,
    eig,
    in_hi,
    in_lo,
    in_t_hi,
    in_t_lo,
    out_hi,
    out_lo,
    out_t_hi,
    out_t_lo,
    gathered_hi,
    gathered_lo,
    result,
    rows_stat,
    pooled,
    shares,
    shares_x,
    dpool,
    head_pad,
    scale_rows,
    square_sum,
    w_sem,
    load_sem,
    out_sem,
    send_sem,
    recv_sem,
    more_sem,
    sm_send,
    sm_recv,
    core_send,
    core_recv,
    chip_send,
    chip_recv,
):
    dp_count, rep_count, count_img = sizes
    area = 64
    cells = 16
    chips = dp_count * rep_count // 2
    dp = lax.axis_index("dp")
    rep = lax.axis_index("rep")
    core = rep % 2
    chip = dp * (rep_count // 2) + rep // 2
    bits = [("rep", 1), ("dp", 1), ("rep", 2), ("dp", 2), ("dp", 4)]
    step = 8
    while step < dp_count:
        bits.append(("dp", step))
        step *= 2
    step = 4
    while step < rep_count:
        bits.append(("rep", step))
        step *= 2
    extra = len(bits) - 5
    mine = [((dp if name == "dp" else rep) // weight_of) % 2 for name, weight_of in bits]

    def partner(k):
        name, weight_of = bits[k]
        change = (1 - 2 * mine[k]) * weight_of
        return (dp + change, rep) if name == "dp" else (dp, rep + change)

    def chip_device(q):
        return (q // (rep_count // 2), (q % (rep_count // 2)) * 2 + core)

    first_loads = [
        pltpu.make_async_copy(src, dst, load_sem.at[5 + k])
        for k, (src, dst) in enumerate(
            (
                (images_hbm, images),
                (micro_hbm, micro),
                (labels_hbm, labels),
                (gain_hbm, gain_ref),
                (shift_hbm, shift_ref),
                (head_hbm, head),
            )
        )
    ]
    first_loads[0].start()
    first_loads[1].start()
    def weight_copy(unit):
        tap, cols = unit // 2, pl.ds(pl.multiple_of((unit % 2) * 256, 256), 256)
        return pltpu.make_async_copy(weight.at[tap, :, :, :, :, :, :, cols], work.at[unit], w_sem.at[unit])

    def start_weight(unit, carry):
        weight_copy(unit).start()
        return carry

    lax.fori_loop(0, 2 * TAPS, start_weight, 0)
    loads = [
        pltpu.make_async_copy(src, dst, load_sem.at[k])
        for k, (src, dst) in enumerate(
            (
                (in_hbm.at[:, 0:256], result.at[0]),
                (in_hbm.at[:, 256:512], result.at[1]),
                (out_hbm.at[:, 0:256], basis_out.at[0]),
                (out_hbm.at[:, 256:512], basis_out.at[1]),
                (eig_hbm, eig),
            )
        )
    ]
    for copy in loads + first_loads[2:]:
        copy.start()

    barrier = pltpu.get_barrier_semaphore()

    def greet(k, carry):
        pl.semaphore_signal(barrier, inc=1, device_id=chip_device((chip + k) % chips), device_id_type=MESH)
        return carry

    lax.fori_loop(1, chips, greet, 0)
    pl.semaphore_signal(barrier, inc=1, device_id=partner(0), device_id_type=MESH)

    stride = count_img * 8
    column = lax.broadcasted_iota(jnp.int32, (2, 8, 512), 1)
    for k in range(3):
        narrow[k, 0:stride] = jnp.zeros((stride, 512), BF16)
        narrow[k, 9 * stride : 10 * stride] = jnp.zeros((stride, 512), BF16)

    def build(h, carry):
        for pair in range(count_img // 2):
            block = images[2 * pair : 2 * pair + 2, h].astype(F32)
            left = jnp.where(column == 0, 0.0, pltpu.roll(block, 1, 1))
            right = jnp.where(column == 7, 0.0, pltpu.roll(block, 7, 1))
            at = pl.ds(pl.multiple_of((h + 1) * stride + 16 * pair, 16), 16)
            at_wide = pl.ds(pl.multiple_of(h * 128 + 16 * pair, 16), 16)
            for k, value in enumerate((left, block, right)):
                low = value.reshape(16, 512).astype(BF16)
                narrow[k, at] = low
                wide[k, at_wide] = low
        fill = pl.ds(pl.multiple_of(h * 128 + stride, 16), 128 - stride)
        for k in range(3):
            wide[k, fill] = jnp.zeros((128 - stride, 512), BF16)
        grad_low[fill] = jnp.zeros((128 - stride, 512), BF16)
        return carry

    first_loads[0].wait()
    lax.fori_loop(0, 8, build, 0)

    def clear(h, carry):
        conv[h] = jnp.zeros((stride, 512), F32)
        return carry

    lax.fori_loop(0, 8, clear, 0)

    def conv_row(dy, carry):
        for dx in range(3):
            for j in range(2):
                unit = 2 * (dy * 3 + dx) + j
                weight_copy(unit).wait()

                def cast(k, inner):
                    piece = work[unit, k // 4, (k // 2) % 2, k % 2].reshape(64, 256)
                    weight_low[dx, pl.ds(pl.multiple_of(k * 64, 64), 64), j * 256 : j * 256 + 256] = piece.astype(BF16)
                    return inner

                lax.fori_loop(0, 8, cast, 0)
        for m in range(2):
            for n in range(2):
                total = None
                for dx in range(3):
                    rows = pl.ds(pl.multiple_of(dy * stride + m * 4 * stride, 16), 4 * stride)
                    term = dot(narrow[dx, rows], weight_low[dx, :, n * 256 : n * 256 + 256])
                    total = term if total is None else total + term
                conv[4 * m : 4 * m + 4, :, n * 256 : n * 256 + 256] += total.reshape(4, stride, 256)
        return carry

    lax.fori_loop(0, 3, conv_row, 0)

    for copy in first_loads[1:]:
        copy.wait()
    def member(n):
        return [jnp.where(micro[n] == m, 1.0, 0.0).astype(F32) for m in range(3)]

    def gather_sums(n, carry):
        at = pl.ds(pl.multiple_of(n * 8, 8), 8)
        first = jnp.zeros((8, 512), F32)
        second = jnp.zeros((8, 512), F32)
        for h in range(8):
            value = conv[h, at]
            first = first + value
            second = second + value * value
        kinds = member(n)
        return tuple(c + k * first for c, k in zip(carry[:3], kinds)) + tuple(
            c + k * second for c, k in zip(carry[3:6], kinds)
        )

    zero_tile = jnp.zeros((8, 512), F32)
    sums = lax.fori_loop(0, count_img, gather_sums, (zero_tile,) * 6)
    counts = [jnp.zeros((), F32)] * 3
    for n in range(count_img):
        counts = [c + k for c, k in zip(counts, member(n))]
    row8 = lax.broadcasted_iota(jnp.int32, (8, 512), 0)
    lane8 = lax.broadcasted_iota(jnp.int32, (8, 512), 1)

    def stack_rows(rows):
        tile = zero_tile
        for k, row in enumerate(rows):
            tile = jnp.where(row8 == k, jnp.broadcast_to(row, (8, 512)), tile)
        return tile

    count_row = zero_tile
    for m in range(3):
        count_row = jnp.where(lane8 % 256 == m, counts[m], count_row)
    tile_in[0] = jnp.where(row8 == 6, count_row, stack_rows([jnp.sum(s, axis=0, keepdims=True) for s in sums]))

    def core_half(which):
        return pl.ds(pl.multiple_of(which * 256, 256), 256)

    def tile_copy(i):
        return pltpu.make_async_remote_copy(
            src_ref=tile_in.at[i, :, core_half(1 - core)],
            dst_ref=tile_core.at[i],
            send_sem=core_send.at[2 * i],
            recv_sem=core_recv.at[2 * i],
            device_id=partner(0),
            device_id_type=MESH,
        )

    def tile_start(i):
        tile_copy(i).start()
        tile_copy(i).wait()
        tile_slots[i, 0] = tile_in[i, :, core_half(core)] + tile_core[i]

        def give(k, carry):
            pltpu.make_async_remote_copy(
                src_ref=tile_slots.at[i, 0],
                dst_ref=tile_slots.at[i, k],
                send_sem=chip_send.at[i],
                recv_sem=chip_recv.at[i],
                device_id=chip_device((chip + k) % chips),
                device_id_type=MESH,
            ).start()
            return carry

        lax.fori_loop(1, chips, give, 0)

    def tile_end(i):
        others = tile_slots.at[i, pl.ds(1, chips - 1)]
        pltpu.make_async_remote_copy(
            src_ref=others,
            dst_ref=others,
            send_sem=chip_send.at[i],
            recv_sem=chip_recv.at[i],
            device_id=partner(0),
            device_id_type=MESH,
        ).wait()

        def add(k, total):
            return total + tile_slots[i, (chip - k + chips) % chips]

        tile_out[i, core] = lax.fori_loop(0, chips, add, jnp.zeros((8, 256), F32))
        back = pltpu.make_async_remote_copy(
            src_ref=tile_out.at[i, core],
            dst_ref=tile_out.at[i, core],
            send_sem=core_send.at[2 * i + 1],
            recv_sem=core_recv.at[2 * i + 1],
            device_id=partner(0),
            device_id_type=MESH,
        )
        back.start()
        back.wait()
        return jnp.concatenate([tile_out[i, 0], tile_out[i, 1]], axis=1)

    pl.semaphore_wait(barrier, chips)
    tile_start(0)

    for copy in loads:
        copy.wait()
    value = jnp.concatenate([result[0], result[1]], axis=1)
    in_hi[...], in_lo[...] = split(value)
    in_t_hi[...], in_t_lo[...] = split(value.T)
    for dx in range(3):
        turned_hi[dx, :, 0:128] = jnp.zeros((512, 128), BF16)
        turned_hi[dx, :, 1152:1280] = jnp.zeros((512, 128), BF16)

    def turn(j, carry):
        total = None
        for dx in range(3):
            rows = wide[dx, pl.ds(pl.multiple_of(256 * j, 256), 256)]
            value = dot(in_t_hi[...], rows, ((1,), (1,))) + dot(in_t_lo[...], rows, ((1,), (1,)))
            at = pl.ds(pl.multiple_of(128 + 256 * j, 128), 256)
            turned_hi[dx, :, at] = value.astype(BF16)
            total = value * value if total is None else total + value * value
        result[j] = total
        return carry

    lax.fori_loop(0, 2, turn, 0)

    totals = tile_end(0)

    gain = gain_ref[...]
    shift = shift_ref[...]
    live_total = totals[6:7, 0:1] + totals[6:7, 1:2] + totals[6:7, 2:3]
    pixels = [totals[6:7, m : m + 1] * float(area) for m in range(3)]
    mean_rows, rstd_rows = [], []
    for m in range(3):
        mean = totals[m : m + 1] / pixels[m]
        var = totals[3 + m : 4 + m] / pixels[m] - mean * mean
        mean_rows.append(mean)
        rstd_rows.append(lax.rsqrt(var + NORM_EPS))
    rows_stat[0] = stack_rows(mean_rows)
    rows_stat[1] = stack_rows(rstd_rows)

    def image_rows(n, k):
        kinds = member(n)
        row = sum(kinds[m] * rows_stat[k, m : m + 1] for m in range(3))
        return row, 1.0 - (kinds[0] + kinds[1] + kinds[2])

    even = lax.broadcasted_iota(jnp.int32, (8, 512), 0) % 2 == 0
    pooled[...] = jnp.zeros((16, 512), F32)
    shares[...] = jnp.zeros((16, 512), F32)
    shares_x[...] = jnp.zeros((16, 512), F32)

    def forward(n, carry):
        mean, dead = image_rows(n, 0)
        rstd, _ = image_rows(n, 1)
        rstd = rstd + dead
        at = pl.ds(pl.multiple_of(n * 8, 8), 8)
        cell_sum, share_sum, share_x_sum = zero_tile, zero_tile, zero_tile
        for a in range(4):
            xs = [(conv[2 * a + k, at] - mean) * rstd for k in range(2)]
            exps = [jnp.exp(gain * x + shift) for x in xs]
            both = exps[0] + exps[1]
            both = both + jnp.where(even, pltpu.roll(both, 7, 0), pltpu.roll(both, 1, 0))
            both = both + 4.0
            cell_sum = cell_sum + jnp.log(both)
            inverse = 1.0 / both
            for k in range(2):
                part = exps[k] * inverse
                share[2 * a + k, at] = part
                share_sum = share_sum + part
                share_x_sum = share_x_sum + part * xs[k]
        row = pl.ds(n, 1)
        pooled[row] = jnp.sum(cell_sum, axis=0, keepdims=True) * (0.5 / cells)
        shares[row] = jnp.sum(share_sum, axis=0, keepdims=True)
        shares_x[row] = jnp.sum(share_x_sum, axis=0, keepdims=True)
        return carry

    lax.fori_loop(0, count_img, forward, 0)

    head_pad[...] = jnp.zeros((128, 640), F32)
    head_pad[0:NCLS, 0:513] = head[...]
    head_rows = head_pad[:, 0:512].astype(BF16)
    pooled_low = pooled[...].astype(BF16)
    logits = dot(pooled_low, head_rows, ((1,), (1,))) + head_pad[:, 512:640].T[0:1, :]
    row16 = lax.broadcasted_iota(jnp.int32, (16, 128), 0)
    lane16 = lax.broadcasted_iota(jnp.int32, (16, 128), 1)
    label_of = jnp.zeros((16, 128), jnp.int32)
    micro_of = jnp.full((16, 128), 3, jnp.int32)
    for n in range(count_img):
        label_of = jnp.where(row16 == n, labels[n], label_of)
        micro_of = jnp.where(row16 == n, micro[n], micro_of)
    is_class = lane16 < NCLS
    live = jnp.where(micro_of < 3, 1.0, 0.0)
    onehot = jnp.where(lane16 == label_of, 1.0, 0.0)
    top = jnp.max(jnp.where(is_class, logits, -3e38), axis=1, keepdims=True)
    shifted = jnp.where(is_class, logits - top, 0.0)
    log_sum = jnp.log(jnp.sum(jnp.where(is_class, jnp.exp(shifted), 0.0), axis=1, keepdims=True))
    logp = jnp.where(is_class, shifted - log_sum, 0.0)
    per_img = -(
        0.9 * jnp.sum(onehot * logp, axis=1, keepdims=True) + 0.1 / NCLS * jnp.sum(logp, axis=1, keepdims=True)
    )
    loss = jnp.sum(live[:, 0:1] * per_img, axis=0, keepdims=True)
    dlogits = jnp.where(is_class, jnp.exp(logp) - 0.9 * onehot - 0.1 / NCLS, 0.0) * (live / live_total)
    dpool[...] = dot_exact(dlogits, head_rows.astype(F32)) * (1.0 / cells)
    head_grad = dot_exact(dlogits, pooled_low.astype(F32), ((0,), (0,)))
    row16w = lax.broadcasted_iota(jnp.int32, (16, 512), 0)
    bias_grad = jnp.concatenate(
        [jnp.sum(dlogits, axis=0, keepdims=True), jnp.zeros((1, 384), F32)], axis=1
    )
    block = jnp.where(row16w < NCLS, head_grad[0:16], 0.0)
    block = jnp.where(row16w == NCLS, bias_grad, block)
    small[...] = jnp.where(row16w == NCLS + 1, loss, block)

    back_rows = []
    for which in (shares, shares_x):
        for m in range(3):
            inside = jnp.where(micro_of[:, 0:1] == m, 1.0, 0.0)
            back_rows.append(jnp.sum(inside * (dpool[...] * which[...]), axis=0, keepdims=True))
    tile_in[1] = stack_rows(back_rows)
    tile_start(1)

    lax.fori_loop(2, 4, turn, 0)
    def squares(h):
        return result[h // 2, :, (h % 2) * 128 : (h % 2) * 128 + 128]

    for h in range(8):
        value = squares(h)
        if h > 0:
            value = value + squares(h - 1)
        if h < 7:
            value = value + squares(h + 1)
        box_hi[:, h * 128 : h * 128 + 128], box_lo[:, h * 128 : h * 128 + 128] = split(value)

    value = jnp.concatenate([basis_out[0], basis_out[1]], axis=1)
    out_hi[...], out_lo[...] = split(value)
    out_t_hi[...], out_t_lo[...] = split(value.T)
    totals = tile_end(1)
    norm_grads = [
        totals[3:4] + totals[4:5] + totals[5:6],
        totals[0:1] + totals[1:2] + totals[2:3],
    ]
    rows_stat[2] = stack_rows([gain * totals[m : m + 1] / pixels[m] for m in range(3)])
    rows_stat[3] = stack_rows([gain * totals[3 + m : 4 + m] / pixels[m] for m in range(3)])

    def backward(pair, carry):
        parts = []
        for k in range(2):
            n = 2 * pair + k
            mean, dead = image_rows(n, 0)
            rstd, _ = image_rows(n, 1)
            rstd = rstd + dead
            offset, _ = image_rows(n, 2)
            slope, _ = image_rows(n, 3)
            parts.append((mean, rstd, offset, slope, gain * dpool[pl.ds(n, 1)], pl.ds(pl.multiple_of(n * 8, 8), 8)))
        for h in range(8):
            values = []
            for mean, rstd, offset, slope, factor, at in parts:
                xhat = (conv[h, at] - mean) * rstd
                values.append(rstd * (factor * share[h, at] - offset - xhat * slope))
            rows = pl.ds(pl.multiple_of(h * 128 + 16 * pair, 16), 16)
            grad_low[rows] = jnp.concatenate(values, axis=0).astype(BF16)
        return carry

    lax.fori_loop(0, count_img // 2, backward, 0)

    def rotate(k, carry):
        rows = pl.ds(pl.multiple_of(k * 256, 256), 256)
        value = dot(grad_low[rows], out_hi[...]) + dot(grad_low[rows], out_lo[...])
        rot_hi[rows] = value.astype(BF16)
        rot2_hi[rows], rot2_lo[rows] = split(value * value)
        return carry

    lax.fori_loop(0, 4, rotate, 0)

    got = (got0, got1, got2, got3, got4)
    left_home = set()

    def region(unit, fixed, first=1):
        return (unit,) + tuple(fixed.get(k, slice(None)) for k in range(first, 5))

    def rs_copy(unit, stage):
        if stage < 5:
            order = (0,) + RS_ORDER[unit]
            fixed = {k: mine[k] for k in order[:stage]}
            fixed[order[stage]] = 1 - mine[order[stage]]
            target, to = got[stage].at[RS_SLOT[unit][stage]], partner(order[stage])
            sems = (send_sem.at[RS_SEND[unit][stage]], recv_sem.at[sum(GOT_COUNT[:stage]) + RS_SLOT[unit][stage]])
        else:
            fixed = dict(enumerate(mine[:5]))
            target, to = got_more.at[unit, stage - 5], partner(stage)
            sems = (more_sem.at[0, unit, stage - 5], more_sem.at[1, unit, stage - 5])
        source = half_sum.at[region(unit, fixed)] if stage else away.at[UNITS.index(unit) % AWAY]
        return pltpu.make_async_remote_copy(
            src_ref=source,
            dst_ref=target,
            send_sem=sems[0],
            recv_sem=sems[1],
            device_id=to,
            device_id_type=MESH,
        )

    def ag_copy(unit, stage):
        order = (0,) + AG_ORDER[unit]
        where = work.at[region(unit, {k: mine[k] for k in order[: 5 - stage]}, 0)]
        return pltpu.make_async_remote_copy(
            src_ref=where,
            dst_ref=where,
            send_sem=send_sem.at[AG_SEND[unit][stage]],
            recv_sem=recv_sem.at[AG_RECV[unit][stage]],
            device_id=partner(order[4 - stage]),
            device_id_type=MESH,
        )

    def sm_copy(stage):
        return pltpu.make_async_remote_copy(
            src_ref=small,
            dst_ref=small_got.at[stage],
            send_sem=sm_send.at[stage],
            recv_sem=sm_recv.at[stage],
            device_id=partner(stage),
            device_id_type=MESH,
        )

    def do_mm(unit, stage):
        tap, cols = unit // 2, slice((unit % 2) * 256, (unit % 2) * 256 + 256)
        dy, dx = tap // 3, tap % 3
        place = UNITS.index(unit)
        if place >= AWAY and UNITS[place - AWAY] not in left_home:
            left_home.add(UNITS[place - AWAY])
            rs_copy(UNITS[place - AWAY], 0).wait_send()
        for stays, half in enumerate((1 - core, core)):
            rows = pl.ds(pl.multiple_of(half * 256, 256), 256)
            if tap == STAT:
                value = (
                    dot(box_hi[rows], rot2_hi[:, cols])
                    + dot(box_hi[rows], rot2_lo[:, cols])
                    + dot(box_lo[rows], rot2_hi[:, cols])
                )
            else:
                value = dot(turned_hi[dx, rows, dy * 128 : dy * 128 + 1024], rot_hi[:, cols])
            value = value.reshape(2, 2, 2, 2, 16, 256)
            if stays:
                half_sum[unit] = value
            else:
                away[place % AWAY] = value
                rs_copy(unit, 0).start()

    def do_rs(unit, stage):
        if stage == 0 and unit in left_home:
            rs_copy(unit, stage).wait_recv()
        else:
            rs_copy(unit, stage).wait()
            if stage == 0:
                left_home.add(unit)
        if stage < 5:
            fixed = {k: mine[k] for k in ((0,) + RS_ORDER[unit])[: stage + 1]}
            source, at = got[stage], (RS_SLOT[unit][stage],)
        else:
            fixed = dict(enumerate(mine[:5]))
            source, at = got_more, (unit, stage - 5)
        left = [k for k in range(1, 5) if k not in fixed]

        def add(i, carry):
            inner = dict(fixed)
            where = at
            if len(left) >= 3:
                inner[left[0]], inner[left[1]] = i // 2, i % 2
                where = at + (i // 2, i % 2)
            half_sum[region(unit, inner)] += source[where]
            return carry

        if len(left) >= 3:
            lax.fori_loop(0, 4, add, 0)
        else:
            add(0, 0)
        if stage < 4 + extra:
            rs_copy(unit, stage + 1).start()
        if stage >= 4 and stage < 4 + extra:
            do_rs(unit, stage + 1)

    own = dict(enumerate(mine[:5]))
    own_block = (((mine[0] * 2 + mine[1]) * 2 + mine[2]) * 2 + mine[3]) * 2 + mine[4]

    def do_post(tap, stage):
        pair = (2 * tap, 2 * tap + 1)
        value = jnp.concatenate([half_sum[region(unit, own)] for unit in pair], axis=1)
        if tap == STAT:
            rows = pl.ds(pl.multiple_of(own_block * 16, 16), 16)
            value = 0.95 * eig[rows] + 0.05 * (value * (live_total * float(area * area)))
            scale_rows[...] = value + DAMPING
        else:
            high, low = split(value / scale_rows[...])
            value = dot(high, out_t_hi[...]) + dot(high, out_t_lo[...]) + dot(low, out_t_hi[...])
        for k, unit in enumerate(pair):
            work[region(unit, own, 0)] = value[:, 256 * k : 256 * k + 256]
            ag_copy(unit, 0).start()

    def do_ag(unit, stage):
        ag_copy(unit, stage).wait()
        if stage < 4:
            ag_copy(unit, stage + 1).start()

    done = []

    def result_copy(k):
        tap, cols = done[k] // 2, slice((done[k] % 2) * 256, (done[k] % 2) * 256 + 256)
        return pltpu.make_async_copy(result.at[k % 4], precond.at[pl.ds(tap * 512, 512), cols], out_sem.at[k % 4])

    scale_copies = [
        pltpu.make_async_copy(
            work.at[2 * STAT + k], scales.at[:, :, :, :, :, :, 256 * k : 256 * k + 256], out_sem.at[4 + k]
        )
        for k in range(2)
    ]

    def do_fin(unit, stage):
        if unit // 2 == STAT:
            scale_copies[unit % 2].start()
            return
        k = len(done)
        done.append(unit)
        if k >= 4:
            result_copy(k - 4).wait()

        def cut(i, carry):
            rows = pl.ds(pl.multiple_of(i * 64, 64), 64)
            value = work[unit, i // 4, (i // 2) % 2, i % 2].reshape(64, 256)
            gathered_hi[rows], gathered_lo[rows] = split(value)
            return carry

        lax.fori_loop(0, 8, cut, 0)

        def tile(i, carry):
            rows = pl.ds(pl.multiple_of(i * 256, 256), 256)
            value = (
                dot(in_hi[rows], gathered_hi[...])
                + dot(in_hi[rows], gathered_lo[...])
                + dot(in_lo[rows], gathered_hi[...])
            )
            result[k % 4, rows] = value
            square_sum[...] += jnp.sum((value * value).reshape(32, 8, 256), axis=0)
            return carry

        lax.fori_loop(0, 2, tile, 0)
        result_copy(k).start()

    def do_sm(stage, unused):
        sm_copy(stage).wait()
        small[...] += small_got[stage]
        if stage < 4 + extra:
            sm_copy(stage + 1).start()
        if stage >= 4 and stage < 4 + extra:
            do_sm(stage + 1, 0)

    square_sum[...] = jnp.zeros((8, 256), F32)
    sm_copy(0).start()
    run = (do_mm, do_rs, do_post, do_ag, do_fin, do_sm)
    for kind, which, stage in TASKS:
        run[kind](which, stage)

    block = small[...]
    head_part = jnp.where(row16w <= NCLS, block, 0.0)
    squared = (
        jnp.sum(jnp.sum(square_sum[...], axis=0, keepdims=True), axis=1, keepdims=True)
        + jnp.sum(norm_grads[0] * norm_grads[0] + norm_grads[1] * norm_grads[1], axis=1, keepdims=True)
        + jnp.sum(jnp.sum(head_part * head_part, axis=0, keepdims=True), axis=1, keepdims=True)
    )
    norm = jnp.sqrt(squared)
    factor = jnp.minimum(1.0, CLIP / (norm + 1e-06))
    facts[0:16] = block
    facts[16:24] = stack_rows(norm_grads + [block[NCLS + 1 : NCLS + 2], live_total, norm, factor])
    for k in range(max(len(done) - 4, 0), len(done)):
        result_copy(k).wait()
    for copy in scale_copies:
        copy.wait()


def adamw(weight, grad, first, second, rate):
    first = 0.9 * first + 0.1 * grad
    second = 0.999 * second + 0.001 * grad * grad
    step_size = first / (1.0 - 0.9**STEP) / (jnp.sqrt(second / (1.0 - 0.999**STEP)) + 1e-08)
    return (weight - rate * (step_size + 0.01 * weight), first, second)


def adamw_positive(weight, grad, first, second, rate):
    first = 0.9 * first + 0.1 * grad
    second = 0.999 * second + 0.001 * grad * grad
    scaled = second * (1.0 / (1.0 - 0.999**STEP))
    root = scaled * lax.rsqrt(scaled) + 1e-08
    step = first * (rate / (1.0 - 0.9**STEP)) / root
    return (weight * (1.0 - 0.01 * rate) - step, first, second)


CHUNKS = 18
LOADS = 9
RING = 4


def update_kernel(
    facts,
    gain,
    shift,
    norm_first,
    norm_second,
    head,
    head_first,
    head_second,
    precond,
    weight,
    first,
    second,
    scales,
    loss_parts,
    grad_norm,
    norm_new,
    norm_m,
    norm_v,
    head_new,
    head_m,
    head_v,
    conv_new,
    conv_m,
    conv_v,
    scales_new,
    in_precond,
    in_weight,
    in_first,
    in_second,
    out_new,
    out_m,
    out_v,
    scales_held,
    in_sem,
    out_sem,
    scale_sem,
):
    tall = TAPS * 512 // CHUNKS
    pairs = ((precond, in_precond), (weight, in_weight), (first, in_first), (second, in_second))
    outs = ((out_new, conv_new), (out_m, conv_m), (out_v, conv_v))

    def load(k, i):
        deep = TAPS * 512 // LOADS
        rows = pl.ds(pl.multiple_of(i * deep, deep), deep)
        return pltpu.make_async_copy(pairs[k][0].at[rows], pairs[k][1].at[rows], in_sem.at[k, i])

    def store(k, i):
        rows = pl.ds(pl.multiple_of(i * tall, tall), tall)
        return pltpu.make_async_copy(outs[k][0].at[i % RING], outs[k][1].at[rows], out_sem.at[k, i % RING])

    def start(i, carry):
        for k in range(4):
            load(k, i).start()
        return carry

    lax.fori_loop(0, LOADS, start, 0)
    scale_in = pltpu.make_async_copy(scales, scales_held, scale_sem.at[0])
    scale_out = pltpu.make_async_copy(scales_held, scales_new, scale_sem.at[1])
    scale_in.start()

    factor = facts[21:22, 0:1]
    loss_parts[0] = facts[18, 0]
    loss_parts[1] = facts[19, 0]
    grad_norm[0] = facts[20, 0]
    grads = factor * facts[16:18, :]
    weights = jnp.concatenate([gain[...], shift[...]], axis=0)
    norm_new[...], norm_m[...], norm_v[...] = adamw(weights, grads, norm_first[...], norm_second[...], 0.1)
    block = factor * facts[0:16, :]
    head_new[:, 0:512], head_m[:, 0:512], head_v[:, 0:512] = adamw(
        head[:, 0:512], block[0:NCLS], head_first[:, 0:512], head_second[:, 0:512], 0.05
    )
    bias = jnp.concatenate([block[0:16, 0:128], jnp.zeros((112, 128), F32)], axis=0).T[0:NCLS, NCLS : NCLS + 1]
    head_new[:, 512:513], head_m[:, 512:513], head_v[:, 512:513] = adamw(
        head[:, 512:513], bias, head_first[:, 512:513], head_second[:, 512:513], 0.05
    )

    def chunk(i, carry):
        @pl.when(i % (CHUNKS // LOADS) == 0)
        def _():
            for k in range(4):
                load(k, i // (CHUNKS // LOADS)).wait()

        @pl.when(i >= RING)
        def _():
            for k in range(3):
                store(k, i).wait()

        def piece(j, inner):
            rows = pl.ds(pl.multiple_of(i * tall + j * 32, 32), 32)
            at = pl.ds(pl.multiple_of(j * 32, 32), 32)
            out_new[i % RING, at], out_m[i % RING, at], out_v[i % RING, at] = adamw_positive(
                in_weight[rows],
                factor * in_precond[rows],
                in_first[rows].astype(F32),
                in_second[rows].astype(F32),
                0.02,
            )
            return inner

        lax.fori_loop(0, tall // 32, piece, 0)
        for k in range(3):
            store(k, i).start()
        return carry

    lax.fori_loop(0, CHUNKS, chunk, 0)
    scale_in.wait()
    scale_out.start()
    for i in range(CHUNKS - RING, CHUNKS):
        for k in range(3):
            store(k, i).wait()
    scale_out.wait()


def shards(
    sizes,
    images,
    micro_ids,
    labels,
    conv_weight,
    conv_first,
    conv_second,
    eig_scales,
    basis_in,
    basis_out,
    batchnorm_gain,
    batchnorm_shift,
    norm_first,
    norm_second,
    head,
    head_first,
    head_second,
):
    dp_count, rep_count = sizes
    count_img = images.shape[0]
    chips = dp_count * rep_count // 2
    bit_count = (dp_count * rep_count - 1).bit_length()
    extra = bit_count - 5
    vmem = pl.BlockSpec(memory_space=pltpu.VMEM)
    smem = pl.BlockSpec(memory_space=pltpu.SMEM)
    hbm = pl.BlockSpec(memory_space=pl.ANY)
    gain = batchnorm_gain.reshape(1, 512)
    shift = batchnorm_shift.reshape(1, 512)
    pixels = 8 * count_img
    square = (512, 512)
    dma = pltpu.SemaphoreType.DMA
    scratch = [
        pltpu.SMEM((count_img,), jnp.int32),
        pltpu.SMEM((count_img,), jnp.int32),
        pltpu.VMEM(images.shape, BF16),
        pltpu.VMEM((1, 512), F32),
        pltpu.VMEM((1, 512), F32),
        pltpu.VMEM((NCLS, 513), F32),
        pltpu.VMEM((20, 2, 2, 2, 2, 2, 16, 256), F32),
        pltpu.VMEM((20, 2, 2, 2, 2, 16, 256), F32),
        pltpu.VMEM((AWAY, 2, 2, 2, 2, 16, 256), F32),
        pltpu.VMEM((GOT_COUNT[0], 2, 2, 2, 2, 16, 256), F32),
        pltpu.VMEM((GOT_COUNT[1], 2, 2, 2, 16, 256), F32),
        pltpu.VMEM((GOT_COUNT[2], 2, 2, 16, 256), F32),
        pltpu.VMEM((GOT_COUNT[3], 2, 16, 256), F32),
        pltpu.VMEM((GOT_COUNT[4], 16, 256), F32),
        pltpu.VMEM((20, extra, 16, 256) if extra else (1, 1, 8, 128), F32),
        pltpu.VMEM((16, 512), F32),
        pltpu.VMEM((bit_count, 16, 512), F32),
        pltpu.VMEM((2, 8, 512), F32),
        pltpu.VMEM((2, 8, 256), F32),
        pltpu.VMEM((2, chips, 8, 256), F32),
        pltpu.VMEM((2, 2, 8, 256), F32),
        pltpu.VMEM((3, 10 * pixels, 512), BF16),
        pltpu.VMEM((3, 1024, 512), BF16),
        pltpu.VMEM((8, pixels, 512), F32),
        pltpu.VMEM((8, pixels, 512), F32),
        pltpu.VMEM((3, 512, 512), BF16),
        pltpu.VMEM((3, 512, 1280), BF16),
        pltpu.VMEM((512, 1024), BF16),
        pltpu.VMEM((512, 1024), BF16),
        pltpu.VMEM((1024, 512), BF16),
    ]
    scratch += [pltpu.VMEM((1024, 512), BF16)] * 3
    scratch += [pltpu.VMEM((2, 512, 256), F32), pltpu.VMEM(square, F32)]
    scratch += [pltpu.VMEM(square, BF16)] * 8 + [pltpu.VMEM((512, 256), BF16)] * 2
    scratch += [
        pltpu.VMEM((4, 512, 256), F32),
        pltpu.VMEM((4, 8, 512), F32),
        pltpu.VMEM((16, 512), F32),
        pltpu.VMEM((16, 512), F32),
        pltpu.VMEM((16, 512), F32),
        pltpu.VMEM((16, 512), F32),
        pltpu.VMEM((128, 640), F32),
        pltpu.VMEM((16, 512), F32),
        pltpu.VMEM((8, 256), F32),
        dma((2 * TAPS,)),
        dma((11,)),
        dma((6,)),
        dma((SEND_COUNT,)),
        dma((RECV_COUNT,)),
        dma((2, 20, extra) if extra else (1, 1, 1)),
        dma((bit_count,)),
        dma((bit_count,)),
        dma((4,)),
        dma((4,)),
        dma((2,)),
        dma((2,)),
    ]
    precond, scales, facts = pl.pallas_call(
        functools.partial(main_kernel, (dp_count, rep_count, count_img)),
        out_shape=(
            jax.ShapeDtypeStruct((TAPS * 512, 512), F32),
            jax.ShapeDtypeStruct((2, 2, 2, 2, 2, 16, 512), F32),
            jax.ShapeDtypeStruct((24, 512), F32),
        ),
        in_specs=[hbm] * 10,
        out_specs=(hbm, hbm, vmem),
        scratch_shapes=scratch,
        compiler_params=pltpu.CompilerParams(
            collective_id=0, has_side_effects=True, vmem_limit_bytes=63 * 2**20
        ),
        name="reduce_and_precondition",
    )(
        micro_ids,
        labels,
        images,
        gain,
        shift,
        head.T,
        conv_weight.reshape(TAPS, 2, 2, 2, 2, 2, 16, 512),
        eig_scales,
        basis_in,
        basis_out,
    )
    tall = TAPS * 512 // CHUNKS
    head_shape = (NCLS, 513)
    outs = pl.pallas_call(
        update_kernel,
        out_shape=(
            jax.ShapeDtypeStruct((2,), F32),
            jax.ShapeDtypeStruct((1,), F32),
            *[jax.ShapeDtypeStruct((2, 512), F32)] * 3,
            *[jax.ShapeDtypeStruct(head_shape, F32)] * 3,
            *[jax.ShapeDtypeStruct((TAPS * 512, 512), F32)] * 3,
            jax.ShapeDtypeStruct(square, F32),
        ),
        in_specs=[vmem] * 8 + [hbm] * 5,
        out_specs=(smem, smem) + (vmem,) * 6 + (hbm,) * 4,
        scratch_shapes=[
            pltpu.VMEM((TAPS * 512, 512), F32),
            pltpu.VMEM((TAPS * 512, 512), F32),
            pltpu.VMEM((TAPS * 512, 512), BF16),
            pltpu.VMEM((TAPS * 512, 512), BF16),
            *[pltpu.VMEM((RING, tall, 512), F32)] * 3,
            pltpu.VMEM(square, F32),
            dma((4, LOADS)),
            dma((3, RING)),
            dma((2,)),
        ],
        compiler_params=pltpu.CompilerParams(vmem_limit_bytes=62 * 2**20),
        name="adamw",
    )(
        facts,
        gain,
        shift,
        norm_first,
        norm_second,
        head.T,
        head_first.T,
        head_second.T,
        precond,
        conv_weight,
        conv_first,
        conv_second,
        scales.reshape(square),
    )
    loss_parts, grad_norm, norm_new, norm_m, norm_v, head_new, head_m, head_v, conv_new, conv_m, conv_v, scales_new = outs
    return (
        loss_parts,
        grad_norm.reshape(()),
        conv_new,
        conv_m,
        conv_v,
        scales_new,
        norm_new,
        norm_m,
        norm_v,
        head_new.T,
        head_m.T,
        head_v.T,
    )


def solution(mesh):
    split_images = P(("dp", "rep"))
    in_specs = (P(("dp", "rep"), None, None, None), split_images, split_images) + (P(),) * 13
    sizes = (mesh.shape["dp"], mesh.shape["rep"])
    return jax.shard_map(
        functools.partial(shards, sizes), mesh=mesh, in_specs=in_specs, out_specs=(P(),) * 12, check_vma=False
    )
```

```python
import functools

import jax
import jax.numpy as jnp
from jax import lax
from jax.experimental import pallas as pl
from jax.experimental.pallas import tpu as pltpu
from jax.sharding import PartitionSpec as P

NCLS = 10
STEP = 5
NORM_EPS = 1e-05
DAMPING = 0.001
CLIP = 0.01
MESH = pl.DeviceIdType.MESH
F32 = jnp.float32
BF16 = jnp.bfloat16
HIGHEST = lax.Precision.HIGHEST
TAPS = 9
STAT = 9
AWAY = 4
UNITS = (13, 4, 14, 5, 7, 18, 3, 19, 15, 12, 0, 17, 9, 10, 16, 11, 6, 2, 1, 8)
RS_ORDER = (
    (3, 1, 2, 4), (1, 2, 3, 4), (1, 2, 3, 4), (2, 1, 3, 4), (3, 1, 4, 2),
    (1, 3, 4, 2), (1, 2, 3, 4), (3, 1, 2, 4), (1, 2, 3, 4), (2, 1, 3, 4),
    (2, 3, 4, 1), (2, 3, 1, 4), (1, 2, 3, 4), (2, 3, 1, 4), (1, 2, 3, 4),
    (3, 1, 4, 2), (1, 2, 3, 4), (2, 3, 4, 1), (2, 1, 3, 4), (1, 2, 3, 4),
)
AG_ORDER = (
    (1, 3, 4, 2), (3, 4, 2, 1), (2, 3, 1, 4), (1, 3, 4, 2), (1, 2, 3, 4),
    (1, 2, 3, 4), (3, 1, 2, 4), (1, 2, 3, 4), (2, 3, 4, 1), (3, 4, 1, 2),
    (2, 1, 3, 4), (2, 1, 3, 4), (1, 2, 3, 4), (2, 1, 3, 4), (2, 3, 1, 4),
    (3, 2, 1, 4), (1, 2, 3, 4), (2, 3, 4, 1), (1, 2, 3, 4), (2, 1, 3, 4),
)
TASKS = (
    (0, 13, 0), (0, 4, 0), (0, 14, 0), (5, 0, 0), (1, 13, 0), (0, 5, 0), (1, 4, 0), (1, 14, 0),
    (0, 7, 0), (0, 18, 0), (1, 5, 0), (1, 7, 0), (5, 1, 0), (0, 3, 0), (1, 18, 0), (0, 19, 0),
    (1, 3, 0), (1, 13, 1), (0, 15, 0), (1, 19, 0), (1, 14, 1), (1, 4, 1), (5, 2, 0), (0, 12, 0),
    (0, 0, 0), (1, 15, 0), (0, 17, 0), (1, 12, 0), (1, 7, 1), (1, 5, 1), (1, 0, 0), (1, 18, 1),
    (1, 17, 0), (0, 9, 0), (1, 13, 2), (0, 10, 0), (5, 3, 0), (0, 16, 0), (1, 9, 0), (1, 19, 1),
    (1, 3, 1), (1, 10, 0), (0, 11, 0), (1, 16, 0), (1, 4, 2), (1, 14, 2), (0, 6, 0), (1, 15, 1),
    (0, 2, 0), (1, 11, 0), (0, 1, 0), (1, 5, 2), (1, 6, 0), (0, 8, 0), (1, 2, 0), (1, 12, 1),
    (1, 1, 0), (1, 17, 1), (1, 8, 0), (1, 7, 2), (1, 0, 1), (1, 18, 2), (1, 9, 1), (5, 4, 0),
    (1, 13, 3), (1, 14, 3), (1, 4, 3), (1, 19, 2), (1, 3, 2), (1, 5, 3), (1, 17, 2), (1, 18, 3),
    (1, 10, 1), (1, 16, 1), (1, 13, 4), (1, 19, 3), (1, 14, 4), (1, 3, 3), (1, 15, 2), (1, 11, 1),
    (1, 17, 3), (1, 18, 4), (1, 10, 2), (1, 12, 2), (1, 6, 1), (1, 7, 3), (1, 4, 4), (1, 19, 4),
    (2, 9, 0), (1, 5, 4), (1, 3, 4), (2, 2, 0), (1, 15, 3), (1, 11, 2), (1, 16, 2), (1, 2, 1),
    (1, 12, 3), (1, 6, 2), (1, 10, 3), (1, 15, 4), (2, 7, 0), (1, 7, 4), (3, 18, 0), (1, 1, 1),
    (3, 19, 0), (1, 16, 3), (1, 2, 2), (3, 4, 0), (1, 6, 3), (3, 5, 0), (1, 12, 4), (2, 6, 0),
    (1, 8, 1), (3, 18, 1), (3, 14, 0), (3, 19, 1), (1, 1, 2), (3, 15, 0), (1, 0, 2), (1, 2, 3),
    (1, 16, 4), (3, 4, 1), (1, 9, 2), (1, 17, 4), (2, 8, 0), (3, 5, 1), (1, 8, 2), (1, 6, 4),
    (1, 11, 3), (2, 3, 0), (1, 10, 4), (3, 12, 0), (3, 14, 1), (1, 1, 3), (3, 18, 2), (3, 13, 0),
    (1, 0, 3), (1, 9, 3), (1, 2, 4), (2, 1, 0), (3, 19, 2), (3, 15, 1), (1, 8, 3), (3, 4, 2),
    (3, 16, 0), (3, 17, 0), (1, 11, 4), (2, 5, 0), (3, 5, 2), (3, 6, 0), (3, 12, 1), (3, 3, 0),
    (3, 7, 0), (3, 18, 3), (3, 14, 2), (3, 13, 1), (1, 1, 4), (3, 18, 4), (3, 19, 3), (4, 18, 0),
    (1, 0, 4), (2, 0, 0), (1, 9, 4), (3, 4, 3), (3, 15, 2), (3, 2, 0), (3, 19, 4), (3, 16, 1),
    (1, 8, 4), (2, 4, 0), (3, 6, 1), (4, 19, 0), (3, 4, 4), (4, 4, 0), (3, 12, 2), (3, 11, 0),
    (3, 10, 0), (3, 5, 3), (3, 17, 1), (3, 7, 1), (3, 3, 1), (3, 13, 2), (3, 5, 4), (4, 5, 0),
    (3, 0, 0), (3, 1, 0), (3, 14, 3), (3, 2, 1), (3, 8, 0), (3, 15, 3), (3, 11, 1), (3, 16, 2),
    (3, 6, 2), (3, 14, 4), (3, 9, 0), (4, 14, 0), (3, 10, 1), (3, 15, 4), (4, 15, 0), (3, 17, 2),
    (3, 7, 2), (3, 12, 3), (3, 3, 2), (3, 11, 2), (3, 12, 4), (3, 13, 3), (4, 12, 0), (3, 0, 1),
    (3, 1, 1), (3, 2, 2), (3, 13, 4), (4, 13, 0), (3, 8, 1), (3, 16, 3), (3, 9, 1), (3, 17, 3),
    (3, 16, 4), (4, 16, 0), (3, 10, 2), (3, 17, 4), (3, 6, 3), (4, 17, 0), (3, 0, 2), (3, 11, 3),
    (3, 6, 4), (4, 6, 0), (3, 7, 3), (3, 1, 2), (3, 11, 4), (4, 11, 0), (3, 2, 3), (3, 8, 2),
    (3, 7, 4), (4, 7, 0), (3, 3, 3), (3, 2, 4), (3, 9, 2), (4, 2, 0), (3, 10, 3), (3, 3, 4),
    (4, 3, 0), (3, 1, 3), (3, 0, 3), (3, 10, 4), (4, 10, 0), (3, 1, 4), (3, 8, 3), (4, 1, 0),
    (3, 0, 4), (3, 9, 3), (4, 0, 0), (3, 8, 4), (4, 8, 0), (3, 9, 4), (4, 9, 0),
)
GOT_COUNT = (6, 17, 14, 10, 11)
RECV_COUNT, SEND_COUNT = 59, 20
RS_SLOT = (
    (4, 11, 12, 2, 5), (1, 15, 0, 1, 0), (4, 14, 3, 0, 3), (0, 7, 7, 6, 6), (1, 2, 1, 2, 3),
    (3, 4, 3, 3, 5), (3, 2, 2, 4, 2), (4, 3, 4, 8, 8), (2, 16, 1, 4, 7), (1, 12, 13, 3, 6),
    (2, 13, 0, 2, 10), (0, 1, 1, 9, 4), (3, 9, 10, 1, 0), (0, 0, 0, 0, 0), (2, 1, 2, 1, 1),
    (2, 8, 9, 0, 7), (5, 0, 11, 3, 1), (0, 10, 8, 7, 9), (5, 5, 5, 4, 2), (1, 6, 6, 5, 4),
)
AG_RECV = (
    (12, 17, 10, 24, 6), (29, 6, 11, 4, 1), (22, 14, 18, 12, 2), (4, 28, 4, 23, 0), (2, 8, 0, 20, 1),
    (3, 9, 17, 26, 2), (2, 9, 33, 20, 0), (18, 10, 3, 22, 1), (15, 38, 13, 5, 0), (34, 8, 14, 16, 2),
    (25, 35, 9, 15, 3), (24, 31, 5, 21, 3), (10, 3, 23, 37, 2), (13, 6, 11, 16, 0), (5, 11, 19, 13, 0),
    (7, 15, 21, 30, 1), (1, 8, 32, 7, 1), (16, 27, 36, 19, 2), (0, 4, 12, 5, 58), (1, 6, 14, 7, 0),
)
RS_SEND = (
    (10, 10, 10, 10, 10), (18, 18, 4, 4, 4), (17, 17, 14, 14, 14), (6, 6, 6, 6, 2), (1, 1, 1, 1, 1),
    (3, 3, 3, 3, 3), (16, 16, 11, 11, 11), (4, 4, 4, 4, 4), (19, 19, 17, 17, 17), (12, 12, 12, 12, 12),
    (13, 13, 13, 5, 5), (15, 15, 7, 7, 7), (9, 9, 9, 9, 9), (0, 0, 0, 0, 0), (2, 2, 2, 2, 2),
    (8, 8, 8, 6, 6), (14, 14, 14, 13, 13), (11, 11, 11, 11, 8), (5, 5, 5, 5, 5), (7, 7, 7, 7, 0),
)
AG_SEND = (
    (1, 1, 1, 1, 1), (4, 3, 3, 3, 3), (14, 12, 6, 6, 5), (16, 16, 16, 13, 6), (2, 2, 2, 2, 2),
    (3, 3, 3, 3, 3), (11, 11, 11, 11, 7), (18, 18, 15, 12, 7), (8, 8, 2, 2, 0), (14, 4, 4, 4, 1),
    (7, 7, 7, 0, 0), (19, 5, 5, 5, 5), (9, 5, 5, 2, 2), (16, 9, 9, 9, 2), (6, 6, 6, 6, 4),
    (15, 15, 15, 10, 10), (8, 8, 0, 0, 0), (13, 13, 13, 10, 8), (0, 0, 0, 0, 0), (1, 1, 1, 1, 0),
)


def split(value):
    high = value.astype(BF16)
    return high, (value - high.astype(F32)).astype(BF16)


def dot(a, b, dims=((1,), (0,))):
    return lax.dot_general(a, b, (dims, ((), ())), preferred_element_type=F32)


def dot_exact(a, b, dims=((1,), (0,))):
    return lax.dot_general(a, b, (dims, ((), ())), precision=HIGHEST, preferred_element_type=F32)


def main_kernel(
    sizes,
    micro_hbm,
    labels_hbm,
    images_hbm,
    gain_hbm,
    shift_hbm,
    head_hbm,
    weight,
    eig_hbm,
    in_hbm,
    out_hbm,
    precond,
    scales,
    facts,
    micro,
    labels,
    images,
    gain_ref,
    shift_ref,
    head,
    work,
    half_sum,
    away,
    got0,
    got1,
    got2,
    got3,
    got4,
    got_more,
    small,
    small_got,
    tile_in,
    tile_core,
    tile_slots,
    tile_out,
    narrow,
    wide,
    conv,
    share,
    weight_low,
    turned_hi,
    box_hi,
    box_lo,
    grad_low,
    rot_hi,
    rot2_hi,
    rot2_lo,
    eig,
    in_hi,
    in_lo,
    in_t_hi,
    in_t_lo,
    out_hi,
    out_lo,
    out_t_hi,
    out_t_lo,
    gathered_hi,
    gathered_lo,
    rows_stat,
    pooled,
    shares,
    shares_x,
    dpool,
    head_pad,
    scale_rows,
    square_sum,
    w_sem,
    load_sem,
    send_sem,
    recv_sem,
    more_sem,
    sm_send,
    sm_recv,
    core_send,
    core_recv,
    chip_send,
    chip_recv,
):
    dp_count, rep_count, count_img = sizes
    area = 64
    cells = 16
    chips = dp_count * rep_count // 2
    dp = lax.axis_index("dp")
    rep = lax.axis_index("rep")
    core = rep % 2
    chip = dp * (rep_count // 2) + rep // 2
    bits = [("rep", 1), ("dp", 1), ("rep", 2), ("dp", 2), ("dp", 4)]
    step = 8
    while step < dp_count:
        bits.append(("dp", step))
        step *= 2
    step = 4
    while step < rep_count:
        bits.append(("rep", step))
        step *= 2
    extra = len(bits) - 5
    mine = [((dp if name == "dp" else rep) // weight_of) % 2 for name, weight_of in bits]

    own = dict(enumerate(mine[:5]))
    own_block = (((mine[0] * 2 + mine[1]) * 2 + mine[2]) * 2 + mine[3]) * 2 + mine[4]

    def partner(k):
        name, weight_of = bits[k]
        change = (1 - 2 * mine[k]) * weight_of
        return (dp + change, rep) if name == "dp" else (dp, rep + change)

    def chip_device(q):
        return (q // (rep_count // 2), (q % (rep_count // 2)) * 2 + core)

    first_loads = [
        pltpu.make_async_copy(src, dst, load_sem.at[5 + k])
        for k, (src, dst) in enumerate(
            (
                (images_hbm, images),
                (micro_hbm, micro),
                (labels_hbm, labels),
                (gain_hbm, gain_ref),
                (shift_hbm, shift_ref),
                (head_hbm, head),
            )
        )
    ]
    first_loads[0].start()
    first_loads[1].start()
    def weight_copy(unit):
        tap, cols = unit // 2, pl.ds(pl.multiple_of((unit % 2) * 256, 256), 256)
        return pltpu.make_async_copy(weight.at[tap, :, :, :, :, :, :, cols], work.at[unit], w_sem.at[unit])

    def start_weight(unit, carry):
        weight_copy(unit).start()
        return carry

    lax.fori_loop(0, 12, start_weight, 0)
    loads = [
        pltpu.make_async_copy(src, dst, load_sem.at[k])
        for k, (src, dst) in enumerate(
            (
                (in_hbm.at[:, :, :, :, :, :, 0:256], work.at[4]),
                (in_hbm.at[:, :, :, :, :, :, 256:512], work.at[5]),
                (out_hbm.at[:, :, :, :, :, :, 0:256], work.at[6]),
                (out_hbm.at[:, :, :, :, :, :, 256:512], work.at[7]),
                (eig_hbm.at[pl.ds(pl.multiple_of(own_block * 16, 16), 16)], eig),
            )
        )
    ]
    for copy in first_loads[2:]:
        copy.start()

    barrier = pltpu.get_barrier_semaphore()

    def greet(k, carry):
        pl.semaphore_signal(barrier, inc=1, device_id=chip_device((chip + k) % chips), device_id_type=MESH)
        return carry

    lax.fori_loop(1, chips, greet, 0)
    pl.semaphore_signal(barrier, inc=1, device_id=partner(0), device_id_type=MESH)

    stride = count_img * 8
    column = lax.broadcasted_iota(jnp.int32, (2, 8, 512), 1)
    for k in range(3):
        narrow[k, 0:stride] = jnp.zeros((stride, 512), BF16)
        narrow[k, 9 * stride : 10 * stride] = jnp.zeros((stride, 512), BF16)

    def build(h, carry):
        for pair in range(count_img // 2):
            block = images[2 * pair : 2 * pair + 2, h].astype(F32)
            left = jnp.where(column == 0, 0.0, pltpu.roll(block, 1, 1))
            right = jnp.where(column == 7, 0.0, pltpu.roll(block, 7, 1))
            at = pl.ds(pl.multiple_of((h + 1) * stride + 16 * pair, 16), 16)
            at_wide = pl.ds(pl.multiple_of(h * 128 + 16 * pair, 16), 16)
            for k, value in enumerate((left, block, right)):
                low = value.reshape(16, 512).astype(BF16)
                narrow[k, at] = low
                wide[k, at_wide] = low
        fill = pl.ds(pl.multiple_of(h * 128 + stride, 16), 128 - stride)
        for k in range(3):
            wide[k, fill] = jnp.zeros((128 - stride, 512), BF16)
        grad_low[fill] = jnp.zeros((128 - stride, 512), BF16)
        return carry

    first_loads[0].wait()
    lax.fori_loop(0, 8, build, 0)

    def wait_row(dy):
        for unit in range(6 * dy, 6 * dy + 6):
            weight_copy(unit).wait()

    def cast(dy, k):
        dx, j, half = k // 4, (k // 2) % 2, k % 2
        piece = work[2 * (3 * dy + dx) + j, half].reshape(256, 256)
        weight_low[dy % 2, dx, 256 * half : 256 * half + 256, 256 * j : 256 * j + 256] = piece.astype(BF16)

    wait_row(0)
    lax.fori_loop(12, 2 * TAPS, start_weight, 0)
    for k in range(12):
        cast(0, k)
    for dy in range(3):
        if dy < 2:
            wait_row(dy + 1)
        if dy == 1:
            for copy in loads:
                copy.start()
        for m in range(2):
            for n in range(2):
                total = None
                for dx in range(3):
                    begin = (dy + 4 * m) * stride
                    term = dot(
                        narrow[dx, begin : begin + 4 * stride], weight_low[dy % 2, dx, :, n * 256 : n * 256 + 256]
                    )
                    total = term if total is None else total + term
                    if dy < 2:
                        cast(dy + 1, 6 * m + 3 * n + dx)
                at = (slice(4 * m, 4 * m + 4), slice(None), slice(n * 256, n * 256 + 256))
                total = total.reshape(4, stride, 256)
                conv[at] = total if dy == 0 else conv[at] + total

    for copy in first_loads[1:]:
        copy.wait()
    def member(n):
        return [jnp.where(micro[n] == m, 1.0, 0.0).astype(F32) for m in range(3)]

    def gather_sums(n, carry):
        at = pl.ds(pl.multiple_of(n * 8, 8), 8)
        first = jnp.zeros((8, 512), F32)
        second = jnp.zeros((8, 512), F32)
        for h in range(8):
            value = conv[h, at]
            first = first + value
            second = second + value * value
        kinds = member(n)
        return tuple(c + k * first for c, k in zip(carry[:3], kinds)) + tuple(
            c + k * second for c, k in zip(carry[3:6], kinds)
        )

    zero_tile = jnp.zeros((8, 512), F32)
    sums = lax.fori_loop(0, count_img, gather_sums, (zero_tile,) * 6)
    counts = [jnp.zeros((), F32)] * 3
    for n in range(count_img):
        counts = [c + k for c, k in zip(counts, member(n))]
    row8 = lax.broadcasted_iota(jnp.int32, (8, 512), 0)
    lane8 = lax.broadcasted_iota(jnp.int32, (8, 512), 1)

    def stack_rows(rows):
        tile = zero_tile
        for k, row in enumerate(rows):
            tile = jnp.where(row8 == k, jnp.broadcast_to(row, (8, 512)), tile)
        return tile

    count_row = zero_tile
    for m in range(3):
        count_row = jnp.where(lane8 % 256 == m, counts[m], count_row)
    tile_in[0] = jnp.where(row8 == 6, count_row, stack_rows([jnp.sum(s, axis=0, keepdims=True) for s in sums]))

    def core_half(which):
        return pl.ds(pl.multiple_of(which * 256, 256), 256)

    def tile_copy(i):
        return pltpu.make_async_remote_copy(
            src_ref=tile_in.at[i, :, core_half(1 - core)],
            dst_ref=tile_core.at[i],
            send_sem=core_send.at[2 * i],
            recv_sem=core_recv.at[2 * i],
            device_id=partner(0),
            device_id_type=MESH,
        )

    def tile_start(i):
        tile_copy(i).start()
        tile_copy(i).wait()
        tile_slots[i, 0] = tile_in[i, :, core_half(core)] + tile_core[i]

        def give(k, carry):
            pltpu.make_async_remote_copy(
                src_ref=tile_slots.at[i, 0],
                dst_ref=tile_slots.at[i, k],
                send_sem=chip_send.at[i],
                recv_sem=chip_recv.at[i],
                device_id=chip_device((chip + k) % chips),
                device_id_type=MESH,
            ).start()
            return carry

        lax.fori_loop(1, chips, give, 0)

    def tile_end(i):
        others = tile_slots.at[i, pl.ds(1, chips - 1)]
        pltpu.make_async_remote_copy(
            src_ref=others,
            dst_ref=others,
            send_sem=chip_send.at[i],
            recv_sem=chip_recv.at[i],
            device_id=partner(0),
            device_id_type=MESH,
        ).wait()

        def add(k, total):
            return total + tile_slots[i, (chip - k + chips) % chips]

        tile_out[i, core] = lax.fori_loop(0, chips, add, jnp.zeros((8, 256), F32))
        back = pltpu.make_async_remote_copy(
            src_ref=tile_out.at[i, core],
            dst_ref=tile_out.at[i, core],
            send_sem=core_send.at[2 * i + 1],
            recv_sem=core_recv.at[2 * i + 1],
            device_id=partner(0),
            device_id_type=MESH,
        )
        back.start()
        back.wait()
        return jnp.concatenate([tile_out[i, 0], tile_out[i, 1]], axis=1)

    pl.semaphore_wait(barrier, chips)
    tile_start(0)

    for copy in loads:
        copy.wait()
    value = jnp.concatenate([work[4].reshape(512, 256), work[5].reshape(512, 256)], axis=1)
    in_hi[...], in_lo[...] = split(value)
    in_t_hi[...], in_t_lo[...] = split(value.T)
    for dx in range(3):
        turned_hi[dx, :, 0:128] = jnp.zeros((512, 128), BF16)
        turned_hi[dx, :, 1152:1280] = jnp.zeros((512, 128), BF16)

    def turn(j, carry):
        total = None
        for dx in range(3):
            rows = wide[dx, pl.ds(pl.multiple_of(256 * j, 256), 256)]
            value = dot(in_t_hi[...], rows, ((1,), (1,))) + dot(in_t_lo[...], rows, ((1,), (1,)))
            at = pl.ds(pl.multiple_of(128 + 256 * j, 128), 256)
            turned_hi[dx, :, at] = value.astype(BF16)
            total = value * value if total is None else total + value * value
        work[j] = total.reshape(2, 2, 2, 2, 2, 16, 256)
        return carry

    lax.fori_loop(0, 2, turn, 0)

    totals = tile_end(0)

    gain = gain_ref[...]
    shift = shift_ref[...]
    live_total = totals[6:7, 0:1] + totals[6:7, 1:2] + totals[6:7, 2:3]
    pixels = [totals[6:7, m : m + 1] * float(area) for m in range(3)]
    mean_rows, rstd_rows = [], []
    for m in range(3):
        mean = totals[m : m + 1] / pixels[m]
        var = totals[3 + m : 4 + m] / pixels[m] - mean * mean
        mean_rows.append(mean)
        rstd_rows.append(lax.rsqrt(var + NORM_EPS))
    rows_stat[0] = stack_rows(mean_rows)
    rows_stat[1] = stack_rows(rstd_rows)

    def image_rows(n, k):
        kinds = member(n)
        row = sum(kinds[m] * rows_stat[k, m : m + 1] for m in range(3))
        return row, 1.0 - (kinds[0] + kinds[1] + kinds[2])

    even = lax.broadcasted_iota(jnp.int32, (8, 512), 0) % 2 == 0
    pooled[...] = jnp.zeros((16, 512), F32)
    shares[...] = jnp.zeros((16, 512), F32)
    shares_x[...] = jnp.zeros((16, 512), F32)

    def forward(n, carry):
        mean, dead = image_rows(n, 0)
        rstd, _ = image_rows(n, 1)
        rstd = rstd + dead
        at = pl.ds(pl.multiple_of(n * 8, 8), 8)
        cell_sum, share_sum, share_x_sum = zero_tile, zero_tile, zero_tile
        for a in range(4):
            xs = [(conv[2 * a + k, at] - mean) * rstd for k in range(2)]
            exps = [jnp.exp(gain * x + shift) for x in xs]
            both = exps[0] + exps[1]
            both = both + jnp.where(even, pltpu.roll(both, 7, 0), pltpu.roll(both, 1, 0))
            both = both + 4.0
            cell_sum = cell_sum + jnp.log(both)
            inverse = 1.0 / both
            for k in range(2):
                part = exps[k] * inverse
                share[2 * a + k, at] = part
                share_sum = share_sum + part
                share_x_sum = share_x_sum + part * xs[k]
        row = pl.ds(n, 1)
        pooled[row] = jnp.sum(cell_sum, axis=0, keepdims=True) * (0.5 / cells)
        shares[row] = jnp.sum(share_sum, axis=0, keepdims=True)
        shares_x[row] = jnp.sum(share_x_sum, axis=0, keepdims=True)
        return carry

    lax.fori_loop(0, count_img, forward, 0)

    head_pad[...] = jnp.zeros((128, 640), F32)
    head_pad[0:NCLS, 0:513] = head[...]
    head_rows = head_pad[:, 0:512].astype(BF16)
    pooled_low = pooled[...].astype(BF16)
    logits = dot(pooled_low, head_rows, ((1,), (1,))) + head_pad[:, 512:640].T[0:1, :]
    row16 = lax.broadcasted_iota(jnp.int32, (16, 128), 0)
    lane16 = lax.broadcasted_iota(jnp.int32, (16, 128), 1)
    label_of = jnp.zeros((16, 128), jnp.int32)
    micro_of = jnp.full((16, 128), 3, jnp.int32)
    for n in range(count_img):
        label_of = jnp.where(row16 == n, labels[n], label_of)
        micro_of = jnp.where(row16 == n, micro[n], micro_of)
    is_class = lane16 < NCLS
    live = jnp.where(micro_of < 3, 1.0, 0.0)
    onehot = jnp.where(lane16 == label_of, 1.0, 0.0)
    top = jnp.max(jnp.where(is_class, logits, -3e38), axis=1, keepdims=True)
    shifted = jnp.where(is_class, logits - top, 0.0)
    log_sum = jnp.log(jnp.sum(jnp.where(is_class, jnp.exp(shifted), 0.0), axis=1, keepdims=True))
    logp = jnp.where(is_class, shifted - log_sum, 0.0)
    per_img = -(
        0.9 * jnp.sum(onehot * logp, axis=1, keepdims=True) + 0.1 / NCLS * jnp.sum(logp, axis=1, keepdims=True)
    )
    loss = jnp.sum(live[:, 0:1] * per_img, axis=0, keepdims=True)
    dlogits = jnp.where(is_class, jnp.exp(logp) - 0.9 * onehot - 0.1 / NCLS, 0.0) * (live / live_total)
    dpool[...] = dot_exact(dlogits, head_rows.astype(F32)) * (1.0 / cells)
    head_grad = dot_exact(dlogits, pooled_low.astype(F32), ((0,), (0,)))
    row16w = lax.broadcasted_iota(jnp.int32, (16, 512), 0)
    bias_grad = jnp.concatenate(
        [jnp.sum(dlogits, axis=0, keepdims=True), jnp.zeros((1, 384), F32)], axis=1
    )
    block = jnp.where(row16w < NCLS, head_grad[0:16], 0.0)
    block = jnp.where(row16w == NCLS, bias_grad, block)
    small[...] = jnp.where(row16w == NCLS + 1, loss, block)

    back_rows = []
    for which in (shares, shares_x):
        for m in range(3):
            inside = jnp.where(micro_of[:, 0:1] == m, 1.0, 0.0)
            back_rows.append(jnp.sum(inside * (dpool[...] * which[...]), axis=0, keepdims=True))
    tile_in[1] = stack_rows(back_rows)
    tile_start(1)

    lax.fori_loop(2, 4, turn, 0)
    def squares(h):
        return work[h // 2, :, :, :, :, :, :, (h % 2) * 128 : (h % 2) * 128 + 128].reshape(512, 128)

    for h in range(8):
        value = squares(h)
        if h > 0:
            value = value + squares(h - 1)
        if h < 7:
            value = value + squares(h + 1)
        box_hi[:, h * 128 : h * 128 + 128], box_lo[:, h * 128 : h * 128 + 128] = split(value)

    value = jnp.concatenate([work[6].reshape(512, 256), work[7].reshape(512, 256)], axis=1)
    out_hi[...], out_lo[...] = split(value)
    out_t_hi[...], out_t_lo[...] = split(value.T)
    totals = tile_end(1)
    norm_grads = [
        totals[3:4] + totals[4:5] + totals[5:6],
        totals[0:1] + totals[1:2] + totals[2:3],
    ]
    rows_stat[2] = stack_rows([gain * totals[m : m + 1] / pixels[m] for m in range(3)])
    rows_stat[3] = stack_rows([gain * totals[3 + m : 4 + m] / pixels[m] for m in range(3)])

    def backward(pair, carry):
        parts = []
        for k in range(2):
            n = 2 * pair + k
            mean, dead = image_rows(n, 0)
            rstd, _ = image_rows(n, 1)
            rstd = rstd + dead
            offset, _ = image_rows(n, 2)
            slope, _ = image_rows(n, 3)
            parts.append((mean, rstd, offset, slope, gain * dpool[pl.ds(n, 1)], pl.ds(pl.multiple_of(n * 8, 8), 8)))
        for h in range(8):
            values = []
            for mean, rstd, offset, slope, factor, at in parts:
                xhat = (conv[h, at] - mean) * rstd
                values.append(rstd * (factor * share[h, at] - offset - xhat * slope))
            rows = pl.ds(pl.multiple_of(h * 128 + 16 * pair, 16), 16)
            grad_low[rows] = jnp.concatenate(values, axis=0).astype(BF16)
        return carry

    lax.fori_loop(0, count_img // 2, backward, 0)

    def rotate(k, carry):
        rows = pl.ds(pl.multiple_of(k * 256, 256), 256)
        value = dot(grad_low[rows], out_hi[...]) + dot(grad_low[rows], out_lo[...])
        rot_hi[rows] = value.astype(BF16)
        rot2_hi[rows], rot2_lo[rows] = split(value * value)
        return carry

    lax.fori_loop(0, 4, rotate, 0)

    got = (got0, got1, got2, got3, got4)
    left_home = set()

    def region(unit, fixed, first=1):
        return (unit,) + tuple(fixed.get(k, slice(None)) for k in range(first, 5))

    def rs_copy(unit, stage):
        if stage < 5:
            order = (0,) + RS_ORDER[unit]
            fixed = {k: mine[k] for k in order[:stage]}
            fixed[order[stage]] = 1 - mine[order[stage]]
            target, to = got[stage].at[RS_SLOT[unit][stage]], partner(order[stage])
            sems = (send_sem.at[RS_SEND[unit][stage]], recv_sem.at[sum(GOT_COUNT[:stage]) + RS_SLOT[unit][stage]])
        else:
            fixed = dict(enumerate(mine[:5]))
            target, to = got_more.at[unit, stage - 5], partner(stage)
            sems = (more_sem.at[0, unit, stage - 5], more_sem.at[1, unit, stage - 5])
        source = half_sum.at[region(unit, fixed)] if stage else away.at[UNITS.index(unit) % AWAY]
        return pltpu.make_async_remote_copy(
            src_ref=source,
            dst_ref=target,
            send_sem=sems[0],
            recv_sem=sems[1],
            device_id=to,
            device_id_type=MESH,
        )

    def ag_copy(unit, stage):
        order = (0,) + AG_ORDER[unit]
        where = work.at[region(unit, {k: mine[k] for k in order[: 5 - stage]}, 0)]
        return pltpu.make_async_remote_copy(
            src_ref=where,
            dst_ref=where,
            send_sem=send_sem.at[AG_SEND[unit][stage]],
            recv_sem=recv_sem.at[AG_RECV[unit][stage]],
            device_id=partner(order[4 - stage]),
            device_id_type=MESH,
        )

    def sm_copy(stage):
        return pltpu.make_async_remote_copy(
            src_ref=small,
            dst_ref=small_got.at[stage],
            send_sem=sm_send.at[stage],
            recv_sem=sm_recv.at[stage],
            device_id=partner(stage),
            device_id_type=MESH,
        )

    def do_mm(unit, stage):
        tap, cols = unit // 2, slice((unit % 2) * 256, (unit % 2) * 256 + 256)
        dy, dx = tap // 3, tap % 3
        place = UNITS.index(unit)
        if place >= AWAY and UNITS[place - AWAY] not in left_home:
            left_home.add(UNITS[place - AWAY])
            rs_copy(UNITS[place - AWAY], 0).wait_send()
        for stays, half in enumerate((1 - core, core)):
            rows = pl.ds(pl.multiple_of(half * 256, 256), 256)
            if tap == STAT:
                value = (
                    dot(box_hi[rows], rot2_hi[:, cols])
                    + dot(box_hi[rows], rot2_lo[:, cols])
                    + dot(box_lo[rows], rot2_hi[:, cols])
                )
            else:
                value = dot(turned_hi[dx, rows, dy * 128 : dy * 128 + 1024], rot_hi[:, cols])
            value = value.reshape(2, 2, 2, 2, 16, 256)
            if stays:
                half_sum[unit] = value
            else:
                away[place % AWAY] = value
                rs_copy(unit, 0).start()

    def do_rs(unit, stage):
        if stage == 0 and unit in left_home:
            rs_copy(unit, stage).wait_recv()
        else:
            rs_copy(unit, stage).wait()
            if stage == 0:
                left_home.add(unit)
        if stage < 5:
            fixed = {k: mine[k] for k in ((0,) + RS_ORDER[unit])[: stage + 1]}
            source, at = got[stage], (RS_SLOT[unit][stage],)
        else:
            fixed = dict(enumerate(mine[:5]))
            source, at = got_more, (unit, stage - 5)
        left = [k for k in range(1, 5) if k not in fixed]

        def add(i, carry):
            inner = dict(fixed)
            where = at
            if len(left) >= 3:
                inner[left[0]], inner[left[1]] = i // 2, i % 2
                where = at + (i // 2, i % 2)
            half_sum[region(unit, inner)] += source[where]
            return carry

        if len(left) >= 3:
            lax.fori_loop(0, 4, add, 0)
        else:
            add(0, 0)
        if stage < 4 + extra:
            rs_copy(unit, stage + 1).start()
        if stage >= 4 and stage < 4 + extra:
            do_rs(unit, stage + 1)

    def do_post(tap, stage):
        pair = (2 * tap, 2 * tap + 1)
        value = jnp.concatenate([half_sum[region(unit, own)] for unit in pair], axis=1)
        if tap == STAT:
            value = 0.95 * eig[...] + 0.05 * (value * (live_total * float(area * area)))
            scale_rows[...] = value + DAMPING
        else:
            high, low = split(value / scale_rows[...])
            value = dot(high, out_t_hi[...]) + dot(high, out_t_lo[...]) + dot(low, out_t_hi[...])
        for k, unit in enumerate(pair):
            work[region(unit, own, 0)] = value[:, 256 * k : 256 * k + 256]
            ag_copy(unit, 0).start()

    def do_ag(unit, stage):
        ag_copy(unit, stage).wait()
        if stage < 4:
            ag_copy(unit, stage + 1).start()


    def do_fin(unit, stage):
        tap, cols = unit // 2, slice((unit % 2) * 256, (unit % 2) * 256 + 256)
        if tap == STAT:
            scales[:, cols] = work[unit].reshape(512, 256)
            return

        def cut(i, carry):
            rows = pl.ds(pl.multiple_of(i * 64, 64), 64)
            value = work[unit, i // 4, (i // 2) % 2, i % 2].reshape(64, 256)
            gathered_hi[rows], gathered_lo[rows] = split(value)
            return carry

        lax.fori_loop(0, 8, cut, 0)

        def tile(i, carry):
            rows = pl.ds(pl.multiple_of(i * 256, 256), 256)
            value = (
                dot(in_hi[rows], gathered_hi[...])
                + dot(in_hi[rows], gathered_lo[...])
                + dot(in_lo[rows], gathered_hi[...])
            )
            precond[pl.ds(pl.multiple_of(tap * 512 + i * 256, 256), 256), cols] = value
            square_sum[...] += jnp.sum((value * value).reshape(32, 8, 256), axis=0)
            return carry

        lax.fori_loop(0, 2, tile, 0)

    def do_sm(stage, unused):
        sm_copy(stage).wait()
        small[...] += small_got[stage]
        if stage < 4 + extra:
            sm_copy(stage + 1).start()
        if stage >= 4 and stage < 4 + extra:
            do_sm(stage + 1, 0)

    square_sum[...] = jnp.zeros((8, 256), F32)
    sm_copy(0).start()
    run = (do_mm, do_rs, do_post, do_ag, do_fin, do_sm)
    for kind, which, stage in TASKS:
        run[kind](which, stage)

    block = small[...]
    head_part = jnp.where(row16w <= NCLS, block, 0.0)
    squared = (
        jnp.sum(jnp.sum(square_sum[...], axis=0, keepdims=True), axis=1, keepdims=True)
        + jnp.sum(norm_grads[0] * norm_grads[0] + norm_grads[1] * norm_grads[1], axis=1, keepdims=True)
        + jnp.sum(jnp.sum(head_part * head_part, axis=0, keepdims=True), axis=1, keepdims=True)
    )
    norm = jnp.sqrt(squared)
    factor = jnp.minimum(1.0, CLIP / (norm + 1e-06))
    facts[0:16] = block
    facts[16:24] = stack_rows(norm_grads + [block[NCLS + 1 : NCLS + 2], live_total, norm, factor])


def adamw(weight, grad, first, second, rate):
    first = 0.9 * first + 0.1 * grad
    second = 0.999 * second + 0.001 * grad * grad
    step_size = first / (1.0 - 0.9**STEP) / (jnp.sqrt(second / (1.0 - 0.999**STEP)) + 1e-08)
    return (weight - rate * (step_size + 0.01 * weight), first, second)


def adamw_positive(weight, grad, first, second, rate):
    first = 0.9 * first + 0.1 * grad
    second = 0.999 * second + 0.001 * grad * grad
    scaled = second * (1.0 / (1.0 - 0.999**STEP))
    root = scaled * lax.rsqrt(scaled) + 1e-08
    step = first * (rate / (1.0 - 0.9**STEP)) / root
    return (weight * (1.0 - 0.01 * rate) - step, first, second)


CHUNKS = 18
LOADS = 9
RING = 4


def update_kernel(
    facts,
    gain,
    shift,
    norm_first,
    norm_second,
    head,
    head_first,
    head_second,
    in_precond,
    scales,
    weight,
    first,
    second,
    loss_parts,
    grad_norm,
    norm_new,
    norm_m,
    norm_v,
    head_new,
    head_m,
    head_v,
    conv_new,
    conv_m,
    conv_v,
    scales_new,
    in_weight,
    in_first,
    in_second,
    out_new,
    out_m,
    out_v,
    in_sem,
    out_sem,
    scale_sem,
):
    tall = TAPS * 512 // CHUNKS
    pairs = ((weight, in_weight), (first, in_first), (second, in_second))
    outs = ((out_new, conv_new), (out_m, conv_m), (out_v, conv_v))

    def load(k, i):
        deep = TAPS * 512 // LOADS
        rows = pl.ds(pl.multiple_of(i * deep, deep), deep)
        return pltpu.make_async_copy(pairs[k][0].at[rows], pairs[k][1].at[rows], in_sem.at[k, i])

    def store(k, i):
        rows = pl.ds(pl.multiple_of(i * tall, tall), tall)
        return pltpu.make_async_copy(outs[k][0].at[i % RING], outs[k][1].at[rows], out_sem.at[k, i % RING])

    def start(i, carry):
        for k in range(3):
            load(k, i).start()
        return carry

    lax.fori_loop(0, LOADS, start, 0)
    scale_out = pltpu.make_async_copy(scales, scales_new, scale_sem)
    scale_out.start()

    factor = facts[21:22, 0:1]
    loss_parts[0] = facts[18, 0]
    loss_parts[1] = facts[19, 0]
    grad_norm[0] = facts[20, 0]
    grads = factor * facts[16:18, :]
    weights = jnp.concatenate([gain[...], shift[...]], axis=0)
    norm_new[...], norm_m[...], norm_v[...] = adamw(weights, grads, norm_first[...], norm_second[...], 0.1)
    block = factor * facts[0:16, :]
    head_new[:, 0:512], head_m[:, 0:512], head_v[:, 0:512] = adamw(
        head[:, 0:512], block[0:NCLS], head_first[:, 0:512], head_second[:, 0:512], 0.05
    )
    bias = jnp.concatenate([block[0:16, 0:128], jnp.zeros((112, 128), F32)], axis=0).T[0:NCLS, NCLS : NCLS + 1]
    head_new[:, 512:513], head_m[:, 512:513], head_v[:, 512:513] = adamw(
        head[:, 512:513], bias, head_first[:, 512:513], head_second[:, 512:513], 0.05
    )

    def chunk(i, carry):
        @pl.when(i % (CHUNKS // LOADS) == 0)
        def _():
            for k in range(3):
                load(k, i // (CHUNKS // LOADS)).wait()

        @pl.when(i >= RING)
        def _():
            for k in range(3):
                store(k, i).wait()

        def piece(j, inner):
            rows = pl.ds(pl.multiple_of(i * tall + j * 32, 32), 32)
            at = pl.ds(pl.multiple_of(j * 32, 32), 32)
            out_new[i % RING, at], out_m[i % RING, at], out_v[i % RING, at] = adamw_positive(
                in_weight[rows],
                factor * in_precond[rows],
                in_first[rows].astype(F32),
                in_second[rows].astype(F32),
                0.02,
            )
            return inner

        lax.fori_loop(0, tall // 32, piece, 0)
        for k in range(3):
            store(k, i).start()
        return carry

    lax.fori_loop(0, CHUNKS, chunk, 0)
    for i in range(CHUNKS - RING, CHUNKS):
        for k in range(3):
            store(k, i).wait()
    scale_out.wait()


def shards(
    sizes,
    images,
    micro_ids,
    labels,
    conv_weight,
    conv_first,
    conv_second,
    eig_scales,
    basis_in,
    basis_out,
    batchnorm_gain,
    batchnorm_shift,
    norm_first,
    norm_second,
    head,
    head_first,
    head_second,
):
    dp_count, rep_count = sizes
    count_img = images.shape[0]
    chips = dp_count * rep_count // 2
    bit_count = (dp_count * rep_count - 1).bit_length()
    extra = bit_count - 5
    vmem = pl.BlockSpec(memory_space=pltpu.VMEM)
    smem = pl.BlockSpec(memory_space=pltpu.SMEM)
    hbm = pl.BlockSpec(memory_space=pltpu.HBM)
    gain = batchnorm_gain.reshape(1, 512)
    shift = batchnorm_shift.reshape(1, 512)
    pixels = 8 * count_img
    square = (512, 512)
    dma = pltpu.SemaphoreType.DMA
    scratch = [
        pltpu.SMEM((count_img,), jnp.int32),
        pltpu.SMEM((count_img,), jnp.int32),
        pltpu.VMEM(images.shape, BF16),
        pltpu.VMEM((1, 512), F32),
        pltpu.VMEM((1, 512), F32),
        pltpu.VMEM((NCLS, 513), F32),
        pltpu.VMEM((20, 2, 2, 2, 2, 2, 16, 256), F32),
        pltpu.VMEM((20, 2, 2, 2, 2, 16, 256), F32),
        pltpu.VMEM((AWAY, 2, 2, 2, 2, 16, 256), F32),
        pltpu.VMEM((GOT_COUNT[0], 2, 2, 2, 2, 16, 256), F32),
        pltpu.VMEM((GOT_COUNT[1], 2, 2, 2, 16, 256), F32),
        pltpu.VMEM((GOT_COUNT[2], 2, 2, 16, 256), F32),
        pltpu.VMEM((GOT_COUNT[3], 2, 16, 256), F32),
        pltpu.VMEM((GOT_COUNT[4], 16, 256), F32),
        pltpu.VMEM((20, extra, 16, 256) if extra else (1, 1, 8, 128), F32),
        pltpu.VMEM((16, 512), F32),
        pltpu.VMEM((bit_count, 16, 512), F32),
        pltpu.VMEM((2, 8, 512), F32),
        pltpu.VMEM((2, 8, 256), F32),
        pltpu.VMEM((2, chips, 8, 256), F32),
        pltpu.VMEM((2, 2, 8, 256), F32),
        pltpu.VMEM((3, 10 * pixels, 512), BF16),
        pltpu.VMEM((3, 1024, 512), BF16),
        pltpu.VMEM((8, pixels, 512), F32),
        pltpu.VMEM((8, pixels, 512), F32),
        pltpu.VMEM((2, 3, 512, 512), BF16),
        pltpu.VMEM((3, 512, 1280), BF16),
        pltpu.VMEM((512, 1024), BF16),
        pltpu.VMEM((512, 1024), BF16),
        pltpu.VMEM((1024, 512), BF16),
    ]
    scratch += [pltpu.VMEM((1024, 512), BF16)] * 3
    scratch += [pltpu.VMEM((16, 512), F32)]
    scratch += [pltpu.VMEM(square, BF16)] * 8 + [pltpu.VMEM((512, 256), BF16)] * 2
    scratch += [
        pltpu.VMEM((4, 8, 512), F32),
        pltpu.VMEM((16, 512), F32),
        pltpu.VMEM((16, 512), F32),
        pltpu.VMEM((16, 512), F32),
        pltpu.VMEM((16, 512), F32),
        pltpu.VMEM((128, 640), F32),
        pltpu.VMEM((16, 512), F32),
        pltpu.VMEM((8, 256), F32),
        dma((2 * TAPS,)),
        dma((11,)),
        dma((SEND_COUNT,)),
        dma((RECV_COUNT,)),
        dma((2, 20, extra) if extra else (1, 1, 1)),
        dma((bit_count,)),
        dma((bit_count,)),
        dma((4,)),
        dma((4,)),
        dma((2,)),
        dma((2,)),
    ]
    precond, scales, facts = pl.pallas_call(
        functools.partial(main_kernel, (dp_count, rep_count, count_img)),
        out_shape=(
            pltpu.VMEM((TAPS * 512, 512), F32),
            pltpu.VMEM(square, F32),
            pltpu.VMEM((24, 512), F32),
        ),
        in_specs=[hbm] * 10,
        out_specs=(vmem, vmem, vmem),
        scratch_shapes=scratch,
        compiler_params=pltpu.CompilerParams(
            collective_id=0, has_side_effects=True, vmem_limit_bytes=53 * 2**20
        ),
        name="reduce_and_precondition",
    )(
        micro_ids,
        labels,
        images,
        gain,
        shift,
        head.T,
        conv_weight.reshape(TAPS, 2, 2, 2, 2, 2, 16, 512),
        eig_scales,
        basis_in.reshape(2, 2, 2, 2, 2, 16, 512),
        basis_out.reshape(2, 2, 2, 2, 2, 16, 512),
    )
    tall = TAPS * 512 // CHUNKS
    head_shape = (NCLS, 513)
    outs = pl.pallas_call(
        update_kernel,
        out_shape=(
            jax.ShapeDtypeStruct((2,), F32),
            jax.ShapeDtypeStruct((1,), F32),
            *[jax.ShapeDtypeStruct((2, 512), F32)] * 3,
            *[jax.ShapeDtypeStruct(head_shape, F32)] * 3,
            *[jax.ShapeDtypeStruct((TAPS * 512, 512), F32)] * 3,
            jax.ShapeDtypeStruct(square, F32),
        ),
        in_specs=[vmem] * 10 + [hbm] * 3,
        out_specs=(smem, smem) + (vmem,) * 6 + (hbm,) * 4,
        scratch_shapes=[
            pltpu.VMEM((TAPS * 512, 512), F32),
            pltpu.VMEM((TAPS * 512, 512), BF16),
            pltpu.VMEM((TAPS * 512, 512), BF16),
            *[pltpu.VMEM((RING, tall, 512), F32)] * 3,
            dma((3, LOADS)),
            dma((3, RING)),
            dma,
        ],
        compiler_params=pltpu.CompilerParams(vmem_limit_bytes=30 * 2**20),
        name="adamw",
    )(
        facts,
        gain,
        shift,
        norm_first,
        norm_second,
        head.T,
        head_first.T,
        head_second.T,
        precond,
        scales,
        *(pltpu.with_memory_space_constraint(x, pltpu.HBM) for x in (conv_weight, conv_first, conv_second)),
    )
    loss_parts, grad_norm, norm_new, norm_m, norm_v, head_new, head_m, head_v, conv_new, conv_m, conv_v, scales_new = outs
    return (
        loss_parts,
        grad_norm.reshape(()),
        conv_new,
        conv_m,
        conv_v,
        scales_new,
        norm_new,
        norm_m,
        norm_v,
        head_new.T,
        head_m.T,
        head_v.T,
    )


def solution(mesh):
    split_images = P(("dp", "rep"))
    in_specs = (P(("dp", "rep"), None, None, None), split_images, split_images) + (P(),) * 13
    sizes = (mesh.shape["dp"], mesh.shape["rep"])
    return jax.shard_map(
        functools.partial(shards, sizes), mesh=mesh, in_specs=in_specs, out_specs=(P(),) * 12, check_vma=False
    )
```

```python
import functools

import jax
import jax.numpy as jnp
from jax import lax
from jax.experimental import pallas as pl
from jax.experimental.pallas import tpu as pltpu
from jax.sharding import PartitionSpec as P

NCLS = 10
STEP = 5
NORM_EPS = 1e-05
DAMPING = 0.001
CLIP = 0.01
MESH = pl.DeviceIdType.MESH
F32 = jnp.float32
BF16 = jnp.bfloat16
HIGHEST = lax.Precision.HIGHEST
TAPS = 9
STAT = 9
WEIGHT = 20
AWAY = 4
UNITS = (13, 4, 14, 5, 7, 18, 3, 19, 15, 12, 0, 17, 9, 10, 16, 11, 6, 2, 1, 8)
RS_ORDER = (
    (3, 1, 2, 4), (1, 2, 3, 4), (1, 2, 3, 4), (2, 1, 3, 4), (3, 1, 4, 2),
    (1, 3, 4, 2), (1, 2, 3, 4), (3, 1, 2, 4), (1, 2, 3, 4), (2, 1, 3, 4),
    (2, 3, 4, 1), (2, 3, 1, 4), (1, 2, 3, 4), (2, 3, 1, 4), (1, 2, 3, 4),
    (3, 1, 4, 2), (1, 2, 3, 4), (2, 3, 4, 1), (2, 1, 3, 4), (1, 2, 3, 4),
)
AG_ORDER = (
    (1, 3, 4, 2), (3, 4, 2, 1), (2, 3, 1, 4), (1, 3, 4, 2), (1, 2, 3, 4),
    (1, 2, 3, 4), (3, 1, 2, 4), (1, 2, 3, 4), (2, 3, 4, 1), (3, 4, 1, 2),
    (2, 1, 3, 4), (2, 1, 3, 4), (1, 2, 3, 4), (2, 1, 3, 4), (2, 3, 1, 4),
    (3, 2, 1, 4), (1, 2, 3, 4), (2, 3, 4, 1), (1, 2, 3, 4), (2, 1, 3, 4),
)
TASKS = (
    (0, 13, 0), (0, 4, 0), (0, 14, 0), (5, 0, 0), (1, 13, 0), (0, 5, 0), (1, 4, 0), (1, 14, 0),
    (0, 7, 0), (0, 18, 0), (1, 5, 0), (1, 7, 0), (5, 1, 0), (0, 3, 0), (1, 18, 0), (0, 19, 0),
    (1, 3, 0), (1, 13, 1), (0, 15, 0), (1, 19, 0), (1, 14, 1), (1, 4, 1), (5, 2, 0), (0, 12, 0),
    (0, 0, 0), (1, 15, 0), (0, 17, 0), (1, 12, 0), (1, 7, 1), (1, 5, 1), (1, 0, 0), (1, 18, 1),
    (1, 17, 0), (0, 9, 0), (1, 13, 2), (0, 10, 0), (5, 3, 0), (0, 16, 0), (1, 9, 0), (1, 19, 1),
    (1, 3, 1), (1, 10, 0), (0, 11, 0), (1, 16, 0), (1, 4, 2), (1, 14, 2), (0, 6, 0), (1, 15, 1),
    (0, 2, 0), (1, 11, 0), (0, 1, 0), (1, 5, 2), (1, 6, 0), (0, 8, 0), (1, 2, 0), (1, 12, 1),
    (1, 1, 0), (1, 17, 1), (1, 8, 0), (1, 7, 2), (1, 0, 1), (1, 18, 2), (1, 9, 1), (5, 4, 0),
    (1, 13, 3), (1, 14, 3), (1, 4, 3), (1, 19, 2), (1, 3, 2), (1, 5, 3), (1, 17, 2), (1, 18, 3),
    (1, 10, 1), (1, 16, 1), (1, 13, 4), (1, 19, 3), (1, 14, 4), (1, 3, 3), (1, 15, 2), (1, 11, 1),
    (1, 17, 3), (1, 18, 4), (1, 10, 2), (1, 12, 2), (1, 6, 1), (1, 7, 3), (1, 4, 4), (1, 19, 4),
    (2, 9, 0), (1, 5, 4), (1, 3, 4), (2, 2, 0), (1, 15, 3), (1, 11, 2), (1, 16, 2), (1, 2, 1),
    (1, 12, 3), (1, 6, 2), (1, 10, 3), (1, 15, 4), (2, 7, 0), (1, 7, 4), (3, 18, 0), (1, 1, 1),
    (3, 19, 0), (1, 16, 3), (1, 2, 2), (3, 4, 0), (1, 6, 3), (3, 5, 0), (1, 12, 4), (2, 6, 0),
    (1, 8, 1), (3, 18, 1), (3, 14, 0), (3, 19, 1), (1, 1, 2), (3, 15, 0), (1, 0, 2), (1, 2, 3),
    (1, 16, 4), (3, 4, 1), (1, 9, 2), (1, 17, 4), (2, 8, 0), (3, 5, 1), (1, 8, 2), (1, 6, 4),
    (1, 11, 3), (2, 3, 0), (1, 10, 4), (3, 12, 0), (3, 14, 1), (1, 1, 3), (3, 18, 2), (3, 13, 0),
    (1, 0, 3), (1, 9, 3), (1, 2, 4), (2, 1, 0), (3, 19, 2), (3, 15, 1), (1, 8, 3), (3, 4, 2),
    (3, 16, 0), (3, 17, 0), (1, 11, 4), (2, 5, 0), (3, 5, 2), (3, 6, 0), (3, 12, 1), (3, 3, 0),
    (3, 7, 0), (3, 18, 3), (3, 14, 2), (3, 13, 1), (1, 1, 4), (3, 18, 4), (3, 19, 3), (4, 18, 0),
    (1, 0, 4), (2, 0, 0), (1, 9, 4), (3, 4, 3), (3, 15, 2), (3, 2, 0), (3, 19, 4), (3, 16, 1),
    (1, 8, 4), (2, 4, 0), (3, 6, 1), (4, 19, 0), (3, 4, 4), (4, 4, 0), (3, 12, 2), (3, 11, 0),
    (3, 10, 0), (3, 5, 3), (3, 17, 1), (3, 7, 1), (3, 3, 1), (3, 13, 2), (3, 5, 4), (4, 5, 0),
    (3, 0, 0), (3, 1, 0), (3, 14, 3), (3, 2, 1), (3, 8, 0), (3, 15, 3), (3, 11, 1), (3, 16, 2),
    (3, 6, 2), (3, 14, 4), (3, 9, 0), (4, 14, 0), (3, 10, 1), (3, 15, 4), (4, 15, 0), (3, 17, 2),
    (3, 7, 2), (3, 12, 3), (3, 3, 2), (3, 11, 2), (3, 12, 4), (3, 13, 3), (4, 12, 0), (3, 0, 1),
    (3, 1, 1), (3, 2, 2), (3, 13, 4), (4, 13, 0), (3, 8, 1), (3, 16, 3), (3, 9, 1), (3, 17, 3),
    (3, 16, 4), (4, 16, 0), (3, 10, 2), (3, 17, 4), (3, 6, 3), (4, 17, 0), (3, 0, 2), (3, 11, 3),
    (3, 6, 4), (4, 6, 0), (3, 7, 3), (3, 1, 2), (3, 11, 4), (4, 11, 0), (3, 2, 3), (3, 8, 2),
    (3, 7, 4), (4, 7, 0), (3, 3, 3), (3, 2, 4), (3, 9, 2), (4, 2, 0), (3, 10, 3), (3, 3, 4),
    (4, 3, 0), (3, 1, 3), (3, 0, 3), (3, 10, 4), (4, 10, 0), (3, 1, 4), (3, 8, 3), (4, 1, 0),
    (3, 0, 4), (3, 9, 3), (4, 0, 0), (3, 8, 4), (4, 8, 0), (3, 9, 4), (4, 9, 0),
)
GOT_COUNT = (6, 17, 14, 10, 11)
RECV_COUNT, SEND_COUNT = 59, 20
RS_SLOT = (
    (4, 11, 12, 2, 5), (1, 15, 0, 1, 0), (4, 14, 3, 0, 3), (0, 7, 7, 6, 6), (1, 2, 1, 2, 3),
    (3, 4, 3, 3, 5), (3, 2, 2, 4, 2), (4, 3, 4, 8, 8), (2, 16, 1, 4, 7), (1, 12, 13, 3, 6),
    (2, 13, 0, 2, 10), (0, 1, 1, 9, 4), (3, 9, 10, 1, 0), (0, 0, 0, 0, 0), (2, 1, 2, 1, 1),
    (2, 8, 9, 0, 7), (5, 0, 11, 3, 1), (0, 10, 8, 7, 9), (5, 5, 5, 4, 2), (1, 6, 6, 5, 4),
)
AG_RECV = (
    (12, 17, 10, 24, 6), (29, 6, 11, 4, 1), (22, 14, 18, 12, 2), (4, 28, 4, 23, 0), (2, 8, 0, 20, 1),
    (3, 9, 17, 26, 2), (2, 9, 33, 20, 0), (18, 10, 3, 22, 1), (15, 38, 13, 5, 0), (34, 8, 14, 16, 2),
    (25, 35, 9, 15, 3), (24, 31, 5, 21, 3), (10, 3, 23, 37, 2), (13, 6, 11, 16, 0), (5, 11, 19, 13, 0),
    (7, 15, 21, 30, 1), (1, 8, 32, 7, 1), (16, 27, 36, 19, 2), (0, 4, 12, 5, 58), (1, 6, 14, 7, 0),
)
RS_SEND = (
    (10, 10, 10, 10, 10), (18, 18, 4, 4, 4), (17, 17, 14, 14, 14), (6, 6, 6, 6, 2), (1, 1, 1, 1, 1),
    (3, 3, 3, 3, 3), (16, 16, 11, 11, 11), (4, 4, 4, 4, 4), (19, 19, 17, 17, 17), (12, 12, 12, 12, 12),
    (13, 13, 13, 5, 5), (15, 15, 7, 7, 7), (9, 9, 9, 9, 9), (0, 0, 0, 0, 0), (2, 2, 2, 2, 2),
    (8, 8, 8, 6, 6), (14, 14, 14, 13, 13), (11, 11, 11, 11, 8), (5, 5, 5, 5, 5), (7, 7, 7, 7, 0),
)
AG_SEND = (
    (1, 1, 1, 1, 1), (4, 3, 3, 3, 3), (14, 12, 6, 6, 5), (16, 16, 16, 13, 6), (2, 2, 2, 2, 2),
    (3, 3, 3, 3, 3), (11, 11, 11, 11, 7), (18, 18, 15, 12, 7), (8, 8, 2, 2, 0), (14, 4, 4, 4, 1),
    (7, 7, 7, 0, 0), (19, 5, 5, 5, 5), (9, 5, 5, 2, 2), (16, 9, 9, 9, 2), (6, 6, 6, 6, 4),
    (15, 15, 15, 10, 10), (8, 8, 0, 0, 0), (13, 13, 13, 10, 8), (0, 0, 0, 0, 0), (1, 1, 1, 1, 0),
)


def split(value):
    high = value.astype(BF16)
    return high, (value - high.astype(F32)).astype(BF16)


def dot(a, b, dims=((1,), (0,))):
    return lax.dot_general(a, b, (dims, ((), ())), preferred_element_type=F32)


def dot_exact(a, b, dims=((1,), (0,))):
    return lax.dot_general(a, b, (dims, ((), ())), precision=HIGHEST, preferred_element_type=F32)


def main_kernel(
    sizes,
    micro_hbm,
    labels_hbm,
    images_hbm,
    gain_hbm,
    shift_hbm,
    head_hbm,
    weight,
    eig_hbm,
    in_hbm,
    out_hbm,
    work,
    facts,
    micro,
    labels,
    gain_ref,
    shift_ref,
    head,
    got0,
    got1,
    got2,
    got3,
    got4,
    got_more,
    small,
    small_got,
    tile_in,
    tile_core,
    tile_slots,
    tile_out,
    turned_hi,
    box_hi,
    box_lo,
    rot_hi,
    rot2_hi,
    rot2_lo,
    eig,
    in_hi,
    in_lo,
    out_t_hi,
    out_t_lo,
    rows_stat,
    pooled,
    shares,
    shares_x,
    dpool,
    head_pad,
    scale_rows,
    square_sum,
    w_sem,
    load_sem,
    send_sem,
    recv_sem,
    more_sem,
    sm_send,
    sm_recv,
    core_send,
    core_recv,
    chip_send,
    chip_recv,
):
    dp_count, rep_count, count_img = sizes
    area = 64
    cells = 16
    chips = dp_count * rep_count // 2
    dp = lax.axis_index("dp")
    rep = lax.axis_index("rep")
    core = rep % 2
    chip = dp * (rep_count // 2) + rep // 2
    bits = [("rep", 1), ("dp", 1), ("rep", 2), ("dp", 2), ("dp", 4)]
    step = 8
    while step < dp_count:
        bits.append(("dp", step))
        step *= 2
    step = 4
    while step < rep_count:
        bits.append(("rep", step))
        step *= 2
    extra = len(bits) - 5
    stride = count_img * 8
    mine = [((dp if name == "dp" else rep) // weight_of) % 2 for name, weight_of in bits]

    own = dict(enumerate(mine[:5]))
    own_block = (((mine[0] * 2 + mine[1]) * 2 + mine[2]) * 2 + mine[3]) * 2 + mine[4]

    def partner(k):
        name, weight_of = bits[k]
        change = (1 - 2 * mine[k]) * weight_of
        return (dp + change, rep) if name == "dp" else (dp, rep + change)

    def chip_device(q):
        return (q // (rep_count // 2), (q % (rep_count // 2)) * 2 + core)

    def weight_copy(unit):
        cols = pl.ds(pl.multiple_of((unit % 2) * 256, 256), 256)
        return pltpu.make_async_copy(
            weight.at[unit // 2, :, :, :, :, :, :, cols], work.at[WEIGHT + unit], w_sem.at[unit]
        )

    def start_weight(unit, carry):
        weight_copy(unit).start()
        return carry

    loads = [
        pltpu.make_async_copy(src, dst, load_sem.at[k])
        for k, (src, dst) in enumerate(
            (
                (in_hbm.at[:, :, :, :, :, :, 0:256], work.at[4]),
                (in_hbm.at[:, :, :, :, :, :, 256:512], work.at[5]),
                (out_hbm.at[:, :, :, :, :, :, 0:256], work.at[6]),
                (out_hbm.at[:, :, :, :, :, :, 256:512], work.at[7]),
                (eig_hbm.at[pl.ds(pl.multiple_of(own_block * 16, 16), 16)], eig),
            )
        )
    ]

    barrier = pltpu.get_barrier_semaphore()

    def greet(k, carry):
        pl.semaphore_signal(barrier, inc=1, device_id=chip_device((chip + k) % chips), device_id_type=MESH)
        return carry

    lax.fori_loop(1, chips, greet, 0)
    pl.semaphore_signal(barrier, inc=1, device_id=partner(0), device_id_type=MESH)

    row8 = lax.broadcasted_iota(jnp.int32, (8, 512), 0)
    row16w = lax.broadcasted_iota(jnp.int32, (16, 512), 0)
    zero_tile = jnp.zeros((8, 512), F32)

    def stack_rows(rows):
        tile = zero_tile
        for k, row in enumerate(rows):
            tile = jnp.where(row8 == k, jnp.broadcast_to(row, (8, 512)), tile)
        return tile

    def prepare(
        narrow, wide, weight_low, conv, share, images, in_t_hi, in_t_lo, out_hi, out_lo, grad_low
    ):
        first_loads = [
            pltpu.make_async_copy(src, dst, load_sem.at[5 + k])
            for k, (src, dst) in enumerate(
                (
                    (images_hbm, images),
                    (micro_hbm, micro),
                    (labels_hbm, labels),
                    (gain_hbm, gain_ref),
                    (shift_hbm, shift_ref),
                    (head_hbm, head),
                )
            )
        ]
        first_loads[0].start()
        first_loads[1].start()
        lax.fori_loop(0, 12, start_weight, 0)
        for copy in first_loads[2:]:
            copy.start()

        column = lax.broadcasted_iota(jnp.int32, (2, 8, 512), 1)
        for k in range(3):
            narrow[k, 0:stride] = jnp.zeros((stride, 512), BF16)
            narrow[k, 9 * stride : 10 * stride] = jnp.zeros((stride, 512), BF16)

        def build(h, carry):
            for pair in range(count_img // 2):
                block = images[2 * pair : 2 * pair + 2, h].astype(F32)
                left = jnp.where(column == 0, 0.0, pltpu.roll(block, 1, 1))
                right = jnp.where(column == 7, 0.0, pltpu.roll(block, 7, 1))
                at = pl.ds(pl.multiple_of((h + 1) * stride + 16 * pair, 16), 16)
                for k, value in enumerate((left, block, right)):
                    narrow[k, at] = value.reshape(16, 512).astype(BF16)
            return carry

        first_loads[0].wait()
        lax.fori_loop(0, 8, build, 0)

        def wait_row(dy):
            for unit in range(6 * dy, 6 * dy + 6):
                weight_copy(unit).wait()

        def cast(dy, k):
            dx, j, half = k // 4, (k // 2) % 2, k % 2
            piece = work[WEIGHT + 2 * (3 * dy + dx) + j, half].reshape(256, 256)
            weight_low[dy % 2, dx, 256 * half : 256 * half + 256, 256 * j : 256 * j + 256] = piece.astype(BF16)

        wait_row(0)
        lax.fori_loop(12, 2 * TAPS, start_weight, 0)
        for k in range(12):
            cast(0, k)
        for dy in range(3):
            if dy < 2:
                wait_row(dy + 1)
            if dy == 1:
                for copy in loads:
                    copy.start()
            for m in range(2):
                for n in range(2):
                    total = None
                    for dx in range(3):
                        begin = (dy + 4 * m) * stride
                        term = dot(
                            narrow[dx, begin : begin + 4 * stride], weight_low[dy % 2, dx, :, n * 256 : n * 256 + 256]
                        )
                        total = term if total is None else total + term
                        if dy < 2:
                            cast(dy + 1, 6 * m + 3 * n + dx)
                    at = (slice(4 * m, 4 * m + 4), slice(None), slice(n * 256, n * 256 + 256))
                    total = total.reshape(4, stride, 256)
                    conv[at] = total if dy == 0 else conv[at] + total

        for copy in first_loads[1:]:
            copy.wait()
        def member(n):
            return [jnp.where(micro[n] == m, 1.0, 0.0).astype(F32) for m in range(3)]

        def gather_sums(n, carry):
            at = pl.ds(pl.multiple_of(n * 8, 8), 8)
            first = jnp.zeros((8, 512), F32)
            second = jnp.zeros((8, 512), F32)
            for h in range(8):
                value = conv[h, at]
                first = first + value
                second = second + value * value
            kinds = member(n)
            return tuple(c + k * first for c, k in zip(carry[:3], kinds)) + tuple(
                c + k * second for c, k in zip(carry[3:6], kinds)
            )

        sums = lax.fori_loop(0, count_img, gather_sums, (zero_tile,) * 6)
        counts = [jnp.zeros((), F32)] * 3
        for n in range(count_img):
            counts = [c + k for c, k in zip(counts, member(n))]
        lane8 = lax.broadcasted_iota(jnp.int32, (8, 512), 1)

        count_row = zero_tile
        for m in range(3):
            count_row = jnp.where(lane8 % 256 == m, counts[m], count_row)
        tile_in[0] = jnp.where(row8 == 6, count_row, stack_rows([jnp.sum(s, axis=0, keepdims=True) for s in sums]))

        def core_half(which):
            return pl.ds(pl.multiple_of(which * 256, 256), 256)

        def tile_copy(i):
            return pltpu.make_async_remote_copy(
                src_ref=tile_in.at[i, :, core_half(1 - core)],
                dst_ref=tile_core.at[i],
                send_sem=core_send.at[2 * i],
                recv_sem=core_recv.at[2 * i],
                device_id=partner(0),
                device_id_type=MESH,
            )

        def tile_start(i):
            tile_copy(i).start()
            tile_copy(i).wait()
            tile_slots[i, 0] = tile_in[i, :, core_half(core)] + tile_core[i]

            def give(k, carry):
                pltpu.make_async_remote_copy(
                    src_ref=tile_slots.at[i, 0],
                    dst_ref=tile_slots.at[i, k],
                    send_sem=chip_send.at[i],
                    recv_sem=chip_recv.at[i],
                    device_id=chip_device((chip + k) % chips),
                    device_id_type=MESH,
                ).start()
                return carry

            lax.fori_loop(1, chips, give, 0)

        def tile_end(i):
            others = tile_slots.at[i, pl.ds(1, chips - 1)]
            pltpu.make_async_remote_copy(
                src_ref=others,
                dst_ref=others,
                send_sem=chip_send.at[i],
                recv_sem=chip_recv.at[i],
                device_id=partner(0),
                device_id_type=MESH,
            ).wait()

            def add(k, total):
                return total + tile_slots[i, (chip - k + chips) % chips]

            tile_out[i, core] = lax.fori_loop(0, chips, add, jnp.zeros((8, 256), F32))
            back = pltpu.make_async_remote_copy(
                src_ref=tile_out.at[i, core],
                dst_ref=tile_out.at[i, core],
                send_sem=core_send.at[2 * i + 1],
                recv_sem=core_recv.at[2 * i + 1],
                device_id=partner(0),
                device_id_type=MESH,
            )
            back.start()
            back.wait()
            return jnp.concatenate([tile_out[i, 0], tile_out[i, 1]], axis=1)

        pl.semaphore_wait(barrier, chips)
        tile_start(0)

        def widen(h, carry):
            source = pl.ds(pl.multiple_of((h + 1) * stride, 16), stride)
            target = pl.ds(pl.multiple_of(h * 128, 128), stride)
            fill = pl.ds(pl.multiple_of(h * 128 + stride, 16), 128 - stride)
            for k in range(3):
                wide[k, target] = narrow[k, source]
                wide[k, fill] = jnp.zeros((128 - stride, 512), BF16)
            grad_low[fill] = jnp.zeros((128 - stride, 512), BF16)
            return carry

        lax.fori_loop(0, 8, widen, 0)
        for copy in loads:
            copy.wait()
        value = jnp.concatenate([work[4].reshape(512, 256), work[5].reshape(512, 256)], axis=1)
        in_hi[...], in_lo[...] = split(value)
        in_t_hi[...], in_t_lo[...] = split(value.T)
        for dx in range(3):
            turned_hi[dx, :, 0:128] = jnp.zeros((512, 128), BF16)
            turned_hi[dx, :, 1152:1280] = jnp.zeros((512, 128), BF16)

        def turn(j, carry):
            total = None
            for dx in range(3):
                rows = wide[dx, pl.ds(pl.multiple_of(256 * j, 256), 256)]
                value = dot(in_t_hi[...], rows, ((1,), (1,))) + dot(in_t_lo[...], rows, ((1,), (1,)))
                at = pl.ds(pl.multiple_of(128 + 256 * j, 128), 256)
                turned_hi[dx, :, at] = value.astype(BF16)
                total = value * value if total is None else total + value * value
            work[j] = total.reshape(2, 2, 2, 2, 2, 16, 256)
            return carry

        lax.fori_loop(0, 2, turn, 0)

        totals = tile_end(0)

        gain = gain_ref[...]
        shift = shift_ref[...]
        live_total = totals[6:7, 0:1] + totals[6:7, 1:2] + totals[6:7, 2:3]
        pixels = [totals[6:7, m : m + 1] * float(area) for m in range(3)]
        mean_rows, rstd_rows = [], []
        for m in range(3):
            mean = totals[m : m + 1] / pixels[m]
            var = totals[3 + m : 4 + m] / pixels[m] - mean * mean
            mean_rows.append(mean)
            rstd_rows.append(lax.rsqrt(var + NORM_EPS))
        rows_stat[0] = stack_rows(mean_rows)
        rows_stat[1] = stack_rows(rstd_rows)

        def image_rows(n, k):
            kinds = member(n)
            row = sum(kinds[m] * rows_stat[k, m : m + 1] for m in range(3))
            return row, 1.0 - (kinds[0] + kinds[1] + kinds[2])

        even = lax.broadcasted_iota(jnp.int32, (8, 512), 0) % 2 == 0
        pooled[...] = jnp.zeros((16, 512), F32)
        shares[...] = jnp.zeros((16, 512), F32)
        shares_x[...] = jnp.zeros((16, 512), F32)

        def forward(n, carry):
            mean, dead = image_rows(n, 0)
            rstd, _ = image_rows(n, 1)
            rstd = rstd + dead
            at = pl.ds(pl.multiple_of(n * 8, 8), 8)
            cell_sum, share_sum, share_x_sum = zero_tile, zero_tile, zero_tile
            for a in range(4):
                xs = [(conv[2 * a + k, at] - mean) * rstd for k in range(2)]
                exps = [jnp.exp(gain * x + shift) for x in xs]
                both = exps[0] + exps[1]
                both = both + jnp.where(even, pltpu.roll(both, 7, 0), pltpu.roll(both, 1, 0))
                both = both + 4.0
                cell_sum = cell_sum + jnp.log(both)
                inverse = 1.0 / both
                for k in range(2):
                    part = exps[k] * inverse
                    share[2 * a + k, at] = part
                    share_sum = share_sum + part
                    share_x_sum = share_x_sum + part * xs[k]
            row = pl.ds(n, 1)
            pooled[row] = jnp.sum(cell_sum, axis=0, keepdims=True) * (0.5 / cells)
            shares[row] = jnp.sum(share_sum, axis=0, keepdims=True)
            shares_x[row] = jnp.sum(share_x_sum, axis=0, keepdims=True)
            return carry

        lax.fori_loop(0, count_img, forward, 0)

        head_pad[...] = jnp.zeros((128, 640), F32)
        head_pad[0:NCLS, 0:513] = head[...]
        head_rows = head_pad[:, 0:512].astype(BF16)
        pooled_low = pooled[...].astype(BF16)
        logits = dot(pooled_low, head_rows, ((1,), (1,))) + head_pad[:, 512:640].T[0:1, :]
        row16 = lax.broadcasted_iota(jnp.int32, (16, 128), 0)
        lane16 = lax.broadcasted_iota(jnp.int32, (16, 128), 1)
        label_of = jnp.zeros((16, 128), jnp.int32)
        micro_of = jnp.full((16, 128), 3, jnp.int32)
        for n in range(count_img):
            label_of = jnp.where(row16 == n, labels[n], label_of)
            micro_of = jnp.where(row16 == n, micro[n], micro_of)
        is_class = lane16 < NCLS
        live = jnp.where(micro_of < 3, 1.0, 0.0)
        onehot = jnp.where(lane16 == label_of, 1.0, 0.0)
        top = jnp.max(jnp.where(is_class, logits, -3e38), axis=1, keepdims=True)
        shifted = jnp.where(is_class, logits - top, 0.0)
        log_sum = jnp.log(jnp.sum(jnp.where(is_class, jnp.exp(shifted), 0.0), axis=1, keepdims=True))
        logp = jnp.where(is_class, shifted - log_sum, 0.0)
        per_img = -(
            0.9 * jnp.sum(onehot * logp, axis=1, keepdims=True) + 0.1 / NCLS * jnp.sum(logp, axis=1, keepdims=True)
        )
        loss = jnp.sum(live[:, 0:1] * per_img, axis=0, keepdims=True)
        dlogits = jnp.where(is_class, jnp.exp(logp) - 0.9 * onehot - 0.1 / NCLS, 0.0) * (live / live_total)
        dpool[...] = dot_exact(dlogits, head_rows.astype(F32)) * (1.0 / cells)
        head_grad = dot_exact(dlogits, pooled_low.astype(F32), ((0,), (0,)))
        bias_grad = jnp.concatenate(
            [jnp.sum(dlogits, axis=0, keepdims=True), jnp.zeros((1, 384), F32)], axis=1
        )
        block = jnp.where(row16w < NCLS, head_grad[0:16], 0.0)
        block = jnp.where(row16w == NCLS, bias_grad, block)
        small[...] = jnp.where(row16w == NCLS + 1, loss, block)

        back_rows = []
        for which in (shares, shares_x):
            for m in range(3):
                inside = jnp.where(micro_of[:, 0:1] == m, 1.0, 0.0)
                back_rows.append(jnp.sum(inside * (dpool[...] * which[...]), axis=0, keepdims=True))
        tile_in[1] = stack_rows(back_rows)
        tile_start(1)

        lax.fori_loop(2, 4, turn, 0)
        def squares(h):
            return work[h // 2, :, :, :, :, :, :, (h % 2) * 128 : (h % 2) * 128 + 128].reshape(512, 128)

        for h in range(8):
            value = squares(h)
            if h > 0:
                value = value + squares(h - 1)
            if h < 7:
                value = value + squares(h + 1)
            box_hi[:, h * 128 : h * 128 + 128], box_lo[:, h * 128 : h * 128 + 128] = split(value)

        value = jnp.concatenate([work[6].reshape(512, 256), work[7].reshape(512, 256)], axis=1)
        out_hi[...], out_lo[...] = split(value)
        out_t_hi[...], out_t_lo[...] = split(value.T)
        totals = tile_end(1)
        norm_grads = [
            totals[3:4] + totals[4:5] + totals[5:6],
            totals[0:1] + totals[1:2] + totals[2:3],
        ]
        rows_stat[4] = stack_rows(norm_grads + [jnp.broadcast_to(live_total, (1, 512))])
        rows_stat[2] = stack_rows([gain * totals[m : m + 1] / pixels[m] for m in range(3)])
        rows_stat[3] = stack_rows([gain * totals[3 + m : 4 + m] / pixels[m] for m in range(3)])

        def backward(pair, carry):
            parts = []
            for k in range(2):
                n = 2 * pair + k
                mean, dead = image_rows(n, 0)
                rstd, _ = image_rows(n, 1)
                rstd = rstd + dead
                offset, _ = image_rows(n, 2)
                slope, _ = image_rows(n, 3)
                parts.append((mean, rstd, offset, slope, gain * dpool[pl.ds(n, 1)], pl.ds(pl.multiple_of(n * 8, 8), 8)))
            for h in range(8):
                values = []
                for mean, rstd, offset, slope, factor, at in parts:
                    xhat = (conv[h, at] - mean) * rstd
                    values.append(rstd * (factor * share[h, at] - offset - xhat * slope))
                rows = pl.ds(pl.multiple_of(h * 128 + 16 * pair, 16), 16)
                grad_low[rows] = jnp.concatenate(values, axis=0).astype(BF16)
            return carry

        lax.fori_loop(0, count_img // 2, backward, 0)

        def rotate(k, carry):
            rows = pl.ds(pl.multiple_of(k * 256, 256), 256)
            value = dot(grad_low[rows], out_hi[...]) + dot(grad_low[rows], out_lo[...])
            rot_hi[rows] = value.astype(BF16)
            rot2_hi[rows], rot2_lo[rows] = split(value * value)
            return carry

        lax.fori_loop(0, 4, rotate, 0)

    def exchange(half_sum, away, gathered_hi, gathered_lo):
        got = (got0, got1, got2, got3, got4)
        left_home = set()
        live_total = rows_stat[4, 2:3, 0:1]
        norm_grads = [rows_stat[4, 0:1], rows_stat[4, 1:2]]
        moments = [
        ]
        for copy in moments:
            copy.start()

        def region(unit, fixed, first=1):
            return (unit,) + tuple(fixed.get(k, slice(None)) for k in range(first, 5))

        def rs_copy(unit, stage):
            if stage < 5:
                order = (0,) + RS_ORDER[unit]
                fixed = {k: mine[k] for k in order[:stage]}
                fixed[order[stage]] = 1 - mine[order[stage]]
                target, to = got[stage].at[RS_SLOT[unit][stage]], partner(order[stage])
                sems = (send_sem.at[RS_SEND[unit][stage]], recv_sem.at[sum(GOT_COUNT[:stage]) + RS_SLOT[unit][stage]])
            else:
                fixed = dict(enumerate(mine[:5]))
                target, to = got_more.at[unit, stage - 5], partner(stage)
                sems = (more_sem.at[0, unit, stage - 5], more_sem.at[1, unit, stage - 5])
            source = half_sum.at[region(unit, fixed)] if stage else away.at[UNITS.index(unit) % AWAY]
            return pltpu.make_async_remote_copy(
                src_ref=source,
                dst_ref=target,
                send_sem=sems[0],
                recv_sem=sems[1],
                device_id=to,
                device_id_type=MESH,
            )

        def ag_copy(unit, stage):
            order = (0,) + AG_ORDER[unit]
            where = work.at[region(unit, {k: mine[k] for k in order[: 5 - stage]}, 0)]
            return pltpu.make_async_remote_copy(
                src_ref=where,
                dst_ref=where,
                send_sem=send_sem.at[AG_SEND[unit][stage]],
                recv_sem=recv_sem.at[AG_RECV[unit][stage]],
                device_id=partner(order[4 - stage]),
                device_id_type=MESH,
            )

        def sm_copy(stage):
            return pltpu.make_async_remote_copy(
                src_ref=small,
                dst_ref=small_got.at[stage],
                send_sem=sm_send.at[stage],
                recv_sem=sm_recv.at[stage],
                device_id=partner(stage),
                device_id_type=MESH,
            )

        def do_mm(unit, stage):
            tap, cols = unit // 2, slice((unit % 2) * 256, (unit % 2) * 256 + 256)
            dy, dx = tap // 3, tap % 3
            place = UNITS.index(unit)
            if place >= AWAY and UNITS[place - AWAY] not in left_home:
                left_home.add(UNITS[place - AWAY])
                rs_copy(UNITS[place - AWAY], 0).wait_send()
            for stays, half in enumerate((1 - core, core)):
                rows = pl.ds(pl.multiple_of(half * 256, 256), 256)
                if tap == STAT:
                    value = (
                        dot(box_hi[rows], rot2_hi[:, cols])
                        + dot(box_hi[rows], rot2_lo[:, cols])
                        + dot(box_lo[rows], rot2_hi[:, cols])
                    )
                else:
                    value = dot(turned_hi[dx, rows, dy * 128 : dy * 128 + 1024], rot_hi[:, cols])
                value = value.reshape(2, 2, 2, 2, 16, 256)
                if stays:
                    half_sum[unit] = value
                else:
                    away[place % AWAY] = value
                    rs_copy(unit, 0).start()

        def do_rs(unit, stage):
            if stage == 0 and unit in left_home:
                rs_copy(unit, stage).wait_recv()
            else:
                rs_copy(unit, stage).wait()
                if stage == 0:
                    left_home.add(unit)
            if stage < 5:
                fixed = {k: mine[k] for k in ((0,) + RS_ORDER[unit])[: stage + 1]}
                source, at = got[stage], (RS_SLOT[unit][stage],)
            else:
                fixed = dict(enumerate(mine[:5]))
                source, at = got_more, (unit, stage - 5)
            left = [k for k in range(1, 5) if k not in fixed]

            def add(i, carry):
                inner = dict(fixed)
                where = at
                if len(left) >= 3:
                    inner[left[0]], inner[left[1]] = i // 2, i % 2
                    where = at + (i // 2, i % 2)
                half_sum[region(unit, inner)] += source[where]
                return carry

            if len(left) >= 3:
                lax.fori_loop(0, 4, add, 0)
            else:
                add(0, 0)
            if stage < 4 + extra:
                rs_copy(unit, stage + 1).start()
            if stage >= 4 and stage < 4 + extra:
                do_rs(unit, stage + 1)

        def do_post(tap, stage):
            pair = (2 * tap, 2 * tap + 1)
            value = jnp.concatenate([half_sum[region(unit, own)] for unit in pair], axis=1)
            if tap == STAT:
                value = 0.95 * eig[...] + 0.05 * (value * (live_total * float(area * area)))
                scale_rows[...] = value + DAMPING
            else:
                high, low = split(value / scale_rows[...])
                value = dot(high, out_t_hi[...]) + dot(high, out_t_lo[...]) + dot(low, out_t_hi[...])
            for k, unit in enumerate(pair):
                work[region(unit, own, 0)] = value[:, 256 * k : 256 * k + 256]
                ag_copy(unit, 0).start()

        def do_ag(unit, stage):
            ag_copy(unit, stage).wait()
            if stage < 4:
                ag_copy(unit, stage + 1).start()


        def do_fin(unit, stage):
            if unit // 2 == STAT:
                return

            def cut(i, carry):
                rows = pl.ds(pl.multiple_of(i * 64, 64), 64)
                value = work[unit, i // 4, (i // 2) % 2, i % 2].reshape(64, 256)
                gathered_hi[rows], gathered_lo[rows] = split(value)
                return carry

            lax.fori_loop(0, 8, cut, 0)

            def tile(i, carry):
                rows = pl.ds(pl.multiple_of(i * 256, 256), 256)
                value = (
                    dot(in_hi[rows], gathered_hi[...])
                    + dot(in_hi[rows], gathered_lo[...])
                    + dot(in_lo[rows], gathered_hi[...])
                )
                work[unit, i] = value.reshape(2, 2, 2, 2, 16, 256)
                square_sum[...] += jnp.sum((value * value).reshape(32, 8, 256), axis=0)
                return carry

            lax.fori_loop(0, 2, tile, 0)

        def do_sm(stage, unused):
            sm_copy(stage).wait()
            small[...] += small_got[stage]
            if stage < 4 + extra:
                sm_copy(stage + 1).start()
            if stage >= 4 and stage < 4 + extra:
                do_sm(stage + 1, 0)

        square_sum[...] = jnp.zeros((8, 256), F32)
        sm_copy(0).start()
        run = (do_mm, do_rs, do_post, do_ag, do_fin, do_sm)
        for kind, which, stage in TASKS:
            run[kind](which, stage)

        block = small[...]
        head_part = jnp.where(row16w <= NCLS, block, 0.0)
        squared = (
            jnp.sum(jnp.sum(square_sum[...], axis=0, keepdims=True), axis=1, keepdims=True)
            + jnp.sum(norm_grads[0] * norm_grads[0] + norm_grads[1] * norm_grads[1], axis=1, keepdims=True)
            + jnp.sum(jnp.sum(head_part * head_part, axis=0, keepdims=True), axis=1, keepdims=True)
        )
        norm = jnp.sqrt(squared)
        factor = jnp.minimum(1.0, CLIP / (norm + 1e-06))
        facts[0:16] = block
        facts[16:24] = stack_rows(norm_grads + [block[NCLS + 1 : NCLS + 2], live_total, norm, factor])
        for copy in moments:
            copy.wait()

    square = (512, 512)
    pl.run_scoped(
        prepare,
        pltpu.VMEM((3, 10 * stride, 512), BF16),
        pltpu.VMEM((3, 1024, 512), BF16),
        pltpu.VMEM((2, 3, 512, 512), BF16),
        pltpu.VMEM((8, stride, 512), F32),
        pltpu.VMEM((8, stride, 512), F32),
        pltpu.VMEM((count_img, 8, 8, 512), BF16),
        *[pltpu.VMEM(square, BF16)] * 4,
        pltpu.VMEM((1024, 512), BF16),
    )
    pl.run_scoped(
        exchange,
        pltpu.VMEM((20, 2, 2, 2, 2, 16, 256), F32),
        pltpu.VMEM((AWAY, 2, 2, 2, 2, 16, 256), F32),
        pltpu.VMEM((512, 256), BF16),
        pltpu.VMEM((512, 256), BF16),
    )


def adamw(weight, grad, first, second, rate):
    first = 0.9 * first + 0.1 * grad
    second = 0.999 * second + 0.001 * grad * grad
    step_size = first / (1.0 - 0.9**STEP) / (jnp.sqrt(second / (1.0 - 0.999**STEP)) + 1e-08)
    return (weight - rate * (step_size + 0.01 * weight), first, second)


def adamw_positive(weight, grad, first, second, rate):
    first = 0.9 * first + 0.1 * grad
    second = 0.999 * second + 0.001 * grad * grad
    scaled = second * (1.0 / (1.0 - 0.999**STEP))
    root = scaled * lax.rsqrt(scaled) + 1e-08
    step = first * (rate / (1.0 - 0.9**STEP)) / root
    return (weight * (1.0 - 0.01 * rate) - step, first, second)


CHUNKS = 18
LOADS = 6
RING = 4


def update_kernel(
    facts,
    gain,
    shift,
    norm_first,
    norm_second,
    head,
    head_first,
    head_second,
    gradients,
    first_hbm,
    second_hbm,
    loss_parts,
    grad_norm,
    norm_new,
    norm_m,
    norm_v,
    head_new,
    head_m,
    head_v,
    conv_new,
    conv_m,
    conv_v,
    scales_new,
    out_new,
    out_m,
    out_v,
    first,
    second,
    in_sem,
    out_sem,
    scale_sem,
):
    tall = TAPS * 512 // CHUNKS
    outs = ((out_new, conv_new), (out_m, conv_m), (out_v, conv_v))

    def store(k, i):
        rows = pl.ds(pl.multiple_of(i * tall, tall), tall)
        return pltpu.make_async_copy(outs[k][0].at[i % RING], outs[k][1].at[rows], out_sem.at[k, i % RING])

    pairs = ((first_hbm, first), (second_hbm, second))

    def load(k, i):
        deep = TAPS * 512 // LOADS
        rows = pl.ds(pl.multiple_of(i * deep, deep), deep)
        return pltpu.make_async_copy(pairs[k][0].at[rows], pairs[k][1].at[rows], in_sem.at[k, i])

    def start(i, carry):
        for k in range(len(pairs)):
            load(k, i).start()
        return carry

    lax.fori_loop(0, LOADS, start, 0)
    factor = facts[21:22, 0:1]

    def chunk(i, carry):
        @pl.when(i % (CHUNKS // LOADS) == 0)
        def _():
            for k in range(len(pairs)):
                load(k, i // (CHUNKS // LOADS)).wait()

        @pl.when(i >= RING)
        def _():
            for k in range(3):
                store(k, i).wait()

        def piece(j, inner):
            rows = pl.ds(pl.multiple_of(i * tall + j * 128, 128), 128)
            at = pl.ds(pl.multiple_of(j * 128, 128), 128)
            for half in range(2):
                cols = slice(256 * half, 256 * half + 256)
                where = (i % 2, j)
                grad = gradients[(2 * (i // 2) + half,) + where].reshape(128, 256)
                weight = gradients[(WEIGHT + 2 * (i // 2) + half,) + where].reshape(128, 256)
                out_new[i % RING, at, cols], out_m[i % RING, at, cols], out_v[i % RING, at, cols] = adamw_positive(
                    weight, factor * grad, first[rows, cols].astype(F32), second[rows, cols].astype(F32), 0.02
                )
            return inner

        lax.fori_loop(0, tall // 128, piece, 0)
        for k in range(3):
            store(k, i).start()
        return carry

    lax.fori_loop(0, CHUNKS, chunk, 0)
    scale_copies = [
        pltpu.make_async_copy(
            gradients.at[2 * STAT + k], scales_new.at[:, :, :, :, :, :, 256 * k : 256 * k + 256], scale_sem.at[k]
        )
        for k in range(2)
    ]
    for copy in scale_copies:
        copy.start()

    loss_parts[0] = facts[18, 0]
    loss_parts[1] = facts[19, 0]
    grad_norm[0] = facts[20, 0]
    grads = factor * facts[16:18, :]
    weights = jnp.concatenate([gain[...], shift[...]], axis=0)
    norm_new[...], norm_m[...], norm_v[...] = adamw(weights, grads, norm_first[...], norm_second[...], 0.1)
    block = factor * facts[0:16, :]
    head_new[:, 0:512], head_m[:, 0:512], head_v[:, 0:512] = adamw(
        head[:, 0:512], block[0:NCLS], head_first[:, 0:512], head_second[:, 0:512], 0.05
    )
    bias = jnp.concatenate([block[0:16, 0:128], jnp.zeros((112, 128), F32)], axis=0).T[0:NCLS, NCLS : NCLS + 1]
    head_new[:, 512:513], head_m[:, 512:513], head_v[:, 512:513] = adamw(
        head[:, 512:513], bias, head_first[:, 512:513], head_second[:, 512:513], 0.05
    )
    for i in range(CHUNKS - RING, CHUNKS):
        for k in range(3):
            store(k, i).wait()
    for copy in scale_copies:
        copy.wait()


def shards(
    sizes,
    images,
    micro_ids,
    labels,
    conv_weight,
    conv_first,
    conv_second,
    eig_scales,
    basis_in,
    basis_out,
    batchnorm_gain,
    batchnorm_shift,
    norm_first,
    norm_second,
    head,
    head_first,
    head_second,
):
    dp_count, rep_count = sizes
    count_img = images.shape[0]
    chips = dp_count * rep_count // 2
    bit_count = (dp_count * rep_count - 1).bit_length()
    extra = bit_count - 5
    vmem = pl.BlockSpec(memory_space=pltpu.VMEM)
    smem = pl.BlockSpec(memory_space=pltpu.SMEM)
    hbm = pl.BlockSpec(memory_space=pltpu.HBM)
    gain = batchnorm_gain.reshape(1, 512)
    shift = batchnorm_shift.reshape(1, 512)
    pixels = 8 * count_img
    square = (512, 512)
    dma = pltpu.SemaphoreType.DMA
    scratch = [
        pltpu.SMEM((count_img,), jnp.int32),
        pltpu.SMEM((count_img,), jnp.int32),
        pltpu.VMEM((1, 512), F32),
        pltpu.VMEM((1, 512), F32),
        pltpu.VMEM((NCLS, 513), F32),
        pltpu.VMEM((GOT_COUNT[0], 2, 2, 2, 2, 16, 256), F32),
        pltpu.VMEM((GOT_COUNT[1], 2, 2, 2, 16, 256), F32),
        pltpu.VMEM((GOT_COUNT[2], 2, 2, 16, 256), F32),
        pltpu.VMEM((GOT_COUNT[3], 2, 16, 256), F32),
        pltpu.VMEM((GOT_COUNT[4], 16, 256), F32),
        pltpu.VMEM((20, extra, 16, 256) if extra else (1, 1, 8, 128), F32),
        pltpu.VMEM((16, 512), F32),
        pltpu.VMEM((bit_count, 16, 512), F32),
        pltpu.VMEM((2, 8, 512), F32),
        pltpu.VMEM((2, 8, 256), F32),
        pltpu.VMEM((2, chips, 8, 256), F32),
        pltpu.VMEM((2, 2, 8, 256), F32),
        pltpu.VMEM((3, 512, 1280), BF16),
        pltpu.VMEM((512, 1024), BF16),
        pltpu.VMEM((512, 1024), BF16),
        *[pltpu.VMEM((1024, 512), BF16)] * 3,
        pltpu.VMEM((16, 512), F32),
        *[pltpu.VMEM(square, BF16)] * 4,
        pltpu.VMEM((5, 8, 512), F32),
        *[pltpu.VMEM((16, 512), F32)] * 4,
        pltpu.VMEM((128, 640), F32),
        pltpu.VMEM((16, 512), F32),
        pltpu.VMEM((8, 256), F32),
        dma((2 * TAPS,)),
        dma((11,)),
        dma((SEND_COUNT,)),
        dma((RECV_COUNT,)),
        dma((2, 20, extra) if extra else (1, 1, 1)),
        dma((bit_count,)),
        dma((bit_count,)),
        dma((4,)),
        dma((4,)),
        dma((2,)),
        dma((2,)),
    ]
    turned_basis = [x.reshape(2, 2, 2, 2, 2, 16, 512) for x in (basis_in, basis_out)]
    gradients, facts = pl.pallas_call(
        functools.partial(main_kernel, (dp_count, rep_count, count_img)),
        out_shape=(
            pltpu.VMEM((WEIGHT + 2 * TAPS, 2, 2, 2, 2, 2, 16, 256), F32),
            pltpu.VMEM((24, 512), F32),
        ),
        in_specs=[hbm] * 10,
        out_specs=(vmem,) * 2,
        scratch_shapes=scratch,
        compiler_params=pltpu.CompilerParams(
            collective_id=0, has_side_effects=True, vmem_limit_bytes=40 * 2**20
        ),
        name="reduce_and_precondition",
    )(
        micro_ids,
        labels,
        images,
        gain,
        shift,
        head.T,
        conv_weight.reshape(TAPS, 2, 2, 2, 2, 2, 16, 512),
        eig_scales,
        *turned_basis,
    )
    tall = TAPS * 512 // CHUNKS
    head_shape = (NCLS, 513)
    outs = pl.pallas_call(
        update_kernel,
        out_shape=(
            jax.ShapeDtypeStruct((2,), F32),
            jax.ShapeDtypeStruct((1,), F32),
            *[jax.ShapeDtypeStruct((2, 512), F32)] * 3,
            *[jax.ShapeDtypeStruct(head_shape, F32)] * 3,
            *[jax.ShapeDtypeStruct((TAPS * 512, 512), F32)] * 3,
            jax.ShapeDtypeStruct((2, 2, 2, 2, 2, 16, 512), F32),
        ),
        in_specs=[vmem] * 9 + [hbm] * 2,
        out_specs=(smem, smem) + (vmem,) * 6 + (hbm,) * 4,
        scratch_shapes=[
            *[pltpu.VMEM((RING, tall, 512), F32)] * 3,
            *[pltpu.VMEM((TAPS * 512, 512), BF16)] * 2,
            dma((2, LOADS)),
            dma((3, RING)),
            dma((2,)),
        ],
        compiler_params=pltpu.CompilerParams(vmem_limit_bytes=17 * 2**20),
        name="adamw",
    )(
        facts,
        gain,
        shift,
        norm_first,
        norm_second,
        head.T,
        head_first.T,
        head_second.T,
        gradients,
        *(pltpu.with_memory_space_constraint(x, pltpu.HBM) for x in (conv_first, conv_second)),
    )
    loss_parts, grad_norm, norm_new, norm_m, norm_v, head_new, head_m, head_v, conv_new, conv_m, conv_v, scales_new = outs
    return (
        loss_parts,
        grad_norm.reshape(()),
        conv_new,
        conv_m,
        conv_v,
        scales_new.reshape(square),
        norm_new,
        norm_m,
        norm_v,
        head_new.T,
        head_m.T,
        head_v.T,
    )


def solution(mesh):
    split_images = P(("dp", "rep"))
    in_specs = (P(("dp", "rep"), None, None, None), split_images, split_images) + (P(),) * 13
    sizes = (mesh.shape["dp"], mesh.shape["rep"])
    return jax.shard_map(
        functools.partial(shards, sizes), mesh=mesh, in_specs=in_specs, out_specs=(P(),) * 12, check_vma=False
    )
```

```python
import functools

import jax
import jax.numpy as jnp
from jax import lax
from jax.experimental import pallas as pl
from jax.experimental.pallas import tpu as pltpu
from jax.sharding import PartitionSpec as P

NCLS = 10
STEP = 5
NORM_EPS = 1e-05
DAMPING = 0.001
CLIP = 0.01
MESH = pl.DeviceIdType.MESH
F32 = jnp.float32
BF16 = jnp.bfloat16
HIGHEST = lax.Precision.HIGHEST
TAPS = 9
STAT = 9
WEIGHT = 20
AWAY = 4
UNITS = (13, 4, 14, 5, 7, 18, 3, 19, 15, 12, 0, 17, 9, 10, 16, 11, 6, 2, 1, 8)
RS_ORDER = (
    (3, 1, 2, 4), (1, 2, 3, 4), (1, 2, 3, 4), (2, 1, 3, 4), (3, 1, 4, 2),
    (1, 3, 4, 2), (1, 2, 3, 4), (3, 1, 2, 4), (1, 2, 3, 4), (2, 1, 3, 4),
    (2, 3, 4, 1), (2, 3, 1, 4), (1, 2, 3, 4), (2, 3, 1, 4), (1, 2, 3, 4),
    (3, 1, 4, 2), (1, 2, 3, 4), (2, 3, 4, 1), (2, 1, 3, 4), (1, 2, 3, 4),
)
AG_ORDER = (
    (1, 3, 4, 2), (3, 4, 2, 1), (2, 3, 1, 4), (1, 3, 4, 2), (1, 2, 3, 4),
    (1, 2, 3, 4), (3, 1, 2, 4), (1, 2, 3, 4), (2, 3, 4, 1), (3, 4, 1, 2),
    (2, 1, 3, 4), (2, 1, 3, 4), (1, 2, 3, 4), (2, 1, 3, 4), (2, 3, 1, 4),
    (3, 2, 1, 4), (1, 2, 3, 4), (2, 3, 4, 1), (1, 2, 3, 4), (2, 1, 3, 4),
)
TASKS = (
    (0, 13, 0), (0, 4, 0), (0, 14, 0), (5, 0, 0), (1, 13, 0), (0, 5, 0), (1, 4, 0), (1, 14, 0),
    (0, 7, 0), (0, 18, 0), (1, 5, 0), (1, 7, 0), (5, 1, 0), (0, 3, 0), (1, 18, 0), (0, 19, 0),
    (1, 3, 0), (1, 13, 1), (0, 15, 0), (1, 19, 0), (1, 14, 1), (1, 4, 1), (5, 2, 0), (0, 12, 0),
    (0, 0, 0), (1, 15, 0), (0, 17, 0), (1, 12, 0), (1, 7, 1), (1, 5, 1), (1, 0, 0), (1, 18, 1),
    (1, 17, 0), (0, 9, 0), (1, 13, 2), (0, 10, 0), (5, 3, 0), (0, 16, 0), (1, 9, 0), (1, 19, 1),
    (1, 3, 1), (1, 10, 0), (0, 11, 0), (1, 16, 0), (1, 4, 2), (1, 14, 2), (0, 6, 0), (1, 15, 1),
    (0, 2, 0), (1, 11, 0), (0, 1, 0), (1, 5, 2), (1, 6, 0), (0, 8, 0), (1, 2, 0), (1, 12, 1),
    (1, 1, 0), (1, 17, 1), (1, 8, 0), (1, 7, 2), (1, 0, 1), (1, 18, 2), (1, 9, 1), (5, 4, 0),
    (1, 13, 3), (1, 14, 3), (1, 4, 3), (1, 19, 2), (1, 3, 2), (1, 5, 3), (1, 17, 2), (1, 18, 3),
    (1, 10, 1), (1, 16, 1), (1, 13, 4), (1, 19, 3), (1, 14, 4), (1, 3, 3), (1, 15, 2), (1, 11, 1),
    (1, 17, 3), (1, 18, 4), (1, 10, 2), (1, 12, 2), (1, 6, 1), (1, 7, 3), (1, 4, 4), (1, 19, 4),
    (2, 9, 0), (1, 5, 4), (1, 3, 4), (2, 2, 0), (1, 15, 3), (1, 11, 2), (1, 16, 2), (1, 2, 1),
    (1, 12, 3), (1, 6, 2), (1, 10, 3), (1, 15, 4), (2, 7, 0), (1, 7, 4), (3, 18, 0), (1, 1, 1),
    (3, 19, 0), (1, 16, 3), (1, 2, 2), (3, 4, 0), (1, 6, 3), (3, 5, 0), (1, 12, 4), (2, 6, 0),
    (1, 8, 1), (3, 18, 1), (3, 14, 0), (3, 19, 1), (1, 1, 2), (3, 15, 0), (1, 0, 2), (1, 2, 3),
    (1, 16, 4), (3, 4, 1), (1, 9, 2), (1, 17, 4), (2, 8, 0), (3, 5, 1), (1, 8, 2), (1, 6, 4),
    (1, 11, 3), (2, 3, 0), (1, 10, 4), (3, 12, 0), (3, 14, 1), (1, 1, 3), (3, 18, 2), (3, 13, 0),
    (1, 0, 3), (1, 9, 3), (1, 2, 4), (2, 1, 0), (3, 19, 2), (3, 15, 1), (1, 8, 3), (3, 4, 2),
    (3, 16, 0), (3, 17, 0), (1, 11, 4), (2, 5, 0), (3, 5, 2), (3, 6, 0), (3, 12, 1), (3, 3, 0),
    (3, 7, 0), (3, 18, 3), (3, 14, 2), (3, 13, 1), (1, 1, 4), (3, 18, 4), (3, 19, 3), (4, 18, 0),
    (1, 0, 4), (2, 0, 0), (1, 9, 4), (3, 4, 3), (3, 15, 2), (3, 2, 0), (3, 19, 4), (3, 16, 1),
    (1, 8, 4), (2, 4, 0), (3, 6, 1), (4, 19, 0), (3, 4, 4), (4, 4, 0), (3, 12, 2), (3, 11, 0),
    (3, 10, 0), (3, 5, 3), (3, 17, 1), (3, 7, 1), (3, 3, 1), (3, 13, 2), (3, 5, 4), (4, 5, 0),
    (3, 0, 0), (3, 1, 0), (3, 14, 3), (3, 2, 1), (3, 8, 0), (3, 15, 3), (3, 11, 1), (3, 16, 2),
    (3, 6, 2), (3, 14, 4), (3, 9, 0), (4, 14, 0), (3, 10, 1), (3, 15, 4), (4, 15, 0), (3, 17, 2),
    (3, 7, 2), (3, 12, 3), (3, 3, 2), (3, 11, 2), (3, 12, 4), (3, 13, 3), (4, 12, 0), (3, 0, 1),
    (3, 1, 1), (3, 2, 2), (3, 13, 4), (4, 13, 0), (3, 8, 1), (3, 16, 3), (3, 9, 1), (3, 17, 3),
    (3, 16, 4), (4, 16, 0), (3, 10, 2), (3, 17, 4), (3, 6, 3), (4, 17, 0), (3, 0, 2), (3, 11, 3),
    (3, 6, 4), (4, 6, 0), (3, 7, 3), (3, 1, 2), (3, 11, 4), (4, 11, 0), (3, 2, 3), (3, 8, 2),
    (3, 7, 4), (4, 7, 0), (3, 3, 3), (3, 2, 4), (3, 9, 2), (4, 2, 0), (3, 10, 3), (3, 3, 4),
    (4, 3, 0), (3, 1, 3), (3, 0, 3), (3, 10, 4), (4, 10, 0), (3, 1, 4), (3, 8, 3), (4, 1, 0),
    (3, 0, 4), (3, 9, 3), (4, 0, 0), (3, 8, 4), (4, 8, 0), (3, 9, 4), (4, 9, 0),
)
GOT_COUNT = (6, 17, 14, 10, 11)
RECV_COUNT, SEND_COUNT = 59, 20
RS_SLOT = (
    (4, 11, 12, 2, 5), (1, 15, 0, 1, 0), (4, 14, 3, 0, 3), (0, 7, 7, 6, 6), (1, 2, 1, 2, 3),
    (3, 4, 3, 3, 5), (3, 2, 2, 4, 2), (4, 3, 4, 8, 8), (2, 16, 1, 4, 7), (1, 12, 13, 3, 6),
    (2, 13, 0, 2, 10), (0, 1, 1, 9, 4), (3, 9, 10, 1, 0), (0, 0, 0, 0, 0), (2, 1, 2, 1, 1),
    (2, 8, 9, 0, 7), (5, 0, 11, 3, 1), (0, 10, 8, 7, 9), (5, 5, 5, 4, 2), (1, 6, 6, 5, 4),
)
AG_RECV = (
    (12, 17, 10, 24, 6), (29, 6, 11, 4, 1), (22, 14, 18, 12, 2), (4, 28, 4, 23, 0), (2, 8, 0, 20, 1),
    (3, 9, 17, 26, 2), (2, 9, 33, 20, 0), (18, 10, 3, 22, 1), (15, 38, 13, 5, 0), (34, 8, 14, 16, 2),
    (25, 35, 9, 15, 3), (24, 31, 5, 21, 3), (10, 3, 23, 37, 2), (13, 6, 11, 16, 0), (5, 11, 19, 13, 0),
    (7, 15, 21, 30, 1), (1, 8, 32, 7, 1), (16, 27, 36, 19, 2), (0, 4, 12, 5, 58), (1, 6, 14, 7, 0),
)
RS_SEND = (
    (10, 10, 10, 10, 10), (18, 18, 4, 4, 4), (17, 17, 14, 14, 14), (6, 6, 6, 6, 2), (1, 1, 1, 1, 1),
    (3, 3, 3, 3, 3), (16, 16, 11, 11, 11), (4, 4, 4, 4, 4), (19, 19, 17, 17, 17), (12, 12, 12, 12, 12),
    (13, 13, 13, 5, 5), (15, 15, 7, 7, 7), (9, 9, 9, 9, 9), (0, 0, 0, 0, 0), (2, 2, 2, 2, 2),
    (8, 8, 8, 6, 6), (14, 14, 14, 13, 13), (11, 11, 11, 11, 8), (5, 5, 5, 5, 5), (7, 7, 7, 7, 0),
)
AG_SEND = (
    (1, 1, 1, 1, 1), (4, 3, 3, 3, 3), (14, 12, 6, 6, 5), (16, 16, 16, 13, 6), (2, 2, 2, 2, 2),
    (3, 3, 3, 3, 3), (11, 11, 11, 11, 7), (18, 18, 15, 12, 7), (8, 8, 2, 2, 0), (14, 4, 4, 4, 1),
    (7, 7, 7, 0, 0), (19, 5, 5, 5, 5), (9, 5, 5, 2, 2), (16, 9, 9, 9, 2), (6, 6, 6, 6, 4),
    (15, 15, 15, 10, 10), (8, 8, 0, 0, 0), (13, 13, 13, 10, 8), (0, 0, 0, 0, 0), (1, 1, 1, 1, 0),
)


def split(value):
    high = value.astype(BF16)
    return high, (value - high.astype(F32)).astype(BF16)


def dot(a, b, dims=((1,), (0,))):
    return lax.dot_general(a, b, (dims, ((), ())), preferred_element_type=F32)


def dot_exact(a, b, dims=((1,), (0,))):
    return lax.dot_general(a, b, (dims, ((), ())), precision=HIGHEST, preferred_element_type=F32)


def main_kernel(
    sizes,
    micro_hbm,
    labels_hbm,
    images_hbm,
    gain_hbm,
    shift_hbm,
    head_hbm,
    weight,
    first_hbm,
    second_hbm,
    eig_hbm,
    in_hbm,
    out_hbm,
    work,
    facts,
    moments_held,
    micro,
    labels,
    gain_ref,
    shift_ref,
    head,
    got0,
    got1,
    got2,
    got3,
    got4,
    got_more,
    small,
    small_half,
    small_back,
    small_got,
    tile_in,
    tile_core,
    tile_slots,
    tile_out,
    turned_hi,
    box_hi,
    box_lo,
    rot_hi,
    rot2_hi,
    rot2_lo,
    eig,
    in_hi,
    in_lo,
    out_t_hi,
    out_t_lo,
    rows_stat,
    pooled,
    shares,
    shares_x,
    dpool,
    head_pad,
    scale_rows,
    square_sum,
    w_sem,
    load_sem,
    send_sem,
    recv_sem,
    more_sem,
    sm_send,
    sm_recv,
    core_send,
    core_recv,
    chip_send,
    chip_recv,
):
    dp_count, rep_count, count_img = sizes
    area = 64
    cells = 16
    chips = dp_count * rep_count // 2
    dp = lax.axis_index("dp")
    rep = lax.axis_index("rep")
    core = rep % 2
    chip = dp * (rep_count // 2) + rep // 2
    bits = [("rep", 1), ("dp", 1), ("rep", 2), ("dp", 2), ("dp", 4)]
    step = 8
    while step < dp_count:
        bits.append(("dp", step))
        step *= 2
    step = 4
    while step < rep_count:
        bits.append(("rep", step))
        step *= 2
    extra = len(bits) - 5
    stride = count_img * 8
    mine = [((dp if name == "dp" else rep) // weight_of) % 2 for name, weight_of in bits]

    own = dict(enumerate(mine[:5]))
    own_block = (((mine[0] * 2 + mine[1]) * 2 + mine[2]) * 2 + mine[3]) * 2 + mine[4]

    def partner(k):
        name, weight_of = bits[k]
        change = (1 - 2 * mine[k]) * weight_of
        return (dp + change, rep) if name == "dp" else (dp, rep + change)

    def chip_device(q):
        return (q // (rep_count // 2), (q % (rep_count // 2)) * 2 + core)

    def weight_copy(unit):
        cols = pl.ds(pl.multiple_of((unit % 2) * 256, 256), 256)
        return pltpu.make_async_copy(
            weight.at[unit // 2, :, :, :, :, :, :, cols], work.at[WEIGHT + unit], w_sem.at[unit // 6]
        )

    def start_weight(unit, carry):
        weight_copy(unit).start()
        return carry

    loads = [
        pltpu.make_async_copy(src, dst, load_sem.at[k])
        for k, (src, dst) in enumerate(
            (
                (in_hbm.at[:, :, :, :, :, :, 0:256], work.at[4]),
                (in_hbm.at[:, :, :, :, :, :, 256:512], work.at[5]),
                (out_hbm.at[:, :, :, :, :, :, 0:256], work.at[6]),
                (out_hbm.at[:, :, :, :, :, :, 256:512], work.at[7]),
                (eig_hbm.at[pl.ds(pl.multiple_of(own_block * 16, 16), 16)], eig),
            )
        )
    ]

    barrier = pltpu.get_barrier_semaphore()

    def greet(k, carry):
        pl.semaphore_signal(barrier, inc=1, device_id=chip_device((chip + k) % chips), device_id_type=MESH)
        return carry

    lax.fori_loop(1, chips, greet, 0)
    pl.semaphore_signal(barrier, inc=1, device_id=partner(0), device_id_type=MESH)

    row8 = lax.broadcasted_iota(jnp.int32, (8, 512), 0)
    row16w = lax.broadcasted_iota(jnp.int32, (16, 512), 0)
    zero_tile = jnp.zeros((8, 512), F32)

    def stack_rows(rows):
        tile = zero_tile
        for k, row in enumerate(rows):
            tile = jnp.where(row8 == k, jnp.broadcast_to(row, (8, 512)), tile)
        return tile

    def core_half(which):
        return pl.ds(pl.multiple_of(which * 256, 256), 256)

    def prepare(
        narrow, wide, weight_low, conv, share, images, in_t_hi, in_t_lo, out_hi, out_lo, grad_low
    ):
        first_loads = [
            pltpu.make_async_copy(src, dst, load_sem.at[5 + k])
            for k, (src, dst) in enumerate(
                (
                    (images_hbm, images),
                    (micro_hbm, micro),
                    (labels_hbm, labels),
                    (gain_hbm, gain_ref),
                    (shift_hbm, shift_ref),
                    (head_hbm, head),
                )
            )
        ]
        first_loads[0].start()
        first_loads[1].start()
        lax.fori_loop(0, 12, start_weight, 0)
        for copy in first_loads[2:]:
            copy.start()

        column = lax.broadcasted_iota(jnp.int32, (2, 8, 512), 1)
        for k in range(3):
            narrow[k, 0:stride] = jnp.zeros((stride, 512), BF16)
            narrow[k, 9 * stride : 10 * stride] = jnp.zeros((stride, 512), BF16)

        def build(h, carry):
            for pair in range(count_img // 2):
                block = images[2 * pair : 2 * pair + 2, h].astype(F32)
                left = jnp.where(column == 0, 0.0, pltpu.roll(block, 1, 1))
                right = jnp.where(column == 7, 0.0, pltpu.roll(block, 7, 1))
                at = pl.ds(pl.multiple_of((h + 1) * stride + 16 * pair, 16), 16)
                for k, value in enumerate((left, block, right)):
                    narrow[k, at] = value.reshape(16, 512).astype(BF16)
            return carry

        first_loads[0].wait()
        lax.fori_loop(0, 8, build, 0)

        def wait_row(dy):
            held = work.at[pl.ds(WEIGHT + 6 * dy, 6)]
            pltpu.make_async_copy(held, held, w_sem.at[dy]).wait()

        def cast(dy, k):
            dx, j, half = k // 4, (k // 2) % 2, k % 2
            piece = work[WEIGHT + 2 * (3 * dy + dx) + j, half].reshape(256, 256)
            weight_low[dy % 2, dx, 256 * half : 256 * half + 256, 256 * j : 256 * j + 256] = piece.astype(BF16)

        wait_row(0)
        lax.fori_loop(12, 2 * TAPS, start_weight, 0)
        for k in range(12):
            cast(0, k)
        for dy in range(3):
            if dy < 2:
                wait_row(dy + 1)
            if dy == 1:
                for copy in loads:
                    copy.start()
            for m in range(2):
                for n in range(2):
                    total = None
                    for dx in range(3):
                        begin = (dy + 4 * m) * stride
                        term = dot(
                            narrow[dx, begin : begin + 4 * stride], weight_low[dy % 2, dx, :, n * 256 : n * 256 + 256]
                        )
                        total = term if total is None else total + term
                        if dy < 2:
                            cast(dy + 1, 6 * m + 3 * n + dx)
                    at = (slice(4 * m, 4 * m + 4), slice(None), slice(n * 256, n * 256 + 256))
                    total = total.reshape(4, stride, 256)
                    conv[at] = total if dy == 0 else conv[at] + total

        for copy in first_loads[1:]:
            copy.wait()
        def member(n):
            return [jnp.where(micro[n] == m, 1.0, 0.0).astype(F32) for m in range(3)]

        def gather_sums(n, carry):
            at = pl.ds(pl.multiple_of(n * 8, 8), 8)
            first = jnp.zeros((8, 512), F32)
            second = jnp.zeros((8, 512), F32)
            for h in range(8):
                value = conv[h, at]
                first = first + value
                second = second + value * value
            kinds = member(n)
            return tuple(c + k * first for c, k in zip(carry[:3], kinds)) + tuple(
                c + k * second for c, k in zip(carry[3:6], kinds)
            )

        sums = lax.fori_loop(0, count_img, gather_sums, (zero_tile,) * 6)
        counts = [jnp.zeros((), F32)] * 3
        for n in range(count_img):
            counts = [c + k for c, k in zip(counts, member(n))]
        lane8 = lax.broadcasted_iota(jnp.int32, (8, 512), 1)

        count_row = zero_tile
        for m in range(3):
            count_row = jnp.where(lane8 % 256 == m, counts[m], count_row)
        tile_in[0] = jnp.where(row8 == 6, count_row, stack_rows([jnp.sum(s, axis=0, keepdims=True) for s in sums]))

        def tile_copy(i):
            return pltpu.make_async_remote_copy(
                src_ref=tile_in.at[i, :, core_half(1 - core)],
                dst_ref=tile_core.at[i],
                send_sem=core_send.at[2 * i],
                recv_sem=core_recv.at[2 * i],
                device_id=partner(0),
                device_id_type=MESH,
            )

        def tile_start(i):
            tile_copy(i).start()
            tile_copy(i).wait()
            tile_slots[i, 0] = tile_in[i, :, core_half(core)] + tile_core[i]

            def give(k, carry):
                pltpu.make_async_remote_copy(
                    src_ref=tile_slots.at[i, 0],
                    dst_ref=tile_slots.at[i, k],
                    send_sem=chip_send.at[i],
                    recv_sem=chip_recv.at[i],
                    device_id=chip_device((chip + k) % chips),
                    device_id_type=MESH,
                ).start()
                return carry

            lax.fori_loop(1, chips, give, 0)

        def tile_end(i):
            others = tile_slots.at[i, pl.ds(1, chips - 1)]
            pltpu.make_async_remote_copy(
                src_ref=others,
                dst_ref=others,
                send_sem=chip_send.at[i],
                recv_sem=chip_recv.at[i],
                device_id=partner(0),
                device_id_type=MESH,
            ).wait()

            def add(k, total):
                return total + tile_slots[i, (chip - k + chips) % chips]

            tile_out[i, core] = lax.fori_loop(0, chips, add, jnp.zeros((8, 256), F32))
            back = pltpu.make_async_remote_copy(
                src_ref=tile_out.at[i, core],
                dst_ref=tile_out.at[i, core],
                send_sem=core_send.at[2 * i + 1],
                recv_sem=core_recv.at[2 * i + 1],
                device_id=partner(0),
                device_id_type=MESH,
            )
            back.start()
            back.wait()
            return jnp.concatenate([tile_out[i, 0], tile_out[i, 1]], axis=1)

        pl.semaphore_wait(barrier, chips)
        tile_start(0)

        def widen(h, carry):
            source = pl.ds(pl.multiple_of((h + 1) * stride, 16), stride)
            target = pl.ds(pl.multiple_of(h * 128, 128), stride)
            fill = pl.ds(pl.multiple_of(h * 128 + stride, 16), 128 - stride)
            for k in range(3):
                wide[k, target] = narrow[k, source]
                wide[k, fill] = jnp.zeros((128 - stride, 512), BF16)
            grad_low[fill] = jnp.zeros((128 - stride, 512), BF16)
            return carry

        lax.fori_loop(0, 8, widen, 0)
        for copy in loads:
            copy.wait()
        value = jnp.concatenate([work[4].reshape(512, 256), work[5].reshape(512, 256)], axis=1)
        in_hi[...], in_lo[...] = split(value)
        in_t_hi[...], in_t_lo[...] = split(value.T)
        for dx in range(3):
            turned_hi[dx, :, 0:128] = jnp.zeros((512, 128), BF16)
            turned_hi[dx, :, 1152:1280] = jnp.zeros((512, 128), BF16)

        def turn(j, carry):
            total = None
            for dx in range(3):
                rows = wide[dx, pl.ds(pl.multiple_of(256 * j, 256), 256)]
                value = dot(in_t_hi[...], rows, ((1,), (1,))) + dot(in_t_lo[...], rows, ((1,), (1,)))
                at = pl.ds(pl.multiple_of(128 + 256 * j, 128), 256)
                turned_hi[dx, :, at] = value.astype(BF16)
                total = value * value if total is None else total + value * value
            work[j] = total.reshape(2, 2, 2, 2, 2, 16, 256)
            return carry

        lax.fori_loop(0, 2, turn, 0)

        head_pad[...] = jnp.zeros((128, 640), F32)
        head_pad[0:NCLS, 0:513] = head[...]
        head_rows = head_pad[:, 0:512].astype(BF16)
        row16 = lax.broadcasted_iota(jnp.int32, (16, 128), 0)
        lane16 = lax.broadcasted_iota(jnp.int32, (16, 128), 1)
        label_of = jnp.zeros((16, 128), jnp.int32)
        micro_of = jnp.full((16, 128), 3, jnp.int32)
        for n in range(count_img):
            label_of = jnp.where(row16 == n, labels[n], label_of)
            micro_of = jnp.where(row16 == n, micro[n], micro_of)
        is_class = lane16 < NCLS
        live = jnp.where(micro_of < 3, 1.0, 0.0)
        onehot = jnp.where(lane16 == label_of, 1.0, 0.0)
        totals = tile_end(0)

        gain = gain_ref[...]
        shift = shift_ref[...]
        live_total = totals[6:7, 0:1] + totals[6:7, 1:2] + totals[6:7, 2:3]
        pixels = [totals[6:7, m : m + 1] * float(area) for m in range(3)]
        mean_rows, rstd_rows = [], []
        for m in range(3):
            mean = totals[m : m + 1] / pixels[m]
            var = totals[3 + m : 4 + m] / pixels[m] - mean * mean
            mean_rows.append(mean)
            rstd_rows.append(lax.rsqrt(var + NORM_EPS))
        rows_stat[0] = stack_rows(mean_rows)
        rows_stat[1] = stack_rows(rstd_rows)

        def image_rows(n, k):
            kinds = member(n)
            row = sum(kinds[m] * rows_stat[k, m : m + 1] for m in range(3))
            return row, 1.0 - (kinds[0] + kinds[1] + kinds[2])

        even = lax.broadcasted_iota(jnp.int32, (8, 512), 0) % 2 == 0
        pooled[...] = jnp.zeros((16, 512), F32)
        shares[...] = jnp.zeros((16, 512), F32)
        shares_x[...] = jnp.zeros((16, 512), F32)

        def forward(n, carry):
            mean, dead = image_rows(n, 0)
            rstd, _ = image_rows(n, 1)
            rstd = rstd + dead
            at = pl.ds(pl.multiple_of(n * 8, 8), 8)
            cell_sum, share_sum, share_x_sum = zero_tile, zero_tile, zero_tile
            for a in range(4):
                xs = [(conv[2 * a + k, at] - mean) * rstd for k in range(2)]
                exps = [jnp.exp(gain * x + shift) for x in xs]
                both = exps[0] + exps[1]
                both = both + jnp.where(even, pltpu.roll(both, 7, 0), pltpu.roll(both, 1, 0))
                both = both + 4.0
                cell_sum = cell_sum + jnp.log(both)
                inverse = 1.0 / both
                for k in range(2):
                    part = exps[k] * inverse
                    share[2 * a + k, at] = part
                    share_sum = share_sum + part
                    share_x_sum = share_x_sum + part * xs[k]
            row = pl.ds(n, 1)
            pooled[row] = jnp.sum(cell_sum, axis=0, keepdims=True) * (0.5 / cells)
            shares[row] = jnp.sum(share_sum, axis=0, keepdims=True)
            shares_x[row] = jnp.sum(share_x_sum, axis=0, keepdims=True)
            return carry

        lax.fori_loop(0, count_img, forward, 0)

        pooled_low = pooled[...].astype(BF16)
        logits = dot(pooled_low, head_rows, ((1,), (1,))) + head_pad[:, 512:640].T[0:1, :]
        top = jnp.max(jnp.where(is_class, logits, -3e38), axis=1, keepdims=True)
        shifted = jnp.where(is_class, logits - top, 0.0)
        log_sum = jnp.log(jnp.sum(jnp.where(is_class, jnp.exp(shifted), 0.0), axis=1, keepdims=True))
        logp = jnp.where(is_class, shifted - log_sum, 0.0)
        per_img = -(
            0.9 * jnp.sum(onehot * logp, axis=1, keepdims=True) + 0.1 / NCLS * jnp.sum(logp, axis=1, keepdims=True)
        )
        loss = jnp.sum(live[:, 0:1] * per_img, axis=0, keepdims=True)
        dlogits = jnp.where(is_class, jnp.exp(logp) - 0.9 * onehot - 0.1 / NCLS, 0.0) * (live / live_total)
        dpool[...] = dot_exact(dlogits, head_rows.astype(F32)) * (1.0 / cells)
        back_rows = []
        for which in (shares, shares_x):
            for m in range(3):
                inside = jnp.where(micro_of[:, 0:1] == m, 1.0, 0.0)
                back_rows.append(jnp.sum(inside * (dpool[...] * which[...]), axis=0, keepdims=True))
        tile_in[1] = stack_rows(back_rows)
        tile_start(1)

        head_grad = dot_exact(dlogits, pooled_low.astype(F32), ((0,), (0,)))
        bias_grad = jnp.concatenate(
            [jnp.sum(dlogits, axis=0, keepdims=True), jnp.zeros((1, 384), F32)], axis=1
        )
        block = jnp.where(row16w < NCLS, head_grad[0:16], 0.0)
        block = jnp.where(row16w == NCLS, bias_grad, block)
        small[...] = jnp.where(row16w == NCLS + 1, loss, block)

        def scale(n, carry):
            mean, dead = image_rows(n, 0)
            rstd, _ = image_rows(n, 1)
            rstd = rstd + dead
            factor = rstd * gain * dpool[pl.ds(n, 1)]
            at = pl.ds(pl.multiple_of(n * 8, 8), 8)
            for h in range(8):
                share[h, at] = factor * share[h, at]
                conv[h, at] = (conv[h, at] - mean) * rstd * rstd
            return carry

        lax.fori_loop(0, count_img, scale, 0)

        lax.fori_loop(2, 4, turn, 0)
        def squares(h):
            return work[h // 2, :, :, :, :, :, :, (h % 2) * 128 : (h % 2) * 128 + 128].reshape(512, 128)

        for h in range(8):
            value = squares(h)
            if h > 0:
                value = value + squares(h - 1)
            if h < 7:
                value = value + squares(h + 1)
            box_hi[:, h * 128 : h * 128 + 128], box_lo[:, h * 128 : h * 128 + 128] = split(value)

        value = jnp.concatenate([work[6].reshape(512, 256), work[7].reshape(512, 256)], axis=1)
        out_hi[...], out_lo[...] = split(value)
        out_t_hi[...], out_t_lo[...] = split(value.T)
        totals = tile_end(1)
        norm_grads = [
            totals[3:4] + totals[4:5] + totals[5:6],
            totals[0:1] + totals[1:2] + totals[2:3],
        ]
        rows_stat[4] = stack_rows(norm_grads + [jnp.broadcast_to(live_total, (1, 512))])
        rows_stat[2] = stack_rows([gain * totals[m : m + 1] / pixels[m] for m in range(3)])
        rows_stat[3] = stack_rows([gain * totals[3 + m : 4 + m] / pixels[m] for m in range(3)])

        def backward(pair, carry):
            parts = []
            for k in range(2):
                n = 2 * pair + k
                rstd, dead = image_rows(n, 1)
                offset, _ = image_rows(n, 2)
                slope, _ = image_rows(n, 3)
                parts.append(((rstd + dead) * offset, slope, pl.ds(pl.multiple_of(n * 8, 8), 8)))
            for h in range(8):
                values = [share[h, at] - offset - conv[h, at] * slope for offset, slope, at in parts]
                rows = pl.ds(pl.multiple_of(h * 128 + 16 * pair, 16), 16)
                grad_low[rows] = jnp.concatenate(values, axis=0).astype(BF16)
            return carry

        lax.fori_loop(0, count_img // 2, backward, 0)

        def rotate(k, carry):
            rows = pl.ds(pl.multiple_of(k * 256, 256), 256)
            value = dot(grad_low[rows], out_hi[...]) + dot(grad_low[rows], out_lo[...])
            rot_hi[rows] = value.astype(BF16)
            rot2_hi[rows], rot2_lo[rows] = split(value * value)
            return carry

        lax.fori_loop(0, 4, rotate, 0)

    def exchange(half_sum, away, gathered_hi, gathered_lo):
        got = (got0, got1, got2, got3, got4)
        left_home = set()
        live_total = rows_stat[4, 2:3, 0:1]
        norm_grads = [rows_stat[4, 0:1], rows_stat[4, 1:2]]
        moments = [
            pltpu.make_async_copy(src, moments_held.at[pl.ds(k * TAPS * 512, TAPS * 512)], load_sem.at[k])
            for k, src in enumerate((first_hbm, second_hbm))
        ]
        for copy in moments:
            copy.start()

        def region(unit, fixed, first=1):
            return (unit,) + tuple(fixed.get(k, slice(None)) for k in range(first, 5))

        def rs_copy(unit, stage):
            if stage < 5:
                order = (0,) + RS_ORDER[unit]
                fixed = {k: mine[k] for k in order[:stage]}
                fixed[order[stage]] = 1 - mine[order[stage]]
                target, to = got[stage].at[RS_SLOT[unit][stage]], partner(order[stage])
                sems = (send_sem.at[RS_SEND[unit][stage]], recv_sem.at[sum(GOT_COUNT[:stage]) + RS_SLOT[unit][stage]])
            else:
                fixed = dict(enumerate(mine[:5]))
                target, to = got_more.at[unit, stage - 5], partner(stage)
                sems = (more_sem.at[0, unit, stage - 5], more_sem.at[1, unit, stage - 5])
            source = half_sum.at[region(unit, fixed)] if stage else away.at[UNITS.index(unit) % AWAY]
            return pltpu.make_async_remote_copy(
                src_ref=source,
                dst_ref=target,
                send_sem=sems[0],
                recv_sem=sems[1],
                device_id=to,
                device_id_type=MESH,
            )

        def ag_copy(unit, stage):
            order = (0,) + AG_ORDER[unit]
            where = work.at[region(unit, {k: mine[k] for k in order[: 5 - stage]}, 0)]
            return pltpu.make_async_remote_copy(
                src_ref=where,
                dst_ref=where,
                send_sem=send_sem.at[AG_SEND[unit][stage]],
                recv_sem=recv_sem.at[AG_RECV[unit][stage]],
                device_id=partner(order[4 - stage]),
                device_id_type=MESH,
            )

        def sm_copy(stage):
            if stage == 0:
                source, target, to = small.at[:, core_half(1 - core)], small_got.at[0], partner(0)
            elif stage < len(bits):
                source, target, to = small_half, small_got.at[stage], partner(stage)
            else:
                source, target, to = small_half, small_back, partner(0)
            return pltpu.make_async_remote_copy(
                src_ref=source,
                dst_ref=target,
                send_sem=sm_send.at[stage],
                recv_sem=sm_recv.at[stage],
                device_id=to,
                device_id_type=MESH,
            )

        def do_mm(unit, stage):
            tap, cols = unit // 2, slice((unit % 2) * 256, (unit % 2) * 256 + 256)
            dy, dx = tap // 3, tap % 3
            place = UNITS.index(unit)
            if place >= AWAY and UNITS[place - AWAY] not in left_home:
                left_home.add(UNITS[place - AWAY])
                rs_copy(UNITS[place - AWAY], 0).wait_send()
            for stays, half in enumerate((1 - core, core)):
                rows = pl.ds(pl.multiple_of(half * 256, 256), 256)
                if tap == STAT:
                    value = (
                        dot(box_hi[rows], rot2_hi[:, cols])
                        + dot(box_hi[rows], rot2_lo[:, cols])
                        + dot(box_lo[rows], rot2_hi[:, cols])
                    )
                else:
                    value = dot(turned_hi[dx, rows, dy * 128 : dy * 128 + 1024], rot_hi[:, cols])
                value = value.reshape(2, 2, 2, 2, 16, 256)
                if stays:
                    half_sum[unit] = value
                else:
                    away[place % AWAY] = value
                    rs_copy(unit, 0).start()

        def do_rs(unit, stage):
            if stage == 0 and unit in left_home:
                rs_copy(unit, stage).wait_recv()
            else:
                rs_copy(unit, stage).wait()
                if stage == 0:
                    left_home.add(unit)
            if stage < 5:
                fixed = {k: mine[k] for k in ((0,) + RS_ORDER[unit])[: stage + 1]}
                source, at = got[stage], (RS_SLOT[unit][stage],)
            else:
                fixed = dict(enumerate(mine[:5]))
                source, at = got_more, (unit, stage - 5)
            left = [k for k in range(1, 5) if k not in fixed]

            def add(i, carry):
                inner = dict(fixed)
                where = at
                if len(left) >= 3:
                    inner[left[0]], inner[left[1]] = i // 2, i % 2
                    where = at + (i // 2, i % 2)
                half_sum[region(unit, inner)] += source[where]
                return carry

            if len(left) >= 3:
                lax.fori_loop(0, 4, add, 0)
            else:
                add(0, 0)
            if stage < 4 + extra:
                rs_copy(unit, stage + 1).start()
            if stage >= 4 and stage < 4 + extra:
                do_rs(unit, stage + 1)

        def do_post(tap, stage):
            pair = (2 * tap, 2 * tap + 1)
            value = jnp.concatenate([half_sum[region(unit, own)] for unit in pair], axis=1)
            if tap == STAT:
                value = 0.95 * eig[...] + 0.05 * (value * (live_total * float(area * area)))
                scale_rows[...] = value + DAMPING
            else:
                high, low = split(value / scale_rows[...])
                value = dot(high, out_t_hi[...]) + dot(high, out_t_lo[...]) + dot(low, out_t_hi[...])
            for k, unit in enumerate(pair):
                work[region(unit, own, 0)] = value[:, 256 * k : 256 * k + 256]
                ag_copy(unit, 0).start()

        def do_ag(unit, stage):
            ag_copy(unit, stage).wait()
            if stage < 4:
                ag_copy(unit, stage + 1).start()


        def do_fin(unit, stage):
            if unit // 2 == STAT:
                return

            def cut(i, carry):
                rows = pl.ds(pl.multiple_of(i * 64, 64), 64)
                value = work[unit, i // 4, (i // 2) % 2, i % 2].reshape(64, 256)
                gathered_hi[rows], gathered_lo[rows] = split(value)
                return carry

            lax.fori_loop(0, 8, cut, 0)

            def tile(i, carry):
                rows = pl.ds(pl.multiple_of(i * 256, 256), 256)
                value = (
                    dot(in_hi[rows], gathered_hi[...])
                    + dot(in_hi[rows], gathered_lo[...])
                    + dot(in_lo[rows], gathered_hi[...])
                )
                work[unit, i] = value.reshape(2, 2, 2, 2, 16, 256)
                square_sum[...] += jnp.sum((value * value).reshape(32, 8, 256), axis=0)
                return carry

            lax.fori_loop(0, 2, tile, 0)

        def do_sm(stage, unused):
            sm_copy(stage).wait()
            before = small[:, core_half(core)] if stage == 0 else small_half[...]
            small_half[...] = before + small_got[stage]
            sm_copy(stage + 1).start()
            if stage >= 4 and stage < 4 + extra:
                do_sm(stage + 1, 0)

        square_sum[...] = jnp.zeros((8, 256), F32)
        sm_copy(0).start()
        run = (do_mm, do_rs, do_post, do_ag, do_fin, do_sm)
        for kind, which, stage in TASKS:
            run[kind](which, stage)

        sm_copy(len(bits)).wait()
        kept, came = small_half[...], small_back[...]
        low_half, high_half = jnp.where(core == 0, kept, came), jnp.where(core == 0, came, kept)
        block = jnp.concatenate([low_half, high_half], axis=1)
        head_part = jnp.where(row16w <= NCLS, block, 0.0)
        squared = (
            jnp.sum(jnp.sum(square_sum[...], axis=0, keepdims=True), axis=1, keepdims=True)
            + jnp.sum(norm_grads[0] * norm_grads[0] + norm_grads[1] * norm_grads[1], axis=1, keepdims=True)
            + jnp.sum(jnp.sum(head_part * head_part, axis=0, keepdims=True), axis=1, keepdims=True)
        )
        norm = jnp.sqrt(squared)
        factor = jnp.minimum(1.0, CLIP / (norm + 1e-06))
        facts[0:16] = block
        facts[16:24] = stack_rows(norm_grads + [block[NCLS + 1 : NCLS + 2], live_total, norm, factor])
        for copy in moments:
            copy.wait()

    square = (512, 512)
    pl.run_scoped(
        prepare,
        pltpu.VMEM((3, 10 * stride, 512), BF16),
        pltpu.VMEM((3, 1024, 512), BF16),
        pltpu.VMEM((2, 3, 512, 512), BF16),
        pltpu.VMEM((8, stride, 512), F32),
        pltpu.VMEM((8, stride, 512), F32),
        pltpu.VMEM((count_img, 8, 8, 512), BF16),
        *[pltpu.VMEM(square, BF16)] * 4,
        pltpu.VMEM((1024, 512), BF16),
    )
    pl.run_scoped(
        exchange,
        pltpu.VMEM((20, 2, 2, 2, 2, 16, 256), F32),
        pltpu.VMEM((AWAY, 2, 2, 2, 2, 16, 256), F32),
        pltpu.VMEM((512, 256), BF16),
        pltpu.VMEM((512, 256), BF16),
    )


def adamw(weight, grad, first, second, rate):
    first = 0.9 * first + 0.1 * grad
    second = 0.999 * second + 0.001 * grad * grad
    step_size = first / (1.0 - 0.9**STEP) / (jnp.sqrt(second / (1.0 - 0.999**STEP)) + 1e-08)
    return (weight - rate * (step_size + 0.01 * weight), first, second)


def adamw_positive(weight, grad, first, second, rate):
    first = 0.9 * first + 0.1 * grad
    second = 0.999 * second + 0.001 * grad * grad
    scaled = second * (1.0 / (1.0 - 0.999**STEP))
    root = scaled * lax.rsqrt(scaled) + 1e-08
    step = first * (rate / (1.0 - 0.9**STEP)) / root
    return (weight * (1.0 - 0.01 * rate) - step, first, second)


CHUNKS = 36
RING = 8


def update_kernel(
    facts,
    gain,
    shift,
    norm_first,
    norm_second,
    head,
    head_first,
    head_second,
    gradients,
    moments,
    loss_parts,
    grad_norm,
    norm_new,
    norm_m,
    norm_v,
    head_new,
    head_m,
    head_v,
    conv_new,
    conv_m,
    conv_v,
    scales_new,
    out_new,
    out_m,
    out_v,
    out_sem,
    scale_sem,
):
    tall = TAPS * 512 // CHUNKS
    outs = ((out_new, conv_new), (out_m, conv_m), (out_v, conv_v))

    def store(k, i):
        rows = pl.ds(pl.multiple_of(i * tall, tall), tall)
        return pltpu.make_async_copy(outs[k][0].at[i % RING], outs[k][1].at[rows], out_sem.at[k, i % RING])

    factor = facts[21:22, 0:1]

    def chunk(i, carry):
        @pl.when(i >= RING)
        def _():
            for k in range(3):
                store(k, i).wait()

        rows = pl.ds(pl.multiple_of(i * tall, tall), tall)
        more = pl.ds(pl.multiple_of(TAPS * 512 + i * tall, tall), tall)
        for half in range(2):
            cols = slice(256 * half, 256 * half + 256)
            where = (2 * (i // 4) + half, (i // 2) % 2, i % 2)
            grad = gradients[where].reshape(tall, 256)
            weight = gradients[(WEIGHT + where[0],) + where[1:]].reshape(tall, 256)
            out_new[i % RING, :, cols], out_m[i % RING, :, cols], out_v[i % RING, :, cols] = adamw_positive(
                weight, factor * grad, moments[rows, cols].astype(F32), moments[more, cols].astype(F32), 0.02
            )
        for k in range(3):
            store(k, i).start()
        return carry

    lax.fori_loop(0, CHUNKS, chunk, 0)
    scale_copies = [
        pltpu.make_async_copy(
            gradients.at[2 * STAT + k], scales_new.at[:, :, :, :, :, :, 256 * k : 256 * k + 256], scale_sem.at[k]
        )
        for k in range(2)
    ]
    for copy in scale_copies:
        copy.start()

    loss_parts[0] = facts[18, 0]
    loss_parts[1] = facts[19, 0]
    grad_norm[0] = facts[20, 0]
    grads = factor * facts[16:18, :]
    weights = jnp.concatenate([gain[...], shift[...]], axis=0)
    norm_new[...], norm_m[...], norm_v[...] = adamw(weights, grads, norm_first[...], norm_second[...], 0.1)
    block = factor * facts[0:16, :]
    head_new[:, 0:512], head_m[:, 0:512], head_v[:, 0:512] = adamw(
        head[:, 0:512], block[0:NCLS], head_first[:, 0:512], head_second[:, 0:512], 0.05
    )
    bias = jnp.concatenate([block[0:16, 0:128], jnp.zeros((112, 128), F32)], axis=0).T[0:NCLS, NCLS : NCLS + 1]
    head_new[:, 512:513], head_m[:, 512:513], head_v[:, 512:513] = adamw(
        head[:, 512:513], bias, head_first[:, 512:513], head_second[:, 512:513], 0.05
    )
    for i in range(CHUNKS - RING, CHUNKS):
        for k in range(3):
            store(k, i).wait()
    for copy in scale_copies:
        copy.wait()


def shards(
    sizes,
    images,
    micro_ids,
    labels,
    conv_weight,
    conv_first,
    conv_second,
    eig_scales,
    basis_in,
    basis_out,
    batchnorm_gain,
    batchnorm_shift,
    norm_first,
    norm_second,
    head,
    head_first,
    head_second,
):
    dp_count, rep_count = sizes
    count_img = images.shape[0]
    chips = dp_count * rep_count // 2
    bit_count = (dp_count * rep_count - 1).bit_length()
    extra = bit_count - 5
    vmem = pl.BlockSpec(memory_space=pltpu.VMEM)
    smem = pl.BlockSpec(memory_space=pltpu.SMEM)
    hbm = pl.BlockSpec(memory_space=pltpu.HBM)
    gain = batchnorm_gain.reshape(1, 512)
    shift = batchnorm_shift.reshape(1, 512)
    pixels = 8 * count_img
    square = (512, 512)
    dma = pltpu.SemaphoreType.DMA
    scratch = [
        pltpu.SMEM((count_img,), jnp.int32),
        pltpu.SMEM((count_img,), jnp.int32),
        pltpu.VMEM((1, 512), F32),
        pltpu.VMEM((1, 512), F32),
        pltpu.VMEM((NCLS, 513), F32),
        pltpu.VMEM((GOT_COUNT[0], 2, 2, 2, 2, 16, 256), F32),
        pltpu.VMEM((GOT_COUNT[1], 2, 2, 2, 16, 256), F32),
        pltpu.VMEM((GOT_COUNT[2], 2, 2, 16, 256), F32),
        pltpu.VMEM((GOT_COUNT[3], 2, 16, 256), F32),
        pltpu.VMEM((GOT_COUNT[4], 16, 256), F32),
        pltpu.VMEM((20, extra, 16, 256) if extra else (1, 1, 8, 128), F32),
        pltpu.VMEM((16, 512), F32),
        pltpu.VMEM((16, 256), F32),
        pltpu.VMEM((16, 256), F32),
        pltpu.VMEM((bit_count, 16, 256), F32),
        pltpu.VMEM((2, 8, 512), F32),
        pltpu.VMEM((2, 8, 256), F32),
        pltpu.VMEM((2, chips, 8, 256), F32),
        pltpu.VMEM((2, 2, 8, 256), F32),
        pltpu.VMEM((3, 512, 1280), BF16),
        pltpu.VMEM((512, 1024), BF16),
        pltpu.VMEM((512, 1024), BF16),
        *[pltpu.VMEM((1024, 512), BF16)] * 3,
        pltpu.VMEM((16, 512), F32),
        *[pltpu.VMEM(square, BF16)] * 4,
        pltpu.VMEM((5, 8, 512), F32),
        *[pltpu.VMEM((16, 512), F32)] * 4,
        pltpu.VMEM((128, 640), F32),
        pltpu.VMEM((16, 512), F32),
        pltpu.VMEM((8, 256), F32),
        dma((3,)),
        dma((11,)),
        dma((SEND_COUNT,)),
        dma((RECV_COUNT,)),
        dma((2, 20, extra) if extra else (1, 1, 1)),
        dma((bit_count + 1,)),
        dma((bit_count + 1,)),
        dma((4,)),
        dma((4,)),
        dma((2,)),
        dma((2,)),
    ]
    turned_basis = [x.reshape(2, 2, 2, 2, 2, 16, 512) for x in (basis_in, basis_out)]
    gradients, facts, moments = pl.pallas_call(
        functools.partial(main_kernel, (dp_count, rep_count, count_img)),
        out_shape=(
            pltpu.VMEM((WEIGHT + 2 * TAPS, 2, 2, 2, 2, 2, 16, 256), F32),
            pltpu.VMEM((24, 512), F32),
            pltpu.VMEM((2 * TAPS * 512, 512), BF16),
        ),
        in_specs=[hbm] * 12,
        out_specs=(vmem,) * 3,
        scratch_shapes=scratch,
        compiler_params=pltpu.CompilerParams(
            collective_id=0, has_side_effects=True, vmem_limit_bytes=71 * 2**19
        ),
        name="reduce_and_precondition",
    )(
        micro_ids,
        labels,
        images,
        gain,
        shift,
        head.T,
        conv_weight.reshape(TAPS, 2, 2, 2, 2, 2, 16, 512),
        conv_first,
        conv_second,
        eig_scales,
        *turned_basis,
    )
    tall = TAPS * 512 // CHUNKS
    head_shape = (NCLS, 513)
    outs = pl.pallas_call(
        update_kernel,
        out_shape=(
            jax.ShapeDtypeStruct((2,), F32),
            jax.ShapeDtypeStruct((1,), F32),
            *[jax.ShapeDtypeStruct((2, 512), F32)] * 3,
            *[jax.ShapeDtypeStruct(head_shape, F32)] * 3,
            *[jax.ShapeDtypeStruct((TAPS * 512, 512), F32)] * 3,
            jax.ShapeDtypeStruct((2, 2, 2, 2, 2, 16, 512), F32),
        ),
        in_specs=[vmem] * 10,
        out_specs=(smem, smem) + (vmem,) * 6 + (hbm,) * 4,
        scratch_shapes=[
            *[pltpu.VMEM((RING, tall, 512), F32)] * 3,
            dma((3, RING)),
            dma((2,)),
        ],
        compiler_params=pltpu.CompilerParams(vmem_limit_bytes=27 * 2**18),
        name="adamw",
    )(
        facts,
        gain,
        shift,
        norm_first,
        norm_second,
        head.T,
        head_first.T,
        head_second.T,
        gradients,
        moments,
    )
    loss_parts, grad_norm, norm_new, norm_m, norm_v, head_new, head_m, head_v, conv_new, conv_m, conv_v, scales_new = outs
    return (
        loss_parts,
        grad_norm.reshape(()),
        conv_new,
        conv_m,
        conv_v,
        scales_new.reshape(square),
        norm_new,
        norm_m,
        norm_v,
        head_new.T,
        head_m.T,
        head_v.T,
    )


def solution(mesh):
    split_images = P(("dp", "rep"))
    in_specs = (P(("dp", "rep"), None, None, None), split_images, split_images) + (P(),) * 13
    sizes = (mesh.shape["dp"], mesh.shape["rep"])
    return jax.shard_map(
        functools.partial(shards, sizes), mesh=mesh, in_specs=in_specs, out_specs=(P(),) * 12, check_vma=False
    )
```

```python
import functools

import jax
import jax.numpy as jnp
from jax import lax
from jax.experimental import pallas as pl
from jax.experimental.pallas import tpu as pltpu
from jax.sharding import PartitionSpec as P

NCLS = 10
STEP = 5
NORM_EPS = 1e-05
DAMPING = 0.001
CLIP = 0.01
MESH = pl.DeviceIdType.MESH
F32 = jnp.float32
BF16 = jnp.bfloat16
HIGHEST = lax.Precision.HIGHEST
TAPS = 9
STAT = 9
WEIGHT = 20
AWAY = 4
UNITS = (1, 7, 16, 8, 9, 19, 3, 18, 2, 12, 4, 11, 5, 14, 6, 10, 13, 17, 0, 15)
RS_ORDER = (
    (1, 2, 3, 4), (3, 1, 2, 4), (1, 2, 3, 4), (2, 1, 3, 4), (2, 1, 3, 4),
    (3, 2, 4, 1), (2, 3, 4, 1), (1, 3, 2, 4), (1, 3, 2, 4), (3, 2, 1, 4),
    (1, 3, 2, 4), (1, 3, 4, 2), (3, 2, 1, 4), (2, 1, 3, 4), (1, 2, 3, 4),
    (2, 1, 3, 4), (2, 3, 4, 1), (1, 2, 3, 4), (1, 2, 3, 4), (2, 1, 3, 4),
)
AG_ORDER = (
    (3, 2, 1, 4), (1, 3, 4, 2), (1, 2, 3, 4), (2, 3, 4, 1), (1, 2, 3, 4),
    (1, 3, 4, 2), (2, 1, 3, 4), (1, 2, 3, 4), (1, 2, 3, 4), (1, 2, 3, 4),
    (3, 1, 2, 4), (2, 3, 4, 1), (2, 3, 1, 4), (2, 3, 4, 1), (2, 3, 4, 1),
    (1, 3, 4, 2), (2, 3, 4, 1), (1, 2, 3, 4), (1, 2, 3, 4), (2, 1, 3, 4),
)
TASKS = (
    (0, 1, 0), (0, 7, 0), (0, 16, 0), (5, 0, 0), (1, 1, 0), (0, 8, 0), (1, 7, 0), (1, 16, 0),
    (0, 9, 0), (0, 19, 0), (1, 8, 0), (1, 9, 0), (5, 1, 0), (0, 3, 0), (1, 19, 0), (0, 18, 0),
    (1, 3, 0), (1, 1, 1), (1, 7, 1), (1, 16, 1), (1, 18, 0), (0, 2, 0), (5, 2, 0), (0, 12, 0),
    (0, 4, 0), (1, 9, 1), (1, 2, 0), (1, 8, 1), (1, 12, 0), (0, 11, 0), (1, 19, 1), (1, 7, 2),
    (1, 4, 0), (1, 1, 2), (0, 5, 0), (1, 11, 0), (1, 16, 2), (0, 14, 0), (5, 3, 0), (0, 6, 0),
    (1, 3, 1), (1, 5, 0), (1, 18, 1), (1, 14, 0), (1, 8, 2), (0, 10, 0), (1, 6, 0), (1, 9, 2),
    (0, 13, 0), (1, 7, 3), (0, 17, 0), (1, 10, 0), (1, 2, 1), (0, 0, 0), (1, 12, 1), (1, 13, 0),
    (1, 17, 0), (1, 19, 2), (1, 4, 1), (1, 16, 3), (1, 0, 0), (0, 15, 0), (1, 1, 3), (5, 4, 0),
    (1, 18, 2), (1, 15, 0), (1, 11, 1), (1, 8, 3), (1, 5, 1), (1, 3, 2), (1, 19, 3), (1, 7, 4),
    (1, 18, 3), (1, 1, 4), (1, 6, 1), (1, 11, 2), (1, 14, 1), (1, 2, 2), (1, 9, 3), (1, 3, 3),
    (1, 8, 4), (1, 12, 2), (1, 19, 4), (1, 18, 4), (2, 9, 0), (1, 6, 2), (1, 10, 1), (1, 2, 3),
    (1, 11, 3), (1, 13, 1), (1, 9, 4), (2, 4, 0), (1, 3, 4), (3, 18, 0), (1, 17, 1), (3, 19, 0),
    (1, 15, 1), (1, 4, 2), (1, 10, 2), (1, 16, 4), (1, 6, 3), (1, 5, 2), (1, 2, 4), (2, 1, 0),
    (3, 18, 1), (3, 8, 0), (1, 14, 2), (3, 19, 1), (3, 9, 0), (1, 11, 4), (1, 0, 1), (1, 4, 3),
    (1, 12, 3), (1, 17, 2), (1, 10, 3), (3, 8, 1), (1, 13, 2), (1, 5, 3), (1, 14, 3), (3, 2, 0),
    (3, 18, 2), (3, 9, 1), (1, 15, 2), (1, 6, 4), (2, 3, 0), (3, 3, 0), (1, 4, 4), (1, 0, 2),
    (1, 17, 3), (1, 12, 4), (3, 19, 2), (1, 13, 3), (1, 10, 4), (1, 5, 4), (3, 8, 2), (2, 5, 0),
    (2, 2, 0), (3, 2, 1), (1, 14, 4), (3, 9, 2), (1, 15, 3), (3, 6, 0), (3, 18, 3), (3, 7, 0),
    (1, 0, 3), (3, 3, 1), (3, 18, 4), (4, 18, 0), (3, 19, 3), (1, 17, 4), (2, 8, 0), (3, 5, 0),
    (1, 13, 4), (2, 6, 0), (3, 8, 3), (3, 11, 0), (3, 10, 0), (3, 19, 4), (3, 6, 1), (3, 2, 2),
    (4, 19, 0), (3, 4, 0), (3, 7, 1), (3, 8, 4), (4, 8, 0), (1, 0, 4), (1, 15, 4), (3, 3, 2),
    (2, 0, 0), (3, 9, 3), (3, 10, 1), (3, 16, 0), (2, 7, 0), (3, 13, 0), (3, 17, 0), (3, 5, 1),
    (3, 7, 2), (3, 9, 4), (4, 9, 0), (3, 12, 0), (3, 6, 2), (3, 4, 1), (3, 11, 1), (3, 0, 0),
    (3, 3, 3), (3, 2, 3), (3, 17, 1), (3, 1, 0), (3, 15, 0), (3, 16, 1), (3, 10, 2), (3, 3, 4),
    (3, 5, 2), (4, 3, 0), (3, 13, 1), (3, 14, 0), (3, 11, 2), (3, 2, 4), (4, 2, 0), (3, 6, 3),
    (3, 7, 3), (3, 1, 1), (3, 4, 2), (3, 12, 1), (3, 16, 2), (3, 6, 4), (4, 6, 0), (3, 17, 2),
    (3, 0, 1), (3, 7, 4), (3, 15, 1), (4, 7, 0), (3, 10, 3), (3, 5, 3), (3, 11, 3), (3, 13, 2),
    (3, 10, 4), (4, 10, 0), (3, 11, 4), (3, 5, 4), (4, 11, 0), (3, 16, 3), (3, 14, 1), (3, 4, 3),
    (3, 1, 2), (4, 5, 0), (3, 12, 2), (3, 16, 4), (3, 0, 2), (4, 16, 0), (3, 17, 3), (3, 15, 2),
    (3, 4, 4), (4, 4, 0), (3, 13, 3), (3, 14, 2), (3, 17, 4), (4, 17, 0), (3, 1, 3), (3, 13, 4),
    (4, 13, 0), (3, 12, 3), (3, 0, 3), (3, 1, 4), (4, 1, 0), (3, 15, 3), (3, 12, 4), (4, 12, 0),
    (3, 0, 4), (3, 14, 3), (4, 0, 0), (3, 15, 4), (4, 15, 0), (3, 14, 4), (4, 14, 0),
)
GOT_COUNT = (6, 14, 14, 10, 10)
RECV_COUNT, SEND_COUNT = 54, 20
RS_SLOT = (
    (1, 5, 0, 6, 7), (0, 0, 1, 2, 1), (2, 8, 0, 0, 0), (0, 6, 7, 7, 6), (4, 10, 10, 3, 1),
    (1, 1, 3, 4, 4), (3, 11, 1, 2, 9), (1, 1, 0, 0, 0), (3, 4, 3, 3, 2), (4, 3, 4, 6, 5),
    (0, 12, 2, 9, 3), (0, 0, 8, 1, 8), (3, 9, 9, 8, 2), (4, 3, 12, 2, 6), (2, 2, 11, 0, 5),
    (0, 4, 13, 5, 8), (2, 2, 2, 1, 7), (5, 13, 4, 1, 0), (1, 7, 6, 5, 4), (5, 5, 5, 4, 3),
)
AG_RECV = (
    (10, 35, 10, 7, 4), (30, 6, 23, 5, 0), (6, 2, 17, 29, 2), (12, 16, 12, 28, 1), (18, 9, 7, 22, 4),
    (0, 23, 16, 18, 3), (10, 6, 26, 5, 0), (15, 7, 13, 33, 9), (3, 0, 8, 4, 2), (5, 1, 9, 19, 0),
    (11, 8, 31, 17, 1), (5, 27, 4, 19, 2), (24, 34, 24, 6, 3), (22, 32, 20, 15, 2), (25, 21, 16, 9, 2),
    (3, 12, 14, 8, 1), (21, 15, 8, 13, 0), (20, 14, 11, 36, 1), (0, 2, 7, 14, 25), (1, 4, 13, 3, 1),
)
RS_SEND = (
    (18, 18, 7, 7, 7), (0, 0, 0, 0, 0), (8, 8, 8, 8, 8), (6, 6, 6, 6, 6), (10, 10, 10, 10, 10),
    (12, 12, 12, 2, 2), (14, 14, 0, 0, 0), (1, 1, 1, 1, 1), (3, 3, 3, 3, 3), (4, 4, 4, 4, 4),
    (15, 15, 9, 9, 9), (11, 11, 11, 7, 7), (9, 9, 9, 3, 3), (16, 16, 13, 13, 5), (13, 13, 11, 11, 11),
    (19, 19, 15, 15, 14), (2, 2, 2, 2, 2), (17, 17, 6, 6, 6), (7, 7, 7, 7, 1), (5, 5, 5, 5, 5),
)
AG_SEND = (
    (7, 7, 6, 2, 2), (12, 11, 10, 7, 0), (8, 8, 8, 1, 1), (12, 12, 12, 2, 2), (10, 8, 8, 8, 4),
    (13, 13, 13, 2, 2), (0, 0, 0, 0, 0), (16, 15, 10, 10, 1), (4, 4, 4, 2, 2), (14, 14, 14, 11, 11),
    (4, 4, 4, 4, 4), (9, 9, 9, 9, 7), (5, 5, 5, 5, 4), (16, 16, 13, 9, 4), (14, 14, 3, 3, 1),
    (15, 12, 1, 1, 0), (3, 3, 3, 3, 2), (6, 6, 6, 0, 0), (1, 1, 1, 1, 1), (5, 5, 5, 3, 1),
)


def split(value):
    high = value.astype(BF16)
    return high, (value - high.astype(F32)).astype(BF16)


def dot(a, b, dims=((1,), (0,))):
    return lax.dot_general(a, b, (dims, ((), ())), preferred_element_type=F32)


def dot_exact(a, b, dims=((1,), (0,))):
    return lax.dot_general(a, b, (dims, ((), ())), precision=HIGHEST, preferred_element_type=F32)


def main_kernel(
    sizes,
    micro_hbm,
    labels_hbm,
    images_hbm,
    gain_hbm,
    shift_hbm,
    head_hbm,
    weight,
    first_hbm,
    second_hbm,
    eig_hbm,
    in_hbm,
    out_hbm,
    work,
    facts,
    moments_held,
    micro,
    labels,
    gain_ref,
    shift_ref,
    head,
    got0,
    got1,
    got2,
    got3,
    got4,
    got_more,
    small,
    small_half,
    small_back,
    small_got,
    tile_in,
    tile_core,
    tile_slots,
    tile_out,
    turned_hi,
    box_hi,
    box_lo,
    rot_hi,
    rot2_hi,
    rot2_lo,
    eig,
    in_hi,
    in_lo,
    out_t_hi,
    out_t_lo,
    rows_stat,
    pooled,
    shares,
    shares_x,
    dpool,
    head_pad,
    scale_rows,
    square_sum,
    w_sem,
    load_sem,
    send_sem,
    recv_sem,
    more_sem,
    sm_send,
    sm_recv,
    core_send,
    core_recv,
    chip_send,
    chip_recv,
):
    dp_count, rep_count, count_img = sizes
    area = 64
    cells = 16
    chips = dp_count * rep_count // 2
    dp = lax.axis_index("dp")
    rep = lax.axis_index("rep")
    core = rep % 2
    chip = dp * (rep_count // 2) + rep // 2
    bits = [("rep", 1), ("dp", 1), ("rep", 2), ("dp", 2), ("dp", 4)]
    step = 8
    while step < dp_count:
        bits.append(("dp", step))
        step *= 2
    step = 4
    while step < rep_count:
        bits.append(("rep", step))
        step *= 2
    extra = len(bits) - 5
    stride = count_img * 8
    mine = [((dp if name == "dp" else rep) // weight_of) % 2 for name, weight_of in bits]

    own = dict(enumerate(mine[:5]))
    own_block = (((mine[0] * 2 + mine[1]) * 2 + mine[2]) * 2 + mine[3]) * 2 + mine[4]

    def partner(k):
        name, weight_of = bits[k]
        change = (1 - 2 * mine[k]) * weight_of
        return (dp + change, rep) if name == "dp" else (dp, rep + change)

    def chip_device(q):
        return (q // (rep_count // 2), (q % (rep_count // 2)) * 2 + core)

    def weight_copy(unit):
        cols = pl.ds(pl.multiple_of((unit % 2) * 256, 256), 256)
        return pltpu.make_async_copy(
            weight.at[unit // 2, :, :, :, :, :, :, cols], work.at[WEIGHT + unit], w_sem.at[unit // 6]
        )

    def start_weight(unit, carry):
        weight_copy(unit).start()
        return carry

    loads = [
        pltpu.make_async_copy(src, dst, load_sem.at[k])
        for k, (src, dst) in enumerate(
            (
                (in_hbm.at[:, :, :, :, :, :, 0:256], work.at[4]),
                (in_hbm.at[:, :, :, :, :, :, 256:512], work.at[5]),
                (out_hbm.at[:, :, :, :, :, :, 0:256], work.at[6]),
                (out_hbm.at[:, :, :, :, :, :, 256:512], work.at[7]),
                (eig_hbm.at[pl.ds(pl.multiple_of(own_block * 16, 16), 16)], eig),
            )
        )
    ]

    barrier = pltpu.get_barrier_semaphore()

    def greet(k, carry):
        pl.semaphore_signal(barrier, inc=1, device_id=chip_device((chip + k) % chips), device_id_type=MESH)
        return carry

    lax.fori_loop(1, chips, greet, 0)
    pl.semaphore_signal(barrier, inc=1, device_id=partner(0), device_id_type=MESH)

    row8 = lax.broadcasted_iota(jnp.int32, (8, 512), 0)
    row16w = lax.broadcasted_iota(jnp.int32, (16, 512), 0)
    zero_tile = jnp.zeros((8, 512), F32)

    def stack_rows(rows):
        tile = zero_tile
        for k, row in enumerate(rows):
            tile = jnp.where(row8 == k, jnp.broadcast_to(row, (8, 512)), tile)
        return tile

    def core_half(which):
        return pl.ds(pl.multiple_of(which * 256, 256), 256)

    def prepare(
        narrow, wide, weight_low, conv, share, images, in_t_hi, in_t_lo, out_hi, out_lo, grad_low
    ):
        first_loads = [
            pltpu.make_async_copy(src, dst, load_sem.at[5 + k])
            for k, (src, dst) in enumerate(
                (
                    (images_hbm, images),
                    (micro_hbm, micro),
                    (labels_hbm, labels),
                    (gain_hbm, gain_ref),
                    (shift_hbm, shift_ref),
                    (head_hbm, head),
                )
            )
        ]
        first_loads[0].start()
        first_loads[1].start()
        lax.fori_loop(0, 12, start_weight, 0)
        for copy in first_loads[2:]:
            copy.start()

        column = lax.broadcasted_iota(jnp.int32, (2, 8, 512), 1)
        for k in range(3):
            narrow[k, 0:stride] = jnp.zeros((stride, 512), BF16)
            narrow[k, 9 * stride : 10 * stride] = jnp.zeros((stride, 512), BF16)

        def build(h, carry):
            for pair in range(count_img // 2):
                block = images[2 * pair : 2 * pair + 2, h].astype(F32)
                left = jnp.where(column == 0, 0.0, pltpu.roll(block, 1, 1))
                right = jnp.where(column == 7, 0.0, pltpu.roll(block, 7, 1))
                at = pl.ds(pl.multiple_of((h + 1) * stride + 16 * pair, 16), 16)
                for k, value in enumerate((left, block, right)):
                    narrow[k, at] = value.reshape(16, 512).astype(BF16)
            return carry

        first_loads[0].wait()
        lax.fori_loop(0, 8, build, 0)

        def wait_row(dy):
            held = work.at[pl.ds(WEIGHT + 6 * dy, 6)]
            pltpu.make_async_copy(held, held, w_sem.at[dy]).wait()

        def cast(dy, k):
            dx, j, half = k // 4, (k // 2) % 2, k % 2
            piece = work[WEIGHT + 2 * (3 * dy + dx) + j, half].reshape(256, 256)
            weight_low[dy % 2, dx, 256 * half : 256 * half + 256, 256 * j : 256 * j + 256] = piece.astype(BF16)

        wait_row(0)
        lax.fori_loop(12, 2 * TAPS, start_weight, 0)
        for k in range(12):
            cast(0, k)
        for dy in range(3):
            if dy < 2:
                wait_row(dy + 1)
            if dy == 1:
                for copy in loads:
                    copy.start()
            for m in range(2):
                for n in range(2):
                    total = None
                    for dx in range(3):
                        begin = (dy + 4 * m) * stride
                        term = dot(
                            narrow[dx, begin : begin + 4 * stride], weight_low[dy % 2, dx, :, n * 256 : n * 256 + 256]
                        )
                        total = term if total is None else total + term
                        if dy < 2:
                            cast(dy + 1, 6 * m + 3 * n + dx)
                    at = (slice(4 * m, 4 * m + 4), slice(None), slice(n * 256, n * 256 + 256))
                    total = total.reshape(4, stride, 256)
                    conv[at] = total if dy == 0 else conv[at] + total

        for copy in first_loads[1:]:
            copy.wait()
        def member(n):
            return [jnp.where(micro[n] == m, 1.0, 0.0).astype(F32) for m in range(3)]

        def gather_sums(n, carry):
            at = pl.ds(pl.multiple_of(n * 8, 8), 8)
            first = jnp.zeros((8, 512), F32)
            second = jnp.zeros((8, 512), F32)
            for h in range(8):
                value = conv[h, at]
                first = first + value
                second = second + value * value
            kinds = member(n)
            return tuple(c + k * first for c, k in zip(carry[:3], kinds)) + tuple(
                c + k * second for c, k in zip(carry[3:6], kinds)
            )

        sums = lax.fori_loop(0, count_img, gather_sums, (zero_tile,) * 6)
        counts = [jnp.zeros((), F32)] * 3
        for n in range(count_img):
            counts = [c + k for c, k in zip(counts, member(n))]
        lane8 = lax.broadcasted_iota(jnp.int32, (8, 512), 1)

        count_row = zero_tile
        for m in range(3):
            count_row = jnp.where(lane8 % 256 == m, counts[m], count_row)
        tile_in[0] = jnp.where(row8 == 6, count_row, stack_rows([jnp.sum(s, axis=0, keepdims=True) for s in sums]))

        def tile_copy(i):
            return pltpu.make_async_remote_copy(
                src_ref=tile_in.at[i, :, core_half(1 - core)],
                dst_ref=tile_core.at[i],
                send_sem=core_send.at[2 * i],
                recv_sem=core_recv.at[2 * i],
                device_id=partner(0),
                device_id_type=MESH,
            )

        def tile_start(i):
            tile_copy(i).start()
            tile_copy(i).wait()
            tile_slots[i, 0] = tile_in[i, :, core_half(core)] + tile_core[i]

            def give(k, carry):
                pltpu.make_async_remote_copy(
                    src_ref=tile_slots.at[i, 0],
                    dst_ref=tile_slots.at[i, k],
                    send_sem=chip_send.at[i],
                    recv_sem=chip_recv.at[i],
                    device_id=chip_device((chip + k) % chips),
                    device_id_type=MESH,
                ).start()
                return carry

            lax.fori_loop(1, chips, give, 0)

        def tile_end(i):
            others = tile_slots.at[i, pl.ds(1, chips - 1)]
            pltpu.make_async_remote_copy(
                src_ref=others,
                dst_ref=others,
                send_sem=chip_send.at[i],
                recv_sem=chip_recv.at[i],
                device_id=partner(0),
                device_id_type=MESH,
            ).wait()

            def add(k, total):
                return total + tile_slots[i, (chip - k + chips) % chips]

            tile_out[i, core] = lax.fori_loop(0, chips, add, jnp.zeros((8, 256), F32))
            back = pltpu.make_async_remote_copy(
                src_ref=tile_out.at[i, core],
                dst_ref=tile_out.at[i, core],
                send_sem=core_send.at[2 * i + 1],
                recv_sem=core_recv.at[2 * i + 1],
                device_id=partner(0),
                device_id_type=MESH,
            )
            back.start()
            back.wait()
            return jnp.concatenate([tile_out[i, 0], tile_out[i, 1]], axis=1)

        pl.semaphore_wait(barrier, chips)
        tile_start(0)

        def widen(h, carry):
            source = pl.ds(pl.multiple_of((h + 1) * stride, 16), stride)
            target = pl.ds(pl.multiple_of(h * 128, 128), stride)
            fill = pl.ds(pl.multiple_of(h * 128 + stride, 16), 128 - stride)
            for k in range(3):
                wide[k, target] = narrow[k, source]
                wide[k, fill] = jnp.zeros((128 - stride, 512), BF16)
            grad_low[fill] = jnp.zeros((128 - stride, 512), BF16)
            return carry

        lax.fori_loop(0, 8, widen, 0)
        for copy in loads:
            copy.wait()
        value = jnp.concatenate([work[4].reshape(512, 256), work[5].reshape(512, 256)], axis=1)
        in_hi[...], in_lo[...] = split(value)
        in_t_hi[...], in_t_lo[...] = split(value.T)
        for dx in range(3):
            turned_hi[dx, :, 0:128] = jnp.zeros((512, 128), BF16)
            turned_hi[dx, :, 1152:1280] = jnp.zeros((512, 128), BF16)

        def turn(j, carry):
            total = None
            for dx in range(3):
                rows = wide[dx, pl.ds(pl.multiple_of(256 * j, 256), 256)]
                value = dot(in_t_hi[...], rows, ((1,), (1,))) + dot(in_t_lo[...], rows, ((1,), (1,)))
                at = pl.ds(pl.multiple_of(128 + 256 * j, 128), 256)
                turned_hi[dx, :, at] = value.astype(BF16)
                total = value * value if total is None else total + value * value
            work[j] = total.reshape(2, 2, 2, 2, 2, 16, 256)
            return carry

        lax.fori_loop(0, 2, turn, 0)

        head_pad[...] = jnp.zeros((128, 640), F32)
        head_pad[0:NCLS, 0:513] = head[...]
        head_rows = head_pad[:, 0:512].astype(BF16)
        row16 = lax.broadcasted_iota(jnp.int32, (16, 128), 0)
        lane16 = lax.broadcasted_iota(jnp.int32, (16, 128), 1)
        label_of = jnp.zeros((16, 128), jnp.int32)
        micro_of = jnp.full((16, 128), 3, jnp.int32)
        for n in range(count_img):
            label_of = jnp.where(row16 == n, labels[n], label_of)
            micro_of = jnp.where(row16 == n, micro[n], micro_of)
        is_class = lane16 < NCLS
        live = jnp.where(micro_of < 3, 1.0, 0.0)
        onehot = jnp.where(lane16 == label_of, 1.0, 0.0)
        totals = tile_end(0)

        gain = gain_ref[...]
        shift = shift_ref[...]
        live_total = totals[6:7, 0:1] + totals[6:7, 1:2] + totals[6:7, 2:3]
        pixels = [totals[6:7, m : m + 1] * float(area) for m in range(3)]
        mean_rows, rstd_rows = [], []
        for m in range(3):
            mean = totals[m : m + 1] / pixels[m]
            var = totals[3 + m : 4 + m] / pixels[m] - mean * mean
            mean_rows.append(mean)
            rstd_rows.append(lax.rsqrt(var + NORM_EPS))
        rows_stat[0] = stack_rows(mean_rows)
        rows_stat[1] = stack_rows(rstd_rows)

        def image_rows(n, k):
            kinds = member(n)
            row = sum(kinds[m] * rows_stat[k, m : m + 1] for m in range(3))
            return row, 1.0 - (kinds[0] + kinds[1] + kinds[2])

        even = lax.broadcasted_iota(jnp.int32, (8, 512), 0) % 2 == 0
        pooled[...] = jnp.zeros((16, 512), F32)
        shares[...] = jnp.zeros((16, 512), F32)
        shares_x[...] = jnp.zeros((16, 512), F32)

        def forward(n, carry):
            mean, dead = image_rows(n, 0)
            rstd, _ = image_rows(n, 1)
            rstd = rstd + dead
            at = pl.ds(pl.multiple_of(n * 8, 8), 8)
            cell_sum, share_sum, share_x_sum = zero_tile, zero_tile, zero_tile
            for a in range(4):
                xs = [(conv[2 * a + k, at] - mean) * rstd for k in range(2)]
                exps = [jnp.exp(gain * x + shift) for x in xs]
                both = exps[0] + exps[1]
                both = both + jnp.where(even, pltpu.roll(both, 7, 0), pltpu.roll(both, 1, 0))
                both = both + 4.0
                cell_sum = cell_sum + jnp.log(both)
                inverse = 1.0 / both
                for k in range(2):
                    part = exps[k] * inverse
                    share[2 * a + k, at] = part
                    share_sum = share_sum + part
                    share_x_sum = share_x_sum + part * xs[k]
            row = pl.ds(n, 1)
            pooled[row] = jnp.sum(cell_sum, axis=0, keepdims=True) * (0.5 / cells)
            shares[row] = jnp.sum(share_sum, axis=0, keepdims=True)
            shares_x[row] = jnp.sum(share_x_sum, axis=0, keepdims=True)
            return carry

        lax.fori_loop(0, count_img, forward, 0)

        pooled_low = pooled[...].astype(BF16)
        logits = dot(pooled_low, head_rows, ((1,), (1,))) + head_pad[:, 512:640].T[0:1, :]
        top = jnp.max(jnp.where(is_class, logits, -3e38), axis=1, keepdims=True)
        shifted = jnp.where(is_class, logits - top, 0.0)
        log_sum = jnp.log(jnp.sum(jnp.where(is_class, jnp.exp(shifted), 0.0), axis=1, keepdims=True))
        logp = jnp.where(is_class, shifted - log_sum, 0.0)
        per_img = -(
            0.9 * jnp.sum(onehot * logp, axis=1, keepdims=True) + 0.1 / NCLS * jnp.sum(logp, axis=1, keepdims=True)
        )
        loss = jnp.sum(live[:, 0:1] * per_img, axis=0, keepdims=True)
        dlogits = jnp.where(is_class, jnp.exp(logp) - 0.9 * onehot - 0.1 / NCLS, 0.0) * (live / live_total)
        dpool[...] = dot_exact(dlogits, head_rows.astype(F32)) * (1.0 / cells)
        back_rows = []
        for which in (shares, shares_x):
            for m in range(3):
                inside = jnp.where(micro_of[:, 0:1] == m, 1.0, 0.0)
                back_rows.append(jnp.sum(inside * (dpool[...] * which[...]), axis=0, keepdims=True))
        tile_in[1] = stack_rows(back_rows)
        tile_start(1)

        head_grad = dot_exact(dlogits, pooled_low.astype(F32), ((0,), (0,)))
        bias_grad = jnp.concatenate(
            [jnp.sum(dlogits, axis=0, keepdims=True), jnp.zeros((1, 384), F32)], axis=1
        )
        block = jnp.where(row16w < NCLS, head_grad[0:16], 0.0)
        block = jnp.where(row16w == NCLS, bias_grad, block)
        small[...] = jnp.where(row16w == NCLS + 1, loss, block)

        def scale(n, carry):
            mean, dead = image_rows(n, 0)
            rstd, _ = image_rows(n, 1)
            rstd = rstd + dead
            factor = rstd * gain * dpool[pl.ds(n, 1)]
            at = pl.ds(pl.multiple_of(n * 8, 8), 8)
            for h in range(8):
                share[h, at] = factor * share[h, at]
                conv[h, at] = (conv[h, at] - mean) * rstd * rstd
            return carry

        lax.fori_loop(0, count_img, scale, 0)

        lax.fori_loop(2, 4, turn, 0)
        def squares(h):
            return work[h // 2, :, :, :, :, :, :, (h % 2) * 128 : (h % 2) * 128 + 128].reshape(512, 128)

        for h in range(8):
            value = squares(h)
            if h > 0:
                value = value + squares(h - 1)
            if h < 7:
                value = value + squares(h + 1)
            box_hi[:, h * 128 : h * 128 + 128], box_lo[:, h * 128 : h * 128 + 128] = split(value)

        value = jnp.concatenate([work[6].reshape(512, 256), work[7].reshape(512, 256)], axis=1)
        out_hi[...], out_lo[...] = split(value)
        out_t_hi[...], out_t_lo[...] = split(value.T)
        totals = tile_end(1)
        norm_grads = [
            totals[3:4] + totals[4:5] + totals[5:6],
            totals[0:1] + totals[1:2] + totals[2:3],
        ]
        rows_stat[4] = stack_rows(norm_grads + [jnp.broadcast_to(live_total, (1, 512))])
        rows_stat[2] = stack_rows([gain * totals[m : m + 1] / pixels[m] for m in range(3)])
        rows_stat[3] = stack_rows([gain * totals[3 + m : 4 + m] / pixels[m] for m in range(3)])

        def backward(pair, carry):
            parts = []
            for k in range(2):
                n = 2 * pair + k
                rstd, dead = image_rows(n, 1)
                offset, _ = image_rows(n, 2)
                slope, _ = image_rows(n, 3)
                parts.append(((rstd + dead) * offset, slope, pl.ds(pl.multiple_of(n * 8, 8), 8)))
            for h in range(8):
                values = [share[h, at] - offset - conv[h, at] * slope for offset, slope, at in parts]
                rows = pl.ds(pl.multiple_of(h * 128 + 16 * pair, 16), 16)
                grad_low[rows] = jnp.concatenate(values, axis=0).astype(BF16)
            return carry

        lax.fori_loop(0, count_img // 2, backward, 0)

        def rotate(k, carry):
            rows = pl.ds(pl.multiple_of(k * 256, 256), 256)
            value = dot(grad_low[rows], out_hi[...]) + dot(grad_low[rows], out_lo[...])
            rot_hi[rows] = value.astype(BF16)
            rot2_hi[rows], rot2_lo[rows] = split(value * value)
            return carry

        lax.fori_loop(0, 4, rotate, 0)

    def exchange(half_sum, away, gathered_hi, gathered_lo):
        got = (got0, got1, got2, got3, got4)
        left_home = set()
        live_total = rows_stat[4, 2:3, 0:1]
        norm_grads = [rows_stat[4, 0:1], rows_stat[4, 1:2]]
        moments = [
            pltpu.make_async_copy(src, moments_held.at[pl.ds(k * TAPS * 512, TAPS * 512)], load_sem.at[k])
            for k, src in enumerate((first_hbm, second_hbm))
        ]
        for copy in moments:
            copy.start()

        def region(unit, fixed, first=1):
            return (unit,) + tuple(fixed.get(k, slice(None)) for k in range(first, 5))

        def rs_copy(unit, stage):
            if stage < 5:
                order = (0,) + RS_ORDER[unit]
                fixed = {k: mine[k] for k in order[:stage]}
                fixed[order[stage]] = 1 - mine[order[stage]]
                target, to = got[stage].at[RS_SLOT[unit][stage]], partner(order[stage])
                sems = (send_sem.at[RS_SEND[unit][stage]], recv_sem.at[sum(GOT_COUNT[:stage]) + RS_SLOT[unit][stage]])
            else:
                fixed = dict(enumerate(mine[:5]))
                target, to = got_more.at[unit, stage - 5], partner(stage)
                sems = (more_sem.at[0, unit, stage - 5], more_sem.at[1, unit, stage - 5])
            source = half_sum.at[region(unit, fixed)] if stage else away.at[UNITS.index(unit) % AWAY]
            return pltpu.make_async_remote_copy(
                src_ref=source,
                dst_ref=target,
                send_sem=sems[0],
                recv_sem=sems[1],
                device_id=to,
                device_id_type=MESH,
            )

        def ag_copy(unit, stage):
            order = (0,) + AG_ORDER[unit]
            where = work.at[region(unit, {k: mine[k] for k in order[: 5 - stage]}, 0)]
            return pltpu.make_async_remote_copy(
                src_ref=where,
                dst_ref=where,
                send_sem=send_sem.at[AG_SEND[unit][stage]],
                recv_sem=recv_sem.at[AG_RECV[unit][stage]],
                device_id=partner(order[4 - stage]),
                device_id_type=MESH,
            )

        def sm_copy(stage):
            if stage == 0:
                source, target, to = small.at[:, core_half(1 - core)], small_got.at[0], partner(0)
            elif stage < len(bits):
                source, target, to = small_half, small_got.at[stage], partner(stage)
            else:
                source, target, to = small_half, small_back, partner(0)
            return pltpu.make_async_remote_copy(
                src_ref=source,
                dst_ref=target,
                send_sem=sm_send.at[stage],
                recv_sem=sm_recv.at[stage],
                device_id=to,
                device_id_type=MESH,
            )

        def do_mm(unit, stage):
            tap, cols = unit // 2, slice((unit % 2) * 256, (unit % 2) * 256 + 256)
            dy, dx = tap // 3, tap % 3
            place = UNITS.index(unit)
            if place >= AWAY and UNITS[place - AWAY] not in left_home:
                left_home.add(UNITS[place - AWAY])
                rs_copy(UNITS[place - AWAY], 0).wait_send()
            for stays, half in enumerate((1 - core, core)):
                rows = pl.ds(pl.multiple_of(half * 256, 256), 256)
                if tap == STAT:
                    value = (
                        dot(box_hi[rows], rot2_hi[:, cols])
                        + dot(box_hi[rows], rot2_lo[:, cols])
                        + dot(box_lo[rows], rot2_hi[:, cols])
                    )
                else:
                    value = dot(turned_hi[dx, rows, dy * 128 : dy * 128 + 1024], rot_hi[:, cols])
                value = value.reshape(2, 2, 2, 2, 16, 256)
                if stays:
                    half_sum[unit] = value
                else:
                    away[place % AWAY] = value
                    rs_copy(unit, 0).start()

        def do_rs(unit, stage):
            if stage == 0 and unit in left_home:
                rs_copy(unit, stage).wait_recv()
            else:
                rs_copy(unit, stage).wait()
                if stage == 0:
                    left_home.add(unit)
            if stage < 5:
                fixed = {k: mine[k] for k in ((0,) + RS_ORDER[unit])[: stage + 1]}
                source, at = got[stage], (RS_SLOT[unit][stage],)
            else:
                fixed = dict(enumerate(mine[:5]))
                source, at = got_more, (unit, stage - 5)
            left = [k for k in range(1, 5) if k not in fixed]

            def add(i, carry):
                inner = dict(fixed)
                where = at
                if len(left) >= 3:
                    inner[left[0]], inner[left[1]] = i // 2, i % 2
                    where = at + (i // 2, i % 2)
                half_sum[region(unit, inner)] += source[where]
                return carry

            if len(left) >= 3:
                lax.fori_loop(0, 4, add, 0)
            else:
                add(0, 0)
            if stage < 4 + extra:
                rs_copy(unit, stage + 1).start()
            if stage >= 4 and stage < 4 + extra:
                do_rs(unit, stage + 1)

        def do_post(tap, stage):
            pair = (2 * tap, 2 * tap + 1)
            value = jnp.concatenate([half_sum[region(unit, own)] for unit in pair], axis=1)
            if tap == STAT:
                value = 0.95 * eig[...] + 0.05 * (value * (live_total * float(area * area)))
                scale_rows[...] = value + DAMPING
            else:
                high, low = split(value / scale_rows[...])
                value = dot(high, out_t_hi[...]) + dot(high, out_t_lo[...]) + dot(low, out_t_hi[...])
            for k, unit in enumerate(pair):
                work[region(unit, own, 0)] = value[:, 256 * k : 256 * k + 256]
                ag_copy(unit, 0).start()

        def do_ag(unit, stage):
            ag_copy(unit, stage).wait()
            if stage < 4:
                ag_copy(unit, stage + 1).start()


        def do_fin(unit, stage):
            if unit // 2 == STAT:
                return

            def cut(i, carry):
                rows = pl.ds(pl.multiple_of(i * 64, 64), 64)
                value = work[unit, i // 4, (i // 2) % 2, i % 2].reshape(64, 256)
                gathered_hi[rows], gathered_lo[rows] = split(value)
                return carry

            lax.fori_loop(0, 8, cut, 0)

            def tile(i, carry):
                rows = pl.ds(pl.multiple_of(i * 256, 256), 256)
                value = (
                    dot(in_hi[rows], gathered_hi[...])
                    + dot(in_hi[rows], gathered_lo[...])
                    + dot(in_lo[rows], gathered_hi[...])
                )
                work[unit, i] = value.reshape(2, 2, 2, 2, 16, 256)
                square_sum[...] += jnp.sum((value * value).reshape(32, 8, 256), axis=0)
                return carry

            lax.fori_loop(0, 2, tile, 0)

        def do_sm(stage, unused):
            sm_copy(stage).wait()
            before = small[:, core_half(core)] if stage == 0 else small_half[...]
            small_half[...] = before + small_got[stage]
            sm_copy(stage + 1).start()
            if stage >= 4 and stage < 4 + extra:
                do_sm(stage + 1, 0)

        square_sum[...] = jnp.zeros((8, 256), F32)
        sm_copy(0).start()
        run = (do_mm, do_rs, do_post, do_ag, do_fin, do_sm)
        for kind, which, stage in TASKS:
            run[kind](which, stage)

        sm_copy(len(bits)).wait()
        kept, came = small_half[...], small_back[...]
        low_half, high_half = jnp.where(core == 0, kept, came), jnp.where(core == 0, came, kept)
        block = jnp.concatenate([low_half, high_half], axis=1)
        head_part = jnp.where(row16w <= NCLS, block, 0.0)
        squared = (
            jnp.sum(jnp.sum(square_sum[...], axis=0, keepdims=True), axis=1, keepdims=True)
            + jnp.sum(norm_grads[0] * norm_grads[0] + norm_grads[1] * norm_grads[1], axis=1, keepdims=True)
            + jnp.sum(jnp.sum(head_part * head_part, axis=0, keepdims=True), axis=1, keepdims=True)
        )
        norm = jnp.sqrt(squared)
        factor = jnp.minimum(1.0, CLIP / (norm + 1e-06))
        facts[0:16] = block
        facts[16:24] = stack_rows(norm_grads + [block[NCLS + 1 : NCLS + 2], live_total, norm, factor])
        for copy in moments:
            copy.wait()

    square = (512, 512)
    pl.run_scoped(
        prepare,
        pltpu.VMEM((3, 10 * stride, 512), BF16),
        pltpu.VMEM((3, 1024, 512), BF16),
        pltpu.VMEM((2, 3, 512, 512), BF16),
        pltpu.VMEM((8, stride, 512), F32),
        pltpu.VMEM((8, stride, 512), F32),
        pltpu.VMEM((count_img, 8, 8, 512), BF16),
        *[pltpu.VMEM(square, BF16)] * 4,
        pltpu.VMEM((1024, 512), BF16),
    )
    pl.run_scoped(
        exchange,
        pltpu.VMEM((20, 2, 2, 2, 2, 16, 256), F32),
        pltpu.VMEM((AWAY, 2, 2, 2, 2, 16, 256), F32),
        pltpu.VMEM((512, 256), BF16),
        pltpu.VMEM((512, 256), BF16),
    )


def adamw(weight, grad, first, second, rate):
    first = 0.9 * first + 0.1 * grad
    second = 0.999 * second + 0.001 * grad * grad
    step_size = first / (1.0 - 0.9**STEP) / (jnp.sqrt(second / (1.0 - 0.999**STEP)) + 1e-08)
    return (weight - rate * (step_size + 0.01 * weight), first, second)


def adamw_positive(weight, grad, first, second, rate):
    first = 0.9 * first + 0.1 * grad
    second = 0.999 * second + 0.001 * grad * grad
    scaled = second * (1.0 / (1.0 - 0.999**STEP))
    root = scaled * lax.rsqrt(scaled) + 1e-08
    step = first * (rate / (1.0 - 0.9**STEP)) / root
    return (weight * (1.0 - 0.01 * rate) - step, first, second)


CHUNKS = 36
RING = 8


def update_kernel(
    facts,
    gain,
    shift,
    norm_first,
    norm_second,
    head,
    head_first,
    head_second,
    gradients,
    moments,
    loss_parts,
    grad_norm,
    norm_new,
    norm_m,
    norm_v,
    head_new,
    head_m,
    head_v,
    conv_new,
    conv_m,
    conv_v,
    scales_new,
    out_new,
    out_m,
    out_v,
    out_sem,
    scale_sem,
):
    tall = TAPS * 512 // CHUNKS
    outs = ((out_new, conv_new), (out_m, conv_m), (out_v, conv_v))

    def store(k, i):
        rows = pl.ds(pl.multiple_of(i * tall, tall), tall)
        return pltpu.make_async_copy(outs[k][0].at[i % RING], outs[k][1].at[rows], out_sem.at[k, i % RING])

    factor = facts[21:22, 0:1]

    def chunk(i, carry):
        @pl.when(i >= RING)
        def _():
            for k in range(3):
                store(k, i).wait()

        rows = pl.ds(pl.multiple_of(i * tall, tall), tall)
        more = pl.ds(pl.multiple_of(TAPS * 512 + i * tall, tall), tall)
        for half in range(2):
            cols = slice(256 * half, 256 * half + 256)
            where = (2 * (i // 4) + half, (i // 2) % 2, i % 2)
            grad = gradients[where].reshape(tall, 256)
            weight = gradients[(WEIGHT + where[0],) + where[1:]].reshape(tall, 256)
            out_new[i % RING, :, cols], out_m[i % RING, :, cols], out_v[i % RING, :, cols] = adamw_positive(
                weight, factor * grad, moments[rows, cols].astype(F32), moments[more, cols].astype(F32), 0.02
            )
        for k in range(3):
            store(k, i).start()
        return carry

    lax.fori_loop(0, CHUNKS, chunk, 0)
    scale_copies = [
        pltpu.make_async_copy(
            gradients.at[2 * STAT + k], scales_new.at[:, :, :, :, :, :, 256 * k : 256 * k + 256], scale_sem.at[k]
        )
        for k in range(2)
    ]
    for copy in scale_copies:
        copy.start()

    loss_parts[0] = facts[18, 0]
    loss_parts[1] = facts[19, 0]
    grad_norm[0] = facts[20, 0]
    grads = factor * facts[16:18, :]
    weights = jnp.concatenate([gain[...], shift[...]], axis=0)
    norm_new[...], norm_m[...], norm_v[...] = adamw(weights, grads, norm_first[...], norm_second[...], 0.1)
    block = factor * facts[0:16, :]
    head_new[:, 0:512], head_m[:, 0:512], head_v[:, 0:512] = adamw(
        head[:, 0:512], block[0:NCLS], head_first[:, 0:512], head_second[:, 0:512], 0.05
    )
    bias = jnp.concatenate([block[0:16, 0:128], jnp.zeros((112, 128), F32)], axis=0).T[0:NCLS, NCLS : NCLS + 1]
    head_new[:, 512:513], head_m[:, 512:513], head_v[:, 512:513] = adamw(
        head[:, 512:513], bias, head_first[:, 512:513], head_second[:, 512:513], 0.05
    )
    for i in range(CHUNKS - RING, CHUNKS):
        for k in range(3):
            store(k, i).wait()
    for copy in scale_copies:
        copy.wait()


def shards(
    sizes,
    images,
    micro_ids,
    labels,
    conv_weight,
    conv_first,
    conv_second,
    eig_scales,
    basis_in,
    basis_out,
    batchnorm_gain,
    batchnorm_shift,
    norm_first,
    norm_second,
    head,
    head_first,
    head_second,
):
    dp_count, rep_count = sizes
    count_img = images.shape[0]
    chips = dp_count * rep_count // 2
    bit_count = (dp_count * rep_count - 1).bit_length()
    extra = bit_count - 5
    vmem = pl.BlockSpec(memory_space=pltpu.VMEM)
    smem = pl.BlockSpec(memory_space=pltpu.SMEM)
    hbm = pl.BlockSpec(memory_space=pltpu.HBM)
    gain = batchnorm_gain.reshape(1, 512)
    shift = batchnorm_shift.reshape(1, 512)
    pixels = 8 * count_img
    square = (512, 512)
    dma = pltpu.SemaphoreType.DMA
    scratch = [
        pltpu.SMEM((count_img,), jnp.int32),
        pltpu.SMEM((count_img,), jnp.int32),
        pltpu.VMEM((1, 512), F32),
        pltpu.VMEM((1, 512), F32),
        pltpu.VMEM((NCLS, 513), F32),
        pltpu.VMEM((GOT_COUNT[0], 2, 2, 2, 2, 16, 256), F32),
        pltpu.VMEM((GOT_COUNT[1], 2, 2, 2, 16, 256), F32),
        pltpu.VMEM((GOT_COUNT[2], 2, 2, 16, 256), F32),
        pltpu.VMEM((GOT_COUNT[3], 2, 16, 256), F32),
        pltpu.VMEM((GOT_COUNT[4], 16, 256), F32),
        pltpu.VMEM((20, extra, 16, 256) if extra else (1, 1, 8, 128), F32),
        pltpu.VMEM((16, 512), F32),
        pltpu.VMEM((16, 256), F32),
        pltpu.VMEM((16, 256), F32),
        pltpu.VMEM((bit_count, 16, 256), F32),
        pltpu.VMEM((2, 8, 512), F32),
        pltpu.VMEM((2, 8, 256), F32),
        pltpu.VMEM((2, chips, 8, 256), F32),
        pltpu.VMEM((2, 2, 8, 256), F32),
        pltpu.VMEM((3, 512, 1280), BF16),
        pltpu.VMEM((512, 1024), BF16),
        pltpu.VMEM((512, 1024), BF16),
        *[pltpu.VMEM((1024, 512), BF16)] * 3,
        pltpu.VMEM((16, 512), F32),
        *[pltpu.VMEM(square, BF16)] * 4,
        pltpu.VMEM((5, 8, 512), F32),
        *[pltpu.VMEM((16, 512), F32)] * 4,
        pltpu.VMEM((128, 640), F32),
        pltpu.VMEM((16, 512), F32),
        pltpu.VMEM((8, 256), F32),
        dma((3,)),
        dma((11,)),
        dma((SEND_COUNT,)),
        dma((RECV_COUNT,)),
        dma((2, 20, extra) if extra else (1, 1, 1)),
        dma((bit_count + 1,)),
        dma((bit_count + 1,)),
        dma((4,)),
        dma((4,)),
        dma((2,)),
        dma((2,)),
    ]
    turned_basis = [x.reshape(2, 2, 2, 2, 2, 16, 512) for x in (basis_in, basis_out)]
    gradients, facts, moments = pl.pallas_call(
        functools.partial(main_kernel, (dp_count, rep_count, count_img)),
        out_shape=(
            pltpu.VMEM((WEIGHT + 2 * TAPS, 2, 2, 2, 2, 2, 16, 256), F32),
            pltpu.VMEM((24, 512), F32),
            pltpu.VMEM((2 * TAPS * 512, 512), BF16),
        ),
        in_specs=[hbm] * 12,
        out_specs=(vmem,) * 3,
        scratch_shapes=scratch,
        compiler_params=pltpu.CompilerParams(
            collective_id=0, has_side_effects=True, vmem_limit_bytes=71 * 2**19
        ),
        name="reduce_and_precondition",
    )(
        micro_ids,
        labels,
        images,
        gain,
        shift,
        head.T,
        conv_weight.reshape(TAPS, 2, 2, 2, 2, 2, 16, 512),
        conv_first,
        conv_second,
        eig_scales,
        *turned_basis,
    )
    tall = TAPS * 512 // CHUNKS
    head_shape = (NCLS, 513)
    outs = pl.pallas_call(
        update_kernel,
        out_shape=(
            jax.ShapeDtypeStruct((2,), F32),
            jax.ShapeDtypeStruct((1,), F32),
            *[jax.ShapeDtypeStruct((2, 512), F32)] * 3,
            *[jax.ShapeDtypeStruct(head_shape, F32)] * 3,
            *[jax.ShapeDtypeStruct((TAPS * 512, 512), F32)] * 3,
            jax.ShapeDtypeStruct((2, 2, 2, 2, 2, 16, 512), F32),
        ),
        in_specs=[vmem] * 10,
        out_specs=(smem, smem) + (vmem,) * 6 + (hbm,) * 4,
        scratch_shapes=[
            *[pltpu.VMEM((RING, tall, 512), F32)] * 3,
            dma((3, RING)),
            dma((2,)),
        ],
        compiler_params=pltpu.CompilerParams(vmem_limit_bytes=27 * 2**18),
        name="adamw",
    )(
        facts,
        gain,
        shift,
        norm_first,
        norm_second,
        head.T,
        head_first.T,
        head_second.T,
        gradients,
        moments,
    )
    loss_parts, grad_norm, norm_new, norm_m, norm_v, head_new, head_m, head_v, conv_new, conv_m, conv_v, scales_new = outs
    return (
        loss_parts,
        grad_norm.reshape(()),
        conv_new,
        conv_m,
        conv_v,
        scales_new.reshape(square),
        norm_new,
        norm_m,
        norm_v,
        head_new.T,
        head_m.T,
        head_v.T,
    )


def solution(mesh):
    split_images = P(("dp", "rep"))
    in_specs = (P(("dp", "rep"), None, None, None), split_images, split_images) + (P(),) * 13
    sizes = (mesh.shape["dp"], mesh.shape["rep"])
    return jax.shard_map(
        functools.partial(shards, sizes), mesh=mesh, in_specs=in_specs, out_specs=(P(),) * 12, check_vma=False
    )
```

```python
import functools

import jax
import jax.numpy as jnp
from jax import lax
from jax.experimental import pallas as pl
from jax.experimental.pallas import tpu as pltpu
from jax.sharding import PartitionSpec as P

NCLS = 10
STEP = 5
NORM_EPS = 1e-05
DAMPING = 0.001
CLIP = 0.01
MESH = pl.DeviceIdType.MESH
F32 = jnp.float32
BF16 = jnp.bfloat16
HIGHEST = lax.Precision.HIGHEST
TAPS = 9
STAT = 9
WEIGHT = 20
AWAY = 4
UNITS = (1, 7, 16, 8, 9, 19, 3, 18, 2, 12, 4, 11, 5, 14, 6, 10, 13, 17, 0, 15)
RS_ORDER = (
    (1, 2, 3, 4), (3, 1, 2, 4), (1, 2, 3, 4), (2, 1, 3, 4), (2, 1, 3, 4),
    (3, 2, 4, 1), (2, 3, 4, 1), (1, 3, 2, 4), (1, 3, 2, 4), (3, 2, 1, 4),
    (1, 3, 2, 4), (1, 3, 4, 2), (3, 2, 1, 4), (2, 1, 3, 4), (1, 2, 3, 4),
    (2, 1, 3, 4), (2, 3, 4, 1), (1, 2, 3, 4), (1, 2, 3, 4), (2, 1, 3, 4),
)
AG_ORDER = (
    (3, 2, 1, 4), (1, 3, 4, 2), (1, 2, 3, 4), (2, 3, 4, 1), (1, 2, 3, 4),
    (1, 3, 4, 2), (2, 1, 3, 4), (1, 2, 3, 4), (1, 2, 3, 4), (1, 2, 3, 4),
    (3, 1, 2, 4), (2, 3, 4, 1), (2, 3, 1, 4), (2, 3, 4, 1), (2, 3, 4, 1),
    (1, 3, 4, 2), (2, 3, 4, 1), (1, 2, 3, 4), (1, 2, 3, 4), (2, 1, 3, 4),
)
TASKS = (
    (0, 1, 0), (0, 7, 0), (0, 16, 0), (5, 0, 0), (1, 1, 0), (0, 8, 0), (1, 7, 0), (1, 16, 0),
    (0, 9, 0), (0, 19, 0), (1, 8, 0), (1, 9, 0), (5, 1, 0), (0, 3, 0), (1, 19, 0), (0, 18, 0),
    (1, 3, 0), (1, 1, 1), (1, 7, 1), (1, 16, 1), (1, 18, 0), (0, 2, 0), (5, 2, 0), (0, 12, 0),
    (0, 4, 0), (1, 9, 1), (1, 2, 0), (1, 8, 1), (1, 12, 0), (0, 11, 0), (1, 19, 1), (1, 7, 2),
    (1, 4, 0), (1, 1, 2), (0, 5, 0), (1, 11, 0), (1, 16, 2), (0, 14, 0), (5, 3, 0), (0, 6, 0),
    (1, 3, 1), (1, 5, 0), (1, 18, 1), (1, 14, 0), (1, 8, 2), (0, 10, 0), (1, 6, 0), (1, 9, 2),
    (0, 13, 0), (1, 7, 3), (0, 17, 0), (1, 10, 0), (1, 2, 1), (0, 0, 0), (1, 12, 1), (1, 13, 0),
    (1, 17, 0), (1, 19, 2), (1, 4, 1), (1, 16, 3), (1, 0, 0), (0, 15, 0), (1, 1, 3), (5, 4, 0),
    (1, 18, 2), (1, 15, 0), (1, 11, 1), (1, 8, 3), (1, 5, 1), (1, 3, 2), (1, 19, 3), (1, 7, 4),
    (1, 18, 3), (1, 1, 4), (1, 6, 1), (1, 11, 2), (1, 14, 1), (1, 2, 2), (1, 9, 3), (1, 3, 3),
    (1, 8, 4), (1, 12, 2), (1, 19, 4), (1, 18, 4), (2, 9, 0), (1, 6, 2), (1, 10, 1), (1, 2, 3),
    (1, 11, 3), (1, 13, 1), (1, 9, 4), (2, 4, 0), (1, 3, 4), (3, 18, 0), (1, 17, 1), (3, 19, 0),
    (1, 15, 1), (1, 4, 2), (1, 10, 2), (1, 16, 4), (1, 6, 3), (1, 5, 2), (1, 2, 4), (2, 1, 0),
    (3, 18, 1), (3, 8, 0), (1, 14, 2), (3, 19, 1), (3, 9, 0), (1, 11, 4), (1, 0, 1), (1, 4, 3),
    (1, 12, 3), (1, 17, 2), (1, 10, 3), (3, 8, 1), (1, 13, 2), (1, 5, 3), (1, 14, 3), (3, 2, 0),
    (3, 18, 2), (3, 9, 1), (1, 15, 2), (1, 6, 4), (2, 3, 0), (3, 3, 0), (1, 4, 4), (1, 0, 2),
    (1, 17, 3), (1, 12, 4), (3, 19, 2), (1, 13, 3), (1, 10, 4), (1, 5, 4), (3, 8, 2), (2, 5, 0),
    (2, 2, 0), (3, 2, 1), (1, 14, 4), (3, 9, 2), (1, 15, 3), (3, 6, 0), (3, 18, 3), (3, 7, 0),
    (1, 0, 3), (3, 3, 1), (3, 18, 4), (4, 18, 0), (3, 19, 3), (1, 17, 4), (2, 8, 0), (3, 5, 0),
    (1, 13, 4), (2, 6, 0), (3, 8, 3), (3, 11, 0), (3, 10, 0), (3, 19, 4), (3, 6, 1), (3, 2, 2),
    (4, 19, 0), (3, 4, 0), (3, 7, 1), (3, 8, 4), (4, 8, 0), (1, 0, 4), (1, 15, 4), (3, 3, 2),
    (2, 0, 0), (3, 9, 3), (3, 10, 1), (3, 16, 0), (2, 7, 0), (3, 13, 0), (3, 17, 0), (3, 5, 1),
    (3, 7, 2), (3, 9, 4), (4, 9, 0), (3, 12, 0), (3, 6, 2), (3, 4, 1), (3, 11, 1), (3, 0, 0),
    (3, 3, 3), (3, 2, 3), (3, 17, 1), (3, 1, 0), (3, 15, 0), (3, 16, 1), (3, 10, 2), (3, 3, 4),
    (3, 5, 2), (4, 3, 0), (3, 13, 1), (3, 14, 0), (3, 11, 2), (3, 2, 4), (4, 2, 0), (3, 6, 3),
    (3, 7, 3), (3, 1, 1), (3, 4, 2), (3, 12, 1), (3, 16, 2), (3, 6, 4), (4, 6, 0), (3, 17, 2),
    (3, 0, 1), (3, 7, 4), (3, 15, 1), (4, 7, 0), (3, 10, 3), (3, 5, 3), (3, 11, 3), (3, 13, 2),
    (3, 10, 4), (4, 10, 0), (3, 11, 4), (3, 5, 4), (4, 11, 0), (3, 16, 3), (3, 14, 1), (3, 4, 3),
    (3, 1, 2), (4, 5, 0), (3, 12, 2), (3, 16, 4), (3, 0, 2), (4, 16, 0), (3, 17, 3), (3, 15, 2),
    (3, 4, 4), (4, 4, 0), (3, 13, 3), (3, 14, 2), (3, 17, 4), (4, 17, 0), (3, 1, 3), (3, 13, 4),
    (4, 13, 0), (3, 12, 3), (3, 0, 3), (3, 1, 4), (4, 1, 0), (3, 15, 3), (3, 12, 4), (4, 12, 0),
    (3, 0, 4), (3, 14, 3), (4, 0, 0), (3, 15, 4), (4, 15, 0), (3, 14, 4), (4, 14, 0),
)
GOT_COUNT = (6, 14, 14, 10, 10)
RECV_COUNT, SEND_COUNT = 54, 20
RS_SLOT = (
    (1, 5, 0, 6, 7), (0, 0, 1, 2, 1), (2, 8, 0, 0, 0), (0, 6, 7, 7, 6), (4, 10, 10, 3, 1),
    (1, 1, 3, 4, 4), (3, 11, 1, 2, 9), (1, 1, 0, 0, 0), (3, 4, 3, 3, 2), (4, 3, 4, 6, 5),
    (0, 12, 2, 9, 3), (0, 0, 8, 1, 8), (3, 9, 9, 8, 2), (4, 3, 12, 2, 6), (2, 2, 11, 0, 5),
    (0, 4, 13, 5, 8), (2, 2, 2, 1, 7), (5, 13, 4, 1, 0), (1, 7, 6, 5, 4), (5, 5, 5, 4, 3),
)
AG_RECV = (
    (10, 35, 10, 7, 4), (30, 6, 23, 5, 0), (6, 2, 17, 29, 2), (12, 16, 12, 28, 1), (18, 9, 7, 22, 4),
    (0, 23, 16, 18, 3), (10, 6, 26, 5, 0), (15, 7, 13, 33, 9), (3, 0, 8, 4, 2), (5, 1, 9, 19, 0),
    (11, 8, 31, 17, 1), (5, 27, 4, 19, 2), (24, 34, 24, 6, 3), (22, 32, 20, 15, 2), (25, 21, 16, 9, 2),
    (3, 12, 14, 8, 1), (21, 15, 8, 13, 0), (20, 14, 11, 36, 1), (0, 2, 7, 14, 25), (1, 4, 13, 3, 1),
)
RS_SEND = (
    (18, 18, 7, 7, 7), (0, 0, 0, 0, 0), (8, 8, 8, 8, 8), (6, 6, 6, 6, 6), (10, 10, 10, 10, 10),
    (12, 12, 12, 2, 2), (14, 14, 0, 0, 0), (1, 1, 1, 1, 1), (3, 3, 3, 3, 3), (4, 4, 4, 4, 4),
    (15, 15, 9, 9, 9), (11, 11, 11, 7, 7), (9, 9, 9, 3, 3), (16, 16, 13, 13, 5), (13, 13, 11, 11, 11),
    (19, 19, 15, 15, 14), (2, 2, 2, 2, 2), (17, 17, 6, 6, 6), (7, 7, 7, 7, 1), (5, 5, 5, 5, 5),
)
AG_SEND = (
    (7, 7, 6, 2, 2), (12, 11, 10, 7, 0), (8, 8, 8, 1, 1), (12, 12, 12, 2, 2), (10, 8, 8, 8, 4),
    (13, 13, 13, 2, 2), (0, 0, 0, 0, 0), (16, 15, 10, 10, 1), (4, 4, 4, 2, 2), (14, 14, 14, 11, 11),
    (4, 4, 4, 4, 4), (9, 9, 9, 9, 7), (5, 5, 5, 5, 4), (16, 16, 13, 9, 4), (14, 14, 3, 3, 1),
    (15, 12, 1, 1, 0), (3, 3, 3, 3, 2), (6, 6, 6, 0, 0), (1, 1, 1, 1, 1), (5, 5, 5, 3, 1),
)


def split(value):
    high = value.astype(BF16)
    return high, (value - high.astype(F32)).astype(BF16)


def dot(a, b, dims=((1,), (0,))):
    return lax.dot_general(a, b, (dims, ((), ())), preferred_element_type=F32)


def dot_exact(a, b, dims=((1,), (0,))):
    return lax.dot_general(a, b, (dims, ((), ())), precision=HIGHEST, preferred_element_type=F32)


def main_kernel(
    sizes,
    micro_hbm,
    labels_hbm,
    images_hbm,
    gain_hbm,
    shift_hbm,
    head_hbm,
    weight,
    first_hbm,
    second_hbm,
    eig_hbm,
    in_hbm,
    out_hbm,
    work,
    facts,
    moments_held,
    micro,
    labels,
    gain_ref,
    shift_ref,
    head,
    got0,
    got1,
    got2,
    got3,
    got4,
    got_more,
    small,
    small_half,
    small_back,
    small_got,
    tile_in,
    tile_core,
    tile_slots,
    tile_out,
    turned_hi,
    box_hi,
    box_lo,
    rot_hi,
    rot2_hi,
    rot2_lo,
    eig,
    in_hi,
    in_lo,
    out_t_hi,
    out_t_lo,
    rows_stat,
    pooled,
    shares,
    shares_x,
    dpool,
    head_pad,
    scale_rows,
    square_sum,
    w_sem,
    load_sem,
    send_sem,
    recv_sem,
    more_sem,
    sm_send,
    sm_recv,
    core_send,
    core_recv,
    chip_send,
    chip_recv,
):
    dp_count, rep_count, count_img = sizes
    area = 64
    cells = 16
    chips = dp_count * rep_count // 2
    dp = lax.axis_index("dp")
    rep = lax.axis_index("rep")
    core = rep % 2
    chip = dp * (rep_count // 2) + rep // 2
    bits = [("rep", 1), ("dp", 1), ("rep", 2), ("dp", 2), ("dp", 4)]
    step = 8
    while step < dp_count:
        bits.append(("dp", step))
        step *= 2
    step = 4
    while step < rep_count:
        bits.append(("rep", step))
        step *= 2
    extra = len(bits) - 5
    stride = count_img * 8
    mine = [((dp if name == "dp" else rep) // weight_of) % 2 for name, weight_of in bits]

    own = dict(enumerate(mine[:5]))
    own_block = (((mine[0] * 2 + mine[1]) * 2 + mine[2]) * 2 + mine[3]) * 2 + mine[4]

    def partner(k):
        name, weight_of = bits[k]
        change = (1 - 2 * mine[k]) * weight_of
        return (dp + change, rep) if name == "dp" else (dp, rep + change)

    def chip_device(q):
        return (q // (rep_count // 2), (q % (rep_count // 2)) * 2 + core)

    def weight_copy(unit):
        cols = pl.ds(pl.multiple_of((unit % 2) * 256, 256), 256)
        return pltpu.make_async_copy(
            weight.at[unit // 2, :, :, :, :, :, :, cols], work.at[WEIGHT + unit], w_sem.at[unit // 6]
        )

    def start_weight(unit, carry):
        weight_copy(unit).start()
        return carry

    loads = [
        pltpu.make_async_copy(src, dst, load_sem.at[k])
        for k, (src, dst) in enumerate(
            (
                (in_hbm.at[:, :, :, :, :, :, 0:256], work.at[4]),
                (in_hbm.at[:, :, :, :, :, :, 256:512], work.at[5]),
                (out_hbm.at[:, :, :, :, :, :, 0:256], work.at[6]),
                (out_hbm.at[:, :, :, :, :, :, 256:512], work.at[7]),
                (eig_hbm.at[pl.ds(pl.multiple_of(own_block * 16, 16), 16)], eig),
            )
        )
    ]

    barrier = pltpu.get_barrier_semaphore()

    def greet(k, carry):
        pl.semaphore_signal(barrier, inc=1, device_id=chip_device((chip + k) % chips), device_id_type=MESH)
        return carry

    lax.fori_loop(1, chips, greet, 0)
    pl.semaphore_signal(barrier, inc=1, device_id=partner(0), device_id_type=MESH)

    row8 = lax.broadcasted_iota(jnp.int32, (8, 512), 0)
    row16w = lax.broadcasted_iota(jnp.int32, (16, 512), 0)
    zero_tile = jnp.zeros((8, 512), F32)

    def stack_rows(rows):
        tile = zero_tile
        for k, row in enumerate(rows):
            tile = jnp.where(row8 == k, jnp.broadcast_to(row, (8, 512)), tile)
        return tile

    def core_half(which):
        return pl.ds(pl.multiple_of(which * 256, 256), 256)

    def prepare(
        narrow, wide, weight_low, conv, share, images, in_t_hi, in_t_lo, out_hi, out_lo, grad_low
    ):
        first_loads = [
            pltpu.make_async_copy(src, dst, load_sem.at[5 + k])
            for k, (src, dst) in enumerate(
                (
                    (images_hbm, images),
                    (micro_hbm, micro),
                    (labels_hbm, labels),
                    (gain_hbm, gain_ref),
                    (shift_hbm, shift_ref),
                    (head_hbm, head),
                )
            )
        ]
        first_loads[0].start()
        first_loads[1].start()
        lax.fori_loop(0, 12, start_weight, 0)
        for copy in first_loads[2:]:
            copy.start()

        column = lax.broadcasted_iota(jnp.int32, (2, 8, 512), 1)
        for k in range(3):
            narrow[k, 0:stride] = jnp.zeros((stride, 512), BF16)
            narrow[k, 9 * stride : 10 * stride] = jnp.zeros((stride, 512), BF16)

        def build(h, carry):
            for pair in range(count_img // 2):
                block = images[2 * pair : 2 * pair + 2, h].astype(F32)
                left = jnp.where(column == 0, 0.0, pltpu.roll(block, 1, 1))
                right = jnp.where(column == 7, 0.0, pltpu.roll(block, 7, 1))
                at = pl.ds(pl.multiple_of((h + 1) * stride + 16 * pair, 16), 16)
                for k, value in enumerate((left, block, right)):
                    narrow[k, at] = value.reshape(16, 512).astype(BF16)
            return carry

        first_loads[0].wait()
        lax.fori_loop(0, 8, build, 0)

        def wait_row(dy):
            held = work.at[pl.ds(WEIGHT + 6 * dy, 6)]
            pltpu.make_async_copy(held, held, w_sem.at[dy]).wait()

        def cast(dy, k):
            dx, j, half = k // 4, (k // 2) % 2, k % 2
            piece = work[WEIGHT + 2 * (3 * dy + dx) + j, half].reshape(256, 256)
            weight_low[dy % 2, dx, 256 * half : 256 * half + 256, 256 * j : 256 * j + 256] = piece.astype(BF16)

        wait_row(0)
        lax.fori_loop(12, 2 * TAPS, start_weight, 0)
        for k in range(12):
            cast(0, k)
        for dy in range(3):
            if dy < 2:
                wait_row(dy + 1)
            if dy == 1:
                for copy in loads:
                    copy.start()
            for m in range(2):
                for n in range(2):
                    total = None
                    for dx in range(3):
                        begin = (dy + 4 * m) * stride
                        term = dot(
                            narrow[dx, begin : begin + 4 * stride], weight_low[dy % 2, dx, :, n * 256 : n * 256 + 256]
                        )
                        total = term if total is None else total + term
                        if dy < 2:
                            cast(dy + 1, 6 * m + 3 * n + dx)
                    at = (slice(4 * m, 4 * m + 4), slice(None), slice(n * 256, n * 256 + 256))
                    total = total.reshape(4, stride, 256)
                    conv[at] = total if dy == 0 else conv[at] + total

        for copy in first_loads[1:]:
            copy.wait()
        def member(n):
            return [jnp.where(micro[n] == m, 1.0, 0.0).astype(F32) for m in range(3)]

        def gather_sums(n, carry):
            at = pl.ds(pl.multiple_of(n * 8, 8), 8)
            first = jnp.zeros((8, 512), F32)
            second = jnp.zeros((8, 512), F32)
            for h in range(8):
                value = conv[h, at]
                first = first + value
                second = second + value * value
            kinds = member(n)
            return tuple(c + k * first for c, k in zip(carry[:3], kinds)) + tuple(
                c + k * second for c, k in zip(carry[3:6], kinds)
            )

        sums = lax.fori_loop(0, count_img, gather_sums, (zero_tile,) * 6)
        counts = [jnp.zeros((), F32)] * 3
        for n in range(count_img):
            counts = [c + k for c, k in zip(counts, member(n))]
        lane8 = lax.broadcasted_iota(jnp.int32, (8, 512), 1)

        count_row = zero_tile
        for m in range(3):
            count_row = jnp.where(lane8 % 256 == m, counts[m], count_row)
        tile_in[0] = jnp.where(row8 == 6, count_row, stack_rows([jnp.sum(s, axis=0, keepdims=True) for s in sums]))

        def tile_copy(i):
            return pltpu.make_async_remote_copy(
                src_ref=tile_in.at[i, :, core_half(1 - core)],
                dst_ref=tile_core.at[i],
                send_sem=core_send.at[2 * i],
                recv_sem=core_recv.at[2 * i],
                device_id=partner(0),
                device_id_type=MESH,
            )

        def tile_start(i):
            tile_copy(i).start()
            tile_copy(i).wait()
            tile_slots[i, 0] = tile_in[i, :, core_half(core)] + tile_core[i]

            def give(k, carry):
                pltpu.make_async_remote_copy(
                    src_ref=tile_slots.at[i, 0],
                    dst_ref=tile_slots.at[i, k],
                    send_sem=chip_send.at[i],
                    recv_sem=chip_recv.at[i],
                    device_id=chip_device((chip + k) % chips),
                    device_id_type=MESH,
                ).start()
                return carry

            lax.fori_loop(1, chips, give, 0)

        def tile_end(i):
            others = tile_slots.at[i, pl.ds(1, chips - 1)]
            pltpu.make_async_remote_copy(
                src_ref=others,
                dst_ref=others,
                send_sem=chip_send.at[i],
                recv_sem=chip_recv.at[i],
                device_id=partner(0),
                device_id_type=MESH,
            ).wait()

            def add(k, total):
                return total + tile_slots[i, (chip - k + chips) % chips]

            tile_out[i, core] = lax.fori_loop(0, chips, add, jnp.zeros((8, 256), F32))
            back = pltpu.make_async_remote_copy(
                src_ref=tile_out.at[i, core],
                dst_ref=tile_out.at[i, core],
                send_sem=core_send.at[2 * i + 1],
                recv_sem=core_recv.at[2 * i + 1],
                device_id=partner(0),
                device_id_type=MESH,
            )
            back.start()
            back.wait()
            return jnp.concatenate([tile_out[i, 0], tile_out[i, 1]], axis=1)

        pl.semaphore_wait(barrier, chips)
        tile_start(0)

        def widen(h, carry):
            source = pl.ds(pl.multiple_of((h + 1) * stride, 16), stride)
            target = pl.ds(pl.multiple_of(h * 128, 128), stride)
            fill = pl.ds(pl.multiple_of(h * 128 + stride, 16), 128 - stride)
            for k in range(3):
                wide[k, target] = narrow[k, source]
                wide[k, fill] = jnp.zeros((128 - stride, 512), BF16)
            grad_low[fill] = jnp.zeros((128 - stride, 512), BF16)
            return carry

        lax.fori_loop(0, 8, widen, 0)
        for copy in loads:
            copy.wait()
        value = jnp.concatenate([work[4].reshape(512, 256), work[5].reshape(512, 256)], axis=1)
        in_hi[...], in_lo[...] = split(value)
        in_t_hi[...], in_t_lo[...] = split(value.T)
        for dx in range(3):
            turned_hi[dx, :, 0:128] = jnp.zeros((512, 128), BF16)
            turned_hi[dx, :, 1152:1280] = jnp.zeros((512, 128), BF16)

        def turn(j, carry):
            total = None
            for dx in range(3):
                rows = wide[dx, pl.ds(pl.multiple_of(256 * j, 256), 256)]
                value = dot(in_t_hi[...], rows, ((1,), (1,))) + dot(in_t_lo[...], rows, ((1,), (1,)))
                at = pl.ds(pl.multiple_of(128 + 256 * j, 128), 256)
                turned_hi[dx, :, at] = value.astype(BF16)
                total = value * value if total is None else total + value * value
            work[j] = total.reshape(2, 2, 2, 2, 2, 16, 256)
            return carry

        lax.fori_loop(0, 2, turn, 0)

        head_pad[...] = jnp.zeros((128, 640), F32)
        head_pad[0:NCLS, 0:513] = head[...]
        head_rows = head_pad[:, 0:512].astype(BF16)
        row16 = lax.broadcasted_iota(jnp.int32, (16, 128), 0)
        lane16 = lax.broadcasted_iota(jnp.int32, (16, 128), 1)
        label_of = jnp.zeros((16, 128), jnp.int32)
        micro_of = jnp.full((16, 128), 3, jnp.int32)
        for n in range(count_img):
            label_of = jnp.where(row16 == n, labels[n], label_of)
            micro_of = jnp.where(row16 == n, micro[n], micro_of)
        is_class = lane16 < NCLS
        live = jnp.where(micro_of < 3, 1.0, 0.0)
        onehot = jnp.where(lane16 == label_of, 1.0, 0.0)
        totals = tile_end(0)

        gain = gain_ref[...]
        shift = shift_ref[...]
        live_total = totals[6:7, 0:1] + totals[6:7, 1:2] + totals[6:7, 2:3]
        pixels = [totals[6:7, m : m + 1] * float(area) for m in range(3)]
        mean_rows, rstd_rows = [], []
        for m in range(3):
            mean = totals[m : m + 1] / pixels[m]
            var = totals[3 + m : 4 + m] / pixels[m] - mean * mean
            mean_rows.append(mean)
            rstd_rows.append(lax.rsqrt(var + NORM_EPS))
        rows_stat[0] = stack_rows(mean_rows)
        rows_stat[1] = stack_rows(rstd_rows)

        def image_rows(n, k):
            kinds = member(n)
            row = sum(kinds[m] * rows_stat[k, m : m + 1] for m in range(3))
            return row, 1.0 - (kinds[0] + kinds[1] + kinds[2])

        even = lax.broadcasted_iota(jnp.int32, (8, 512), 0) % 2 == 0
        pooled[...] = jnp.zeros((16, 512), F32)
        shares[...] = jnp.zeros((16, 512), F32)
        shares_x[...] = jnp.zeros((16, 512), F32)

        def forward(n, carry):
            mean, dead = image_rows(n, 0)
            rstd, _ = image_rows(n, 1)
            rstd = rstd + dead
            at = pl.ds(pl.multiple_of(n * 8, 8), 8)
            cell_sum, share_sum, share_x_sum = zero_tile, zero_tile, zero_tile
            for a in range(4):
                xs = [(conv[2 * a + k, at] - mean) * rstd for k in range(2)]
                exps = [jnp.exp(gain * x + shift) for x in xs]
                both = exps[0] + exps[1]
                both = both + jnp.where(even, pltpu.roll(both, 7, 0), pltpu.roll(both, 1, 0))
                both = both + 4.0
                cell_sum = cell_sum + jnp.log(both)
                inverse = 1.0 / both
                for k in range(2):
                    part = exps[k] * inverse
                    share[2 * a + k, at] = part
                    share_sum = share_sum + part
                    share_x_sum = share_x_sum + part * xs[k]
            row = pl.ds(n, 1)
            pooled[row] = jnp.sum(cell_sum, axis=0, keepdims=True) * (0.5 / cells)
            shares[row] = jnp.sum(share_sum, axis=0, keepdims=True)
            shares_x[row] = jnp.sum(share_x_sum, axis=0, keepdims=True)
            return carry

        lax.fori_loop(0, count_img, forward, 0)

        pooled_low = pooled[...].astype(BF16)
        logits = dot(pooled_low, head_rows, ((1,), (1,))) + head_pad[:, 512:640].T[0:1, :]
        top = jnp.max(jnp.where(is_class, logits, -3e38), axis=1, keepdims=True)
        shifted = jnp.where(is_class, logits - top, 0.0)
        log_sum = jnp.log(jnp.sum(jnp.where(is_class, jnp.exp(shifted), 0.0), axis=1, keepdims=True))
        logp = jnp.where(is_class, shifted - log_sum, 0.0)
        per_img = -(
            0.9 * jnp.sum(onehot * logp, axis=1, keepdims=True) + 0.1 / NCLS * jnp.sum(logp, axis=1, keepdims=True)
        )
        loss = jnp.sum(live[:, 0:1] * per_img, axis=0, keepdims=True)
        dlogits = jnp.where(is_class, jnp.exp(logp) - 0.9 * onehot - 0.1 / NCLS, 0.0) * (live / live_total)
        dpool[...] = dot_exact(dlogits, head_rows.astype(F32)) * (1.0 / cells)
        back_rows = []
        for which in (shares, shares_x):
            for m in range(3):
                inside = jnp.where(micro_of[:, 0:1] == m, 1.0, 0.0)
                back_rows.append(jnp.sum(inside * (dpool[...] * which[...]), axis=0, keepdims=True))
        tile_in[1] = stack_rows(back_rows)
        tile_start(1)

        head_grad = dot_exact(dlogits, pooled_low.astype(F32), ((0,), (0,)))
        bias_grad = jnp.concatenate(
            [jnp.sum(dlogits, axis=0, keepdims=True), jnp.zeros((1, 384), F32)], axis=1
        )
        block = jnp.where(row16w < NCLS, head_grad[0:16], 0.0)
        block = jnp.where(row16w == NCLS, bias_grad, block)
        small[...] = jnp.where(row16w == NCLS + 1, loss, block)

        def scale(n, carry):
            mean, dead = image_rows(n, 0)
            rstd, _ = image_rows(n, 1)
            rstd = rstd + dead
            factor = rstd * gain * dpool[pl.ds(n, 1)]
            at = pl.ds(pl.multiple_of(n * 8, 8), 8)
            for h in range(8):
                share[h, at] = factor * share[h, at]
                conv[h, at] = (conv[h, at] - mean) * rstd * rstd
            return carry

        lax.fori_loop(0, count_img, scale, 0)

        lax.fori_loop(2, 4, turn, 0)
        def squares(h):
            return work[h // 2, :, :, :, :, :, :, (h % 2) * 128 : (h % 2) * 128 + 128].reshape(512, 128)

        for h in range(8):
            value = squares(h)
            if h > 0:
                value = value + squares(h - 1)
            if h < 7:
                value = value + squares(h + 1)
            box_hi[:, h * 128 : h * 128 + 128], box_lo[:, h * 128 : h * 128 + 128] = split(value)

        value = jnp.concatenate([work[6].reshape(512, 256), work[7].reshape(512, 256)], axis=1)
        out_hi[...], out_lo[...] = split(value)
        out_t_hi[...], out_t_lo[...] = split(value.T)
        totals = tile_end(1)
        norm_grads = [
            totals[3:4] + totals[4:5] + totals[5:6],
            totals[0:1] + totals[1:2] + totals[2:3],
        ]
        rows_stat[4] = stack_rows(norm_grads + [jnp.broadcast_to(live_total, (1, 512))])
        rows_stat[2] = stack_rows([gain * totals[m : m + 1] / pixels[m] for m in range(3)])
        rows_stat[3] = stack_rows([gain * totals[3 + m : 4 + m] / pixels[m] for m in range(3)])

        def backward(pair, carry):
            parts = []
            for k in range(2):
                n = 2 * pair + k
                rstd, dead = image_rows(n, 1)
                offset, _ = image_rows(n, 2)
                slope, _ = image_rows(n, 3)
                parts.append(((rstd + dead) * offset, slope, pl.ds(pl.multiple_of(n * 8, 8), 8)))
            for h in range(8):
                values = [share[h, at] - offset - conv[h, at] * slope for offset, slope, at in parts]
                rows = pl.ds(pl.multiple_of(h * 128 + 16 * pair, 16), 16)
                grad_low[rows] = jnp.concatenate(values, axis=0).astype(BF16)
            return carry

        lax.fori_loop(0, count_img // 2, backward, 0)

        def rotate(k, carry):
            rows = pl.ds(pl.multiple_of(k * 256, 256), 256)
            value = dot(grad_low[rows], out_hi[...]) + dot(grad_low[rows], out_lo[...])
            rot_hi[rows] = value.astype(BF16)
            rot2_hi[rows], rot2_lo[rows] = split(value * value)
            return carry

        lax.fori_loop(0, 4, rotate, 0)

    def exchange(half_sum, away, gathered_hi, gathered_lo, partial):
        got = (got0, got1, got2, got3, got4)
        left_home = set()
        live_total = rows_stat[4, 2:3, 0:1]
        norm_grads = [rows_stat[4, 0:1], rows_stat[4, 1:2]]
        moments = [
            pltpu.make_async_copy(src, moments_held.at[pl.ds(k * TAPS * 512, TAPS * 512)], load_sem.at[k])
            for k, src in enumerate((first_hbm, second_hbm))
        ]
        for copy in moments:
            copy.start()

        def region(unit, fixed, first=1):
            return (unit,) + tuple(fixed.get(k, slice(None)) for k in range(first, 5))

        def rs_copy(unit, stage):
            if stage < 5:
                order = (0,) + RS_ORDER[unit]
                fixed = {k: mine[k] for k in order[:stage]}
                fixed[order[stage]] = 1 - mine[order[stage]]
                target, to = got[stage].at[RS_SLOT[unit][stage]], partner(order[stage])
                sems = (send_sem.at[RS_SEND[unit][stage]], recv_sem.at[sum(GOT_COUNT[:stage]) + RS_SLOT[unit][stage]])
            else:
                fixed = dict(enumerate(mine[:5]))
                target, to = got_more.at[unit, stage - 5], partner(stage)
                sems = (more_sem.at[0, unit, stage - 5], more_sem.at[1, unit, stage - 5])
            source = half_sum.at[region(unit, fixed)] if stage else away.at[UNITS.index(unit) % AWAY]
            return pltpu.make_async_remote_copy(
                src_ref=source,
                dst_ref=target,
                send_sem=sems[0],
                recv_sem=sems[1],
                device_id=to,
                device_id_type=MESH,
            )

        def ag_copy(unit, stage):
            order = (0,) + AG_ORDER[unit]
            where = work.at[region(unit, {k: mine[k] for k in order[: 5 - stage]}, 0)]
            return pltpu.make_async_remote_copy(
                src_ref=where,
                dst_ref=where,
                send_sem=send_sem.at[AG_SEND[unit][stage]],
                recv_sem=recv_sem.at[AG_RECV[unit][stage]],
                device_id=partner(order[4 - stage]),
                device_id_type=MESH,
            )

        def sm_copy(stage):
            if stage == 0:
                source, target, to = small.at[:, core_half(1 - core)], small_got.at[0], partner(0)
            elif stage < len(bits):
                source, target, to = small_half, small_got.at[stage], partner(stage)
            else:
                source, target, to = small_half, small_back, partner(0)
            return pltpu.make_async_remote_copy(
                src_ref=source,
                dst_ref=target,
                send_sem=sm_send.at[stage],
                recv_sem=sm_recv.at[stage],
                device_id=to,
                device_id_type=MESH,
            )

        def do_mm(unit, stage):
            tap, cols = unit // 2, slice((unit % 2) * 256, (unit % 2) * 256 + 256)
            dy, dx = tap // 3, tap % 3
            place = UNITS.index(unit)
            if place >= AWAY and UNITS[place - AWAY] not in left_home:
                left_home.add(UNITS[place - AWAY])
                rs_copy(UNITS[place - AWAY], 0).wait_send()
            for stays, half in enumerate((1 - core, core)):
                rows = pl.ds(pl.multiple_of(half * 256, 256), 256)
                if tap == STAT:
                    value = (
                        dot(box_hi[rows], rot2_hi[:, cols])
                        + dot(box_hi[rows], rot2_lo[:, cols])
                        + dot(box_lo[rows], rot2_hi[:, cols])
                    )
                else:
                    value = dot(turned_hi[dx, rows, dy * 128 : dy * 128 + 1024], rot_hi[:, cols])
                value = value.reshape(2, 2, 2, 2, 16, 256)
                if stays:
                    half_sum[unit] = value
                else:
                    away[place % AWAY] = value
                    rs_copy(unit, 0).start()

        def do_rs(unit, stage):
            if stage == 0 and unit in left_home:
                rs_copy(unit, stage).wait_recv()
            else:
                rs_copy(unit, stage).wait()
                if stage == 0:
                    left_home.add(unit)
            if stage < 5:
                fixed = {k: mine[k] for k in ((0,) + RS_ORDER[unit])[: stage + 1]}
                source, at = got[stage], (RS_SLOT[unit][stage],)
            else:
                fixed = dict(enumerate(mine[:5]))
                source, at = got_more, (unit, stage - 5)
            left = [k for k in range(1, 5) if k not in fixed]

            def add(i, carry):
                inner = dict(fixed)
                where = at
                if len(left) >= 3:
                    inner[left[0]], inner[left[1]] = i // 2, i % 2
                    where = at + (i // 2, i % 2)
                half_sum[region(unit, inner)] += source[where]
                return carry

            if len(left) >= 3:
                lax.fori_loop(0, 4, add, 0)
            else:
                add(0, 0)
            if stage < 4 + extra:
                rs_copy(unit, stage + 1).start()
            if stage >= 4 and stage < 4 + extra:
                do_rs(unit, stage + 1)

        def do_post(tap, stage):
            pair = (2 * tap, 2 * tap + 1)
            value = jnp.concatenate([half_sum[region(unit, own)] for unit in pair], axis=1)
            if tap == STAT:
                value = 0.95 * eig[...] + 0.05 * (value * (live_total * float(area * area)))
                scale_rows[...] = value + DAMPING
            else:
                high, low = split(value / scale_rows[...])
                value = dot(high, out_t_hi[...]) + dot(high, out_t_lo[...]) + dot(low, out_t_hi[...])
            for k, unit in enumerate(pair):
                work[region(unit, own, 0)] = value[:, 256 * k : 256 * k + 256]
                ag_copy(unit, 0).start()

        def do_ag(unit, stage):
            ag_copy(unit, stage).wait()
            if stage < 4:
                ag_copy(unit, stage + 1).start()
            if stage == 3 and unit in early:
                early_half(unit)

        early = [unit for kind, unit, _ in TASKS if kind == 4 and unit // 2 != STAT][-1:]

        def half_product(unit, half, finish):
            def cut(i, carry):
                rows = pl.ds(pl.multiple_of(i * 64, 64), 64)
                gathered_hi[rows], gathered_lo[rows] = split(work[unit, half, i // 2, i % 2].reshape(64, 256))
                return carry

            lax.fori_loop(0, 4, cut, 0)
            cols = core_half(half)
            high, low = gathered_hi[0:256], gathered_lo[0:256]

            def tile(i, carry):
                rows = pl.ds(pl.multiple_of(i * 256, 256), 256)
                left = in_hi[rows, cols]
                finish(i, rows, dot(left, high) + dot(left, low) + dot(in_lo[rows, cols], high))
                return carry

            lax.fori_loop(0, 2, tile, 0)

        def early_half(unit):
            def keep(i, rows, value):
                partial[early.index(unit), rows] = value

            half_product(unit, core, keep)

        def late_half(unit):
            def keep(i, rows, value):
                value = value + partial[early.index(unit), rows]
                work[unit, i] = value.reshape(2, 2, 2, 2, 16, 256)
                square_sum[...] += jnp.sum((value * value).reshape(32, 8, 256), axis=0)

            half_product(unit, 1 - core, keep)


        def do_fin(unit, stage):
            if unit // 2 == STAT:
                return
            if unit in early:
                late_half(unit)
                return

            def cut(i, carry):
                rows = pl.ds(pl.multiple_of(i * 64, 64), 64)
                value = work[unit, i // 4, (i // 2) % 2, i % 2].reshape(64, 256)
                gathered_hi[rows], gathered_lo[rows] = split(value)
                return carry

            lax.fori_loop(0, 8, cut, 0)

            def tile(i, carry):
                rows = pl.ds(pl.multiple_of(i * 256, 256), 256)
                value = (
                    dot(in_hi[rows], gathered_hi[...])
                    + dot(in_hi[rows], gathered_lo[...])
                    + dot(in_lo[rows], gathered_hi[...])
                )
                work[unit, i] = value.reshape(2, 2, 2, 2, 16, 256)
                square_sum[...] += jnp.sum((value * value).reshape(32, 8, 256), axis=0)
                return carry

            lax.fori_loop(0, 2, tile, 0)

        def do_sm(stage, unused):
            sm_copy(stage).wait()
            before = small[:, core_half(core)] if stage == 0 else small_half[...]
            small_half[...] = before + small_got[stage]
            sm_copy(stage + 1).start()
            if stage >= 4 and stage < 4 + extra:
                do_sm(stage + 1, 0)

        square_sum[...] = jnp.zeros((8, 256), F32)
        sm_copy(0).start()
        run = (do_mm, do_rs, do_post, do_ag, do_fin, do_sm)
        for kind, which, stage in TASKS:
            run[kind](which, stage)

        sm_copy(len(bits)).wait()
        kept, came = small_half[...], small_back[...]
        low_half, high_half = jnp.where(core == 0, kept, came), jnp.where(core == 0, came, kept)
        block = jnp.concatenate([low_half, high_half], axis=1)
        head_part = jnp.where(row16w <= NCLS, block, 0.0)
        squared = (
            jnp.sum(jnp.sum(square_sum[...], axis=0, keepdims=True), axis=1, keepdims=True)
            + jnp.sum(norm_grads[0] * norm_grads[0] + norm_grads[1] * norm_grads[1], axis=1, keepdims=True)
            + jnp.sum(jnp.sum(head_part * head_part, axis=0, keepdims=True), axis=1, keepdims=True)
        )
        norm = jnp.sqrt(squared)
        factor = jnp.minimum(1.0, CLIP / (norm + 1e-06))
        facts[0:16] = block
        facts[16:24] = stack_rows(norm_grads + [block[NCLS + 1 : NCLS + 2], live_total, norm, factor])
        for copy in moments:
            copy.wait()

    square = (512, 512)
    pl.run_scoped(
        prepare,
        pltpu.VMEM((3, 10 * stride, 512), BF16),
        pltpu.VMEM((3, 1024, 512), BF16),
        pltpu.VMEM((2, 3, 512, 512), BF16),
        pltpu.VMEM((8, stride, 512), F32),
        pltpu.VMEM((8, stride, 512), F32),
        pltpu.VMEM((count_img, 8, 8, 512), BF16),
        *[pltpu.VMEM(square, BF16)] * 4,
        pltpu.VMEM((1024, 512), BF16),
    )
    pl.run_scoped(
        exchange,
        pltpu.VMEM((20, 2, 2, 2, 2, 16, 256), F32),
        pltpu.VMEM((AWAY, 2, 2, 2, 2, 16, 256), F32),
        pltpu.VMEM((512, 256), BF16),
        pltpu.VMEM((512, 256), BF16),
        pltpu.VMEM((2, 512, 256), F32),
    )


def adamw(weight, grad, first, second, rate):
    first = 0.9 * first + 0.1 * grad
    second = 0.999 * second + 0.001 * grad * grad
    step_size = first / (1.0 - 0.9**STEP) / (jnp.sqrt(second / (1.0 - 0.999**STEP)) + 1e-08)
    return (weight - rate * (step_size + 0.01 * weight), first, second)


def adamw_positive(weight, grad, first, second, rate):
    first = 0.9 * first + 0.1 * grad
    second = 0.999 * second + 0.001 * grad * grad
    scaled = second * (1.0 / (1.0 - 0.999**STEP))
    root = scaled * lax.rsqrt(scaled) + 1e-08
    step = first * (rate / (1.0 - 0.9**STEP)) / root
    return (weight * (1.0 - 0.01 * rate) - step, first, second)


CHUNKS = 36
RING = 8


def update_kernel(
    facts,
    gain,
    shift,
    norm_first,
    norm_second,
    head,
    head_first,
    head_second,
    gradients,
    moments,
    loss_parts,
    grad_norm,
    norm_new,
    norm_m,
    norm_v,
    head_new,
    head_m,
    head_v,
    conv_new,
    conv_m,
    conv_v,
    scales_new,
    out_new,
    out_m,
    out_v,
    out_sem,
    scale_sem,
):
    tall = TAPS * 512 // CHUNKS
    outs = ((out_new, conv_new), (out_m, conv_m), (out_v, conv_v))

    def store(k, i):
        rows = pl.ds(pl.multiple_of(i * tall, tall), tall)
        return pltpu.make_async_copy(outs[k][0].at[i % RING], outs[k][1].at[rows], out_sem.at[k, i % RING])

    factor = facts[21:22, 0:1]

    def chunk(i, carry):
        @pl.when(i >= RING)
        def _():
            for k in range(3):
                store(k, i).wait()

        rows = pl.ds(pl.multiple_of(i * tall, tall), tall)
        more = pl.ds(pl.multiple_of(TAPS * 512 + i * tall, tall), tall)
        for half in range(2):
            cols = slice(256 * half, 256 * half + 256)
            where = (2 * (i // 4) + half, (i // 2) % 2, i % 2)
            grad = gradients[where].reshape(tall, 256)
            weight = gradients[(WEIGHT + where[0],) + where[1:]].reshape(tall, 256)
            out_new[i % RING, :, cols], out_m[i % RING, :, cols], out_v[i % RING, :, cols] = adamw_positive(
                weight, factor * grad, moments[rows, cols].astype(F32), moments[more, cols].astype(F32), 0.02
            )
        for k in range(3):
            store(k, i).start()
        return carry

    lax.fori_loop(0, CHUNKS, chunk, 0)
    scale_copies = [
        pltpu.make_async_copy(
            gradients.at[2 * STAT + k], scales_new.at[:, :, :, :, :, :, 256 * k : 256 * k + 256], scale_sem.at[k]
        )
        for k in range(2)
    ]
    for copy in scale_copies:
        copy.start()

    loss_parts[0] = facts[18, 0]
    loss_parts[1] = facts[19, 0]
    grad_norm[0] = facts[20, 0]
    grads = factor * facts[16:18, :]
    weights = jnp.concatenate([gain[...], shift[...]], axis=0)
    norm_new[...], norm_m[...], norm_v[...] = adamw(weights, grads, norm_first[...], norm_second[...], 0.1)
    block = factor * facts[0:16, :]
    head_new[:, 0:512], head_m[:, 0:512], head_v[:, 0:512] = adamw(
        head[:, 0:512], block[0:NCLS], head_first[:, 0:512], head_second[:, 0:512], 0.05
    )
    bias = jnp.concatenate([block[0:16, 0:128], jnp.zeros((112, 128), F32)], axis=0).T[0:NCLS, NCLS : NCLS + 1]
    head_new[:, 512:513], head_m[:, 512:513], head_v[:, 512:513] = adamw(
        head[:, 512:513], bias, head_first[:, 512:513], head_second[:, 512:513], 0.05
    )
    for i in range(CHUNKS - RING, CHUNKS):
        for k in range(3):
            store(k, i).wait()
    for copy in scale_copies:
        copy.wait()


def shards(
    sizes,
    images,
    micro_ids,
    labels,
    conv_weight,
    conv_first,
    conv_second,
    eig_scales,
    basis_in,
    basis_out,
    batchnorm_gain,
    batchnorm_shift,
    norm_first,
    norm_second,
    head,
    head_first,
    head_second,
):
    dp_count, rep_count = sizes
    count_img = images.shape[0]
    chips = dp_count * rep_count // 2
    bit_count = (dp_count * rep_count - 1).bit_length()
    extra = bit_count - 5
    vmem = pl.BlockSpec(memory_space=pltpu.VMEM)
    smem = pl.BlockSpec(memory_space=pltpu.SMEM)
    hbm = pl.BlockSpec(memory_space=pltpu.HBM)
    gain = batchnorm_gain.reshape(1, 512)
    shift = batchnorm_shift.reshape(1, 512)
    pixels = 8 * count_img
    square = (512, 512)
    dma = pltpu.SemaphoreType.DMA
    scratch = [
        pltpu.SMEM((count_img,), jnp.int32),
        pltpu.SMEM((count_img,), jnp.int32),
        pltpu.VMEM((1, 512), F32),
        pltpu.VMEM((1, 512), F32),
        pltpu.VMEM((NCLS, 513), F32),
        pltpu.VMEM((GOT_COUNT[0], 2, 2, 2, 2, 16, 256), F32),
        pltpu.VMEM((GOT_COUNT[1], 2, 2, 2, 16, 256), F32),
        pltpu.VMEM((GOT_COUNT[2], 2, 2, 16, 256), F32),
        pltpu.VMEM((GOT_COUNT[3], 2, 16, 256), F32),
        pltpu.VMEM((GOT_COUNT[4], 16, 256), F32),
        pltpu.VMEM((20, extra, 16, 256) if extra else (1, 1, 8, 128), F32),
        pltpu.VMEM((16, 512), F32),
        pltpu.VMEM((16, 256), F32),
        pltpu.VMEM((16, 256), F32),
        pltpu.VMEM((bit_count, 16, 256), F32),
        pltpu.VMEM((2, 8, 512), F32),
        pltpu.VMEM((2, 8, 256), F32),
        pltpu.VMEM((2, chips, 8, 256), F32),
        pltpu.VMEM((2, 2, 8, 256), F32),
        pltpu.VMEM((3, 512, 1280), BF16),
        pltpu.VMEM((512, 1024), BF16),
        pltpu.VMEM((512, 1024), BF16),
        *[pltpu.VMEM((1024, 512), BF16)] * 3,
        pltpu.VMEM((16, 512), F32),
        *[pltpu.VMEM(square, BF16)] * 4,
        pltpu.VMEM((5, 8, 512), F32),
        *[pltpu.VMEM((16, 512), F32)] * 4,
        pltpu.VMEM((128, 640), F32),
        pltpu.VMEM((16, 512), F32),
        pltpu.VMEM((8, 256), F32),
        dma((3,)),
        dma((11,)),
        dma((SEND_COUNT,)),
        dma((RECV_COUNT,)),
        dma((2, 20, extra) if extra else (1, 1, 1)),
        dma((bit_count + 1,)),
        dma((bit_count + 1,)),
        dma((4,)),
        dma((4,)),
        dma((2,)),
        dma((2,)),
    ]
    turned_basis = [x.reshape(2, 2, 2, 2, 2, 16, 512) for x in (basis_in, basis_out)]
    gradients, facts, moments = pl.pallas_call(
        functools.partial(main_kernel, (dp_count, rep_count, count_img)),
        out_shape=(
            pltpu.VMEM((WEIGHT + 2 * TAPS, 2, 2, 2, 2, 2, 16, 256), F32),
            pltpu.VMEM((24, 512), F32),
            pltpu.VMEM((2 * TAPS * 512, 512), BF16),
        ),
        in_specs=[hbm] * 12,
        out_specs=(vmem,) * 3,
        scratch_shapes=scratch,
        compiler_params=pltpu.CompilerParams(
            collective_id=0, has_side_effects=True, vmem_limit_bytes=71 * 2**19
        ),
        name="reduce_and_precondition",
    )(
        micro_ids,
        labels,
        images,
        gain,
        shift,
        head.T,
        conv_weight.reshape(TAPS, 2, 2, 2, 2, 2, 16, 512),
        conv_first,
        conv_second,
        eig_scales,
        *turned_basis,
    )
    tall = TAPS * 512 // CHUNKS
    head_shape = (NCLS, 513)
    outs = pl.pallas_call(
        update_kernel,
        out_shape=(
            jax.ShapeDtypeStruct((2,), F32),
            jax.ShapeDtypeStruct((1,), F32),
            *[jax.ShapeDtypeStruct((2, 512), F32)] * 3,
            *[jax.ShapeDtypeStruct(head_shape, F32)] * 3,
            *[jax.ShapeDtypeStruct((TAPS * 512, 512), F32)] * 3,
            jax.ShapeDtypeStruct((2, 2, 2, 2, 2, 16, 512), F32),
        ),
        in_specs=[vmem] * 10,
        out_specs=(smem, smem) + (vmem,) * 6 + (hbm,) * 4,
        scratch_shapes=[
            *[pltpu.VMEM((RING, tall, 512), F32)] * 3,
            dma((3, RING)),
            dma((2,)),
        ],
        compiler_params=pltpu.CompilerParams(vmem_limit_bytes=27 * 2**18),
        name="adamw",
    )(
        facts,
        gain,
        shift,
        norm_first,
        norm_second,
        head.T,
        head_first.T,
        head_second.T,
        gradients,
        moments,
    )
    loss_parts, grad_norm, norm_new, norm_m, norm_v, head_new, head_m, head_v, conv_new, conv_m, conv_v, scales_new = outs
    return (
        loss_parts,
        grad_norm.reshape(()),
        conv_new,
        conv_m,
        conv_v,
        scales_new.reshape(square),
        norm_new,
        norm_m,
        norm_v,
        head_new.T,
        head_m.T,
        head_v.T,
    )


def solution(mesh):
    split_images = P(("dp", "rep"))
    in_specs = (P(("dp", "rep"), None, None, None), split_images, split_images) + (P(),) * 13
    sizes = (mesh.shape["dp"], mesh.shape["rep"])
    return jax.shard_map(
        functools.partial(shards, sizes), mesh=mesh, in_specs=in_specs, out_specs=(P(),) * 12, check_vma=False
    )
```
